512 devices in a mesh: slab: 64 (over y_lo, z, core), head: 8 (over x, y_hi).
Axes of the slice: x: 4, y: 8 (y_hi: 2, y_lo: 4; y = y_hi * 4 + y_lo), z: 8, core: 2. Of those that a mesh axis runs over, the one named last changes fastest.
Arguments:
- query: bfloat16 [16384, 2048], P(('slab', 'head')), may hold values from -12 to 12
- key: bfloat16 [16384, 2048], P(('slab', 'head')), may hold values from -4 to 4
- value: bfloat16 [16384, 2048], P(('slab', 'head')), may hold values from -6 to 6
- grad_out: bfloat16 [16384, 2048], P(('slab', 'head')), may hold values from -6 to 6
- query_scale: float32 [2048], replicated, may hold values from 0.5 to 2
- key_scale: float32 [2048], replicated, may hold values from 0.5 to 2
- neighbours: int32 [256, 27], P('slab'), may hold values from 0 to 255, as said below
Outputs:
- attention: bfloat16 [16384, 2048], P(('slab', 'head'))
- grad_query: bfloat16 [16384, 2048], P(('slab', 'head'))
- grad_key: bfloat16 [16384, 2048], P(('slab', 'head'))
- grad_value: bfloat16 [16384, 2048], P(('slab', 'head'))
The draws below stay inside these ranges and needn't reach their ends.
Inputs may be any that keep to these rules, and one draw needn't show every extreme that they name: `neighbours`: row t lists tiles of the 3 x 3 x 3 window of tiles around tile t (frame tile, row and column offsets -1, 0, 1 in slot order frame-major), clipped at the grid's edges, with some window tiles left out; tile t itself is always listed, and every unused slot repeats t.
All inputs are finite; a program needn't handle non-finite values.
Results may differ from the reference program's by a relative error of at most 0.039.
Values may be sent and summed in bfloat16 or wider, within the bound.
A program may use at most 64 MiB of HBM per device.

```python
import math
import jax
import jax.numpy as jnp
from jax import lax

HD = 128
HEADS = 16
TILE = 64
FT = 4
TW = 4
D = 2048
SLAB = 256
TOKENS = 16384
TILES = 256
N_SLAB = 64


def draw_query(key, part):
    key = jax.random.fold_in(key, 11)
    base = jnp.clip(jax.random.normal(key, (TOKENS, D), jnp.float32), -4.0, 4.0)
    return base.astype(jnp.bfloat16)


def draw_key(key, part):
    key = jax.random.fold_in(key, 12)
    base = jnp.clip(jax.random.normal(key, (TOKENS, D), jnp.float32), -4.0, 4.0)
    return base.astype(jnp.bfloat16)


def draw_neighbours(key, part):
    key = jax.random.fold_in(key, 5)
    tile_ids = jnp.arange(TILES, dtype=jnp.int32)
    row_total = TILES // (FT * TW)
    column_of = tile_ids % TW
    slab_of = tile_ids // TW
    row_of = slab_of % row_total
    frame_of = slab_of // row_total
    offsets = jnp.arange(27, dtype=jnp.int32)
    new_frame = frame_of[:, None] + (offsets // 9 - 1)[None, :]
    new_row = row_of[:, None] + (offsets // 3 % 3 - 1)[None, :]
    new_column = column_of[:, None] + (offsets % 3 - 1)[None, :]
    inside = (new_frame >= 0) & (new_frame < FT) & (new_row >= 0) & (new_row < row_total) & (new_column >= 0) & (new_column < TW)
    keeping = jax.random.randint(key, (TILES, 27), 0, 4) != 0
    centre = (offsets == 13)[None, :]
    listed = inside & (keeping | centre)
    target = (new_frame * row_total + new_row) * TW + new_column
    return jnp.where(listed, target, tile_ids[:, None]).astype(jnp.int32)


def shard_levels(rng, dims, shards, low, top_value):
    level = 1.0
    for axis_at, parts in shards:
        steps = jax.random.uniform(jax.random.fold_in(jax.random.fold_in(rng, 6), axis_at), (parts,), jnp.float32, low / len(shards), top_value / len(shards))
        level = level * jnp.repeat(jnp.exp(steps), dims[axis_at] // parts).reshape((-1,) + (1,) * (len(dims) - 1 - axis_at))
    return level


def normal_values(key, extent, deviation, bound, cuts=(), held_as=jnp.bfloat16):
    values = deviation * jax.random.normal(key, extent, jnp.float32)
    if cuts:
        values = values * shard_levels(key, extent, cuts, -0.22, 0.18)
    return jnp.clip(values, -bound, bound).astype(held_as)


def setup_inputs(seed: int = 0) -> dict:
    seeds = jax.random.split(jax.random.key(seed), 8)
    return {
        "query": draw_query(jax.random.fold_in(seeds[7], 71), 0),
        "key": draw_key(jax.random.fold_in(seeds[7], 71), 0),
        "value": normal_values(seeds[2], (TOKENS, D), 1.0, 6.0, ((0, 512),)),
        "grad_out": normal_values(seeds[3], (TOKENS, D), 1.0, 6.0, ((0, 512),)),
        "query_scale": jnp.clip(jnp.exp(jax.random.uniform(seeds[4], (D,), jnp.float32, math.log(0.5), math.log(2.0))), 0.5, 2.0),
        "key_scale": jnp.clip(jnp.exp(jax.random.uniform(seeds[5], (D,), jnp.float32, math.log(0.5), math.log(2.0))), 0.5, 2.0),
        "neighbours": draw_neighbours(jax.random.fold_in(seeds[7], 71), 0),
    }


masked_score = -1.0e30


def slab_ids(source, width):
    return (source * width + jnp.arange(width, dtype=jnp.int32)).astype(jnp.int32)


def by_heads(rows):
    return rows.reshape(rows.shape[0], HEADS, HD).transpose(1, 0, 2).astype(jnp.float32)


def tile_allowed(lists, key_ids, tile_size):
    allowed = jnp.any(lists[:, :, None] == key_ids[None, None, :], axis=1)
    return jnp.repeat(jnp.repeat(allowed, tile_size, axis=0), tile_size, axis=1)


def flatten_heads(stacked):
    return stacked.transpose(0, 2, 1, 3).reshape(TOKENS, D)


def pick(array, index):
    return lax.dynamic_slice_in_dim(array, (index * SLAB).astype(jnp.int32), SLAB, 0)


def reference(query, key, value, grad_out, query_scale, key_scale, neighbours):
    factor = query_scale * HD ** -0.5
    q_fold = (query.astype(jnp.float32) * factor).astype(jnp.bfloat16)
    k_fold = (key.astype(jnp.float32) * key_scale).astype(jnp.bfloat16)
    rows_count = N_SLAB // FT
    offsets = [frame_step * rows_count + row_step for frame_step in (-1, 0, 1) for row_step in (-1, 0, 1)]

    def query_side(slab_index):
        sources = [slab_index + step for step in offsets]
        clipped = [jnp.clip(source, 0, N_SLAB - 1).astype(jnp.int32) for source in sources]
        queries = by_heads(pick(q_fold, slab_index))
        keys = by_heads(jnp.concatenate([pick(k_fold, index) for index in clipped]))
        values = by_heads(jnp.concatenate([pick(value, index) for index in clipped]))
        grads = by_heads(pick(grad_out, slab_index))
        lists = lax.dynamic_slice_in_dim(neighbours, (slab_index * TW).astype(jnp.int32), TW, 0)
        key_ids = jnp.concatenate([slab_ids(source, TW) for source in sources])
        allowed = tile_allowed(lists, key_ids, TILE)
        scores = jnp.where(allowed[None], jnp.einsum("hqc,hkc->hqk", queries, keys), masked_score)
        row_max = jnp.max(scores, axis=2, keepdims=True)
        log_total = row_max + jnp.log(jnp.sum(jnp.exp(scores - row_max), axis=2, keepdims=True))
        weights = jnp.exp(scores - log_total)
        weights_low = weights.astype(jnp.bfloat16)
        attended = jnp.einsum("hqk,hkc->hqc", weights_low.astype(jnp.float32), values).astype(jnp.bfloat16)
        row_delta = jnp.sum(grads * attended.astype(jnp.float32), axis=2, keepdims=True)
        grad_weights = jnp.einsum("hqc,hkc->hqk", grads, values)
        grad_scores = (weights * (grad_weights - row_delta)).astype(jnp.bfloat16)
        grad_queries = jnp.einsum("hqk,hkc->hqc", grad_scores.astype(jnp.float32), keys)
        return attended, log_total[..., 0], row_delta[..., 0], grad_queries

    slab_list = jnp.arange(N_SLAB, dtype=jnp.int32)
    attended, log_totals, deltas, grad_queries = lax.map(query_side, slab_list)

    def key_side(slab_index):
        sources = [slab_index - step for step in offsets]
        clipped = [jnp.clip(source, 0, N_SLAB - 1).astype(jnp.int32) for source in sources]
        valid = [(source >= 0) & (source < N_SLAB) for source in sources]
        queries = by_heads(jnp.concatenate([pick(q_fold, index) for index in clipped]))
        grads = by_heads(jnp.concatenate([pick(grad_out, index) for index in clipped]))
        keys = by_heads(pick(k_fold, slab_index))
        values = by_heads(pick(value, slab_index))
        lse_band = jnp.concatenate([log_totals[index] for index in clipped], axis=1)
        delta_band = jnp.concatenate([deltas[index] for index in clipped], axis=1)
        lists = jnp.concatenate([jnp.where(flag, lax.dynamic_slice_in_dim(neighbours, (index * TW).astype(jnp.int32), TW, 0), -1) for index, flag in zip(clipped, valid)])
        allowed = tile_allowed(lists, slab_ids(slab_index, TW), TILE)
        scores = jnp.einsum("hqc,hkc->hqk", queries, keys)
        weights = jnp.exp(jnp.where(allowed[None], scores - lse_band[:, :, None], masked_score))
        weights_low = weights.astype(jnp.bfloat16)
        grad_values = jnp.einsum("hqk,hqc->hkc", weights_low.astype(jnp.float32), grads)
        grad_weights = jnp.einsum("hqc,hkc->hqk", grads, values)
        grad_scores = (weights * (grad_weights - delta_band[:, :, None])).astype(jnp.bfloat16)
        grad_keys = jnp.einsum("hqk,hqc->hkc", grad_scores.astype(jnp.float32), queries)
        return grad_keys, grad_values

    grad_keys, grad_values = lax.map(key_side, slab_list)
    attention = flatten_heads(attended)
    grad_query = (flatten_heads(grad_queries) * factor).astype(jnp.bfloat16)
    grad_key = (flatten_heads(grad_keys) * key_scale).astype(jnp.bfloat16)
    grad_value = flatten_heads(grad_values).astype(jnp.bfloat16)
    return (attention, grad_query, grad_key, grad_value)
```

```python
import functools

import jax
import jax.numpy as jnp
from jax import lax
from jax.experimental import pallas as pl
from jax.experimental.pallas import tpu as pltpu
from jax.sharding import PartitionSpec as P

HD = 128
TILE = 64
FT = 4
TW = 4
SLAB = TILE * TW
RING = 2 * FT
BLOCKS = 9
CENTRE = 4
HIDDEN = -1e30
MESH = pl.DeviceIdType.MESH
BF16 = jnp.bfloat16
F32 = jnp.float32
KV, QD = 0, 1


def dot_nn(a, b):
    return lax.dot_general(a, b, (((1,), (0,)), ((), ())), preferred_element_type=F32)


def dot_nt(a, b):
    return lax.dot_general(a, b, (((1,), (1,)), ((), ())), preferred_element_type=F32)


def dot_tn(a, b):
    return lax.dot_general(a, b, (((0,), (0,)), ((), ())), preferred_element_type=F32)


def by_key_tile(scores, rows):
    shaped = scores.reshape(TW, TILE, SLAB) + rows[:TW][:, None, :]
    return shaped.reshape(SLAB, SLAB)


def kernel(
    rows, columns, unroll,
    query, key, value, grad_out, query_scale, key_scale, neighbours,
    attention_out, grad_query_out, grad_key_out, grad_value_out,
    raw, stage, data, listed, lists, bias, scores, weights, stats, stats_sent, results, landed,
    in_sem, a2a_send, a2a_recv, list_send, list_recv, halo_send, y_recv, r_recv,
    stat_send, stat_recv, out_send, out_recv, done_sem,
):
    slab = lax.axis_index("slab")
    head = lax.axis_index("head")
    y_lo, r = slab // rows, slab % rows
    x, y_hi = head // 2, head % 2
    y = y_hi * FT + y_lo
    origin = (y + RING - 2) % RING
    group, frame = origin // FT, origin % FT
    pair = x * 2 + group
    chunk = SLAB // (2 * columns)

    def device(to_y, to_r, to_x):
        return {"slab": (to_y % FT) * rows + to_r, "head": to_x * 2 + to_y // FT}

    y_up, y_down = (y + 1) % RING, (y + RING - 1) % RING
    r_up, r_down = (r + 1) % rows, (r + rows - 1) % rows
    y_at = (y_down, y, y_up)
    r_at = (r_down, r, r_up)
    y_far = ((y + 2) % RING, (y + RING - 2) % RING)
    x_at = tuple((x + step) % columns for step in range(columns))

    barrier = pltpu.get_barrier_semaphore()
    greeted = 0
    for to_y in y_far:
        for to_x in x_at:
            pl.semaphore_signal(barrier, 1, device_id=device(to_y, r, to_x), device_id_type=MESH)
            greeted += 1
    for block in range(BLOCKS):
        if block != CENTRE:
            pl.semaphore_signal(
                barrier, 1, device_id=device(y_at[block // 3], r_at[block % 3], x),
                device_id_type=MESH,
            )
            greeted += 1

    sources = (key, value, query, grad_out)
    loads = [pltpu.make_async_copy(sources[i], raw.at[i], in_sem.at[i]) for i in range(4)]
    for load in loads:
        load.start()
    listed[...] = jnp.full(listed.shape, -2.0, F32)
    listed[0:TW, 0:27] = neighbours[...].astype(F32)

    def put(kind, which, array):
        for piece in range(4 * columns):
            stage[kind, piece % 2, piece // 2, which] = array[:, piece * HD : (piece + 1) * HD]

    loads[0].wait()
    put(KV, 0, (raw[0].astype(F32) * key_scale[...]).astype(BF16))
    loads[1].wait()
    put(KV, 1, raw[1])
    pl.semaphore_wait(barrier, greeted)

    my_rows = pl.ds(pl.multiple_of(head * chunk, chunk), chunk)

    def send_heads(kind, number):
        for to_x in x_at:
            for way, to_y in enumerate(y_far):
                to_group = (y_hi + way) % 2
                pltpu.make_async_remote_copy(
                    src_ref=stage.at[kind, number, to_x * 2 + to_group],
                    dst_ref=data.at[kind, number, CENTRE, :, my_rows, :],
                    send_sem=a2a_send.at[kind, number],
                    recv_sem=a2a_recv.at[kind, number],
                    device_id=device(to_y, r, to_x),
                    device_id_type=MESH,
                ).start()

    def wait_heads(kind, number):
        whole = data.at[kind, number, CENTRE]
        pltpu.make_async_copy(whole, whole, a2a_recv.at[kind, number]).wait()

    def push(kind, number, source, target, sem, place):
        return pltpu.make_async_remote_copy(
            src_ref=data.at[kind, number, source],
            dst_ref=data.at[kind, number, target],
            send_sem=halo_send.at[kind, number],
            recv_sem=sem,
            device_id=place,
            device_id_type=MESH,
        )

    def y_copies(kind, number):
        return [
            push(kind, number, CENTRE, 1, y_recv.at[kind, number, 0], device(y_up, r, x)),
            push(kind, number, CENTRE, 7, y_recv.at[kind, number, 1], device(y_down, r, x)),
        ]

    def r_copies(kind, number, level):
        base = level * 3
        return [
            push(kind, number, base + 1, base, r_recv.at[kind, number, level, 0],
                 device(y, r_up, x)),
            push(kind, number, base + 1, base + 2, r_recv.at[kind, number, level, 1],
                 device(y, r_down, x)),
        ]

    def spread(kind, number):
        for copy in y_copies(kind, number) + r_copies(kind, number, 1):
            copy.start()

    def forward(kind, number):
        arrivals = y_copies(kind, number)
        for way, level in ((0, 0), (1, 2)):
            arrivals[way].wait_recv()
            for copy in r_copies(kind, number, level):
                copy.start()

    def wait_rows(kind, number):
        for level in (1, 0, 2):
            for copy in r_copies(kind, number, level):
                copy.wait_recv()

    send_heads(KV, 0)
    send_heads(KV, 1)
    list_copy = pltpu.make_async_remote_copy(
        src_ref=listed, dst_ref=lists, send_sem=list_send, recv_sem=list_recv,
        device_id=device(y_far[0], r, x), device_id_type=MESH,
    )
    list_copy.start()

    factor = query_scale[...] * HD ** (-0.5)
    loads[2].wait()
    put(QD, 0, (raw[2].astype(F32) * factor).astype(BF16))
    loads[3].wait()
    put(QD, 1, raw[3])

    wait_heads(KV, 0)
    spread(KV, 0)
    send_heads(QD, 0)
    wait_heads(KV, 1)
    spread(KV, 1)
    send_heads(QD, 1)

    list_copy.wait_recv()
    shape = (BLOCKS * 8, 128)
    line = lax.broadcasted_iota(jnp.int32, shape, 0)
    column = line % 8
    block_of = line // 8
    key_frame = frame + block_of // 3 - 1
    key_row = r + block_of % 3 - 1
    real = (
        (column < TW) & (key_frame >= 0) & (key_frame < FT) & (key_row >= 0) & (key_row < rows)
    )
    ids = jnp.where(real, (key_frame * rows + key_row) * TW + column, -5).astype(F32)
    lane_tile = lax.broadcasted_iota(jnp.int32, (BLOCKS * 8, SLAB), 1) // TILE
    found = jnp.full((BLOCKS * 8, SLAB), HIDDEN, F32)
    for tile in range(TW):
        hit = jnp.max(
            jnp.where(lists[tile : tile + 1, :] == ids, 0.0, HIDDEN), axis=1, keepdims=True
        )
        found = jnp.where(lane_tile == tile, hit, found)
    bias[...] = found.reshape(BLOCKS, 8, SLAB)

    forward(KV, 0)
    wait_heads(QD, 0)
    spread(QD, 0)
    forward(KV, 1)
    wait_heads(QD, 1)
    spread(QD, 1)

    def return_heads(kind, number):
        start = pl.multiple_of(pair * 2 * HD + number * HD, HD)
        for to_x in x_at:
            for way, to_y in enumerate(y_far):
                token_chunk = to_x * 2 + to_y // FT
                part = pl.ds(pl.multiple_of(token_chunk * chunk, chunk), chunk)
                pltpu.make_async_remote_copy(
                    src_ref=results.at[kind, number, :, part, :],
                    dst_ref=landed.at[kind, :, :, pl.ds(start, HD)],
                    send_sem=out_send.at[kind],
                    recv_sem=out_recv.at[kind],
                    device_id=device(to_y, r, to_x),
                    device_id_type=MESH,
                ).start()

    def my_scale(scale, number):
        return scale[:, pl.ds(pl.multiple_of(pair * 2 * HD + number * HD, HD), HD)]

    def query_side(number, between):
        queries = data[QD, number, CENTRE, 0]
        grads = data[QD, number, CENTRE, 1]

        def score(block, row_max):
            part = by_key_tile(dot_nt(data[KV, number, block, 0], queries), bias[block])
            scores[block] = part
            return jnp.maximum(row_max, jnp.max(part, axis=0, keepdims=True))

        row_max = lax.fori_loop(
            0, BLOCKS, score, jnp.full((1, SLAB), -3e38, F32), unroll=unroll
        )
        between()

        def attend(block, carry):
            total, attended = carry
            part = jnp.exp(scores[block] - row_max)
            low = part.astype(BF16)
            weights[block] = low
            total = total + jnp.sum(part, axis=0, keepdims=True)
            return total, attended + dot_tn(data[KV, number, block, 1], low)

        total, attended = lax.fori_loop(
            0, BLOCKS, attend,
            (jnp.zeros((1, SLAB), F32), jnp.zeros((HD, SLAB), F32)), unroll=unroll,
        )
        inverse = 1.0 / total
        attended = (attended * inverse).astype(BF16).astype(F32)
        delta = jnp.sum(attended * grads.astype(F32).T, axis=0, keepdims=True)
        results[0, number, 0] = attended.T.astype(BF16)
        log_total = row_max + jnp.log(total)
        line8 = lax.broadcasted_iota(jnp.int32, (8, SLAB), 0)
        for block in range(BLOCKS):
            message = jnp.where(line8 == TW, delta, bias[block] - log_total)
            if block == CENTRE:
                stats[number, CENTRE] = message
            else:
                stats_sent[number, block] = message
                stat_copy(number, block).start()
        delta_part = delta * inverse

        def slope(block, carry):
            grad_weights = dot_nt(data[KV, number, block, 1], grads)
            part = weights[block].astype(F32) * (grad_weights * inverse - delta_part)
            return carry + dot_tn(data[KV, number, block, 0], part.astype(BF16))

        grad_queries = lax.fori_loop(
            0, BLOCKS, slope, jnp.zeros((HD, SLAB), F32), unroll=unroll
        )
        scale = my_scale(query_scale, number) * HD ** (-0.5)
        results[0, number, 1] = (grad_queries.T * scale).astype(BF16)
        return_heads(0, number)

    def stat_copy(number, block):
        return pltpu.make_async_remote_copy(
            src_ref=stats_sent.at[number, block],
            dst_ref=stats.at[number, 8 - block],
            send_sem=stat_send.at[number, block],
            recv_sem=stat_recv.at[number, block],
            device_id=device(y_at[block // 3], r_at[block % 3], x),
            device_id_type=MESH,
        )

    def key_side(number):
        keys = data[KV, number, CENTRE, 0]
        values = data[KV, number, CENTRE, 1]

        def step(block, carry):
            grad_keys, grad_values = carry
            queries = data[QD, number, block, 0]
            grads = data[QD, number, block, 1]
            part = jnp.exp(by_key_tile(dot_nt(keys, queries), stats[number, block]))
            grad_weights = dot_nt(values, grads)
            slopes = (part * (grad_weights - stats[number, block, TW : TW + 1])).astype(BF16)
            grad_values = grad_values + dot_nn(part.astype(BF16), grads)
            grad_keys = grad_keys + dot_nn(slopes, queries)
            return grad_keys, grad_values

        zero = jnp.zeros((SLAB, HD), F32)
        grad_keys, grad_values = lax.fori_loop(0, BLOCKS, step, (zero, zero), unroll=unroll)
        results[1, number, 0] = (grad_keys * my_scale(key_scale, number)).astype(BF16)
        results[1, number, 1] = grad_values.astype(BF16)
        return_heads(1, number)

    wait_rows(KV, 0)
    query_side(0, lambda: forward(QD, 0))
    wait_rows(KV, 1)
    query_side(1, lambda: forward(QD, 1))
    for number in range(2):
        wait_rows(QD, number)
        for block in range(BLOCKS):
            if block != CENTRE:
                stat_copy(number, block).wait_recv()
        key_side(number)

    targets = ((attention_out, grad_query_out), (grad_key_out, grad_value_out))
    stores = []
    for kind in range(2):
        pltpu.make_async_copy(landed.at[kind], landed.at[kind], out_recv.at[kind]).wait()
        for which in range(2):
            copy = pltpu.make_async_copy(
                landed.at[kind, which], targets[kind][which], done_sem.at[kind, which]
            )
            copy.start()
            stores.append(copy)
    list_copy.wait_send()
    for kind in range(2):
        for number in range(2):
            sent = stage.at[kind, number]
            pltpu.make_async_copy(sent, sent, a2a_send.at[kind, number]).wait()
            sent = data.at[kind, number, 0:8]
            pltpu.make_async_copy(sent, sent, halo_send.at[kind, number]).wait()
    for number in range(2):
        for block in range(BLOCKS):
            if block != CENTRE:
                stat_copy(number, block).wait_send()
    for kind in range(2):
        sent = results.at[kind]
        pltpu.make_async_copy(sent, sent, out_send.at[kind]).wait()
    for copy in stores:
        copy.wait()


def local(query, key, value, grad_out, query_scale, key_scale, neighbours):
    rows = lax.axis_size("slab") // FT
    columns = lax.axis_size("head") // 2
    chunk, width = query.shape
    out = jax.ShapeDtypeStruct((chunk, width), BF16)
    anywhere = pl.BlockSpec(memory_space=pl.ANY)
    vmem = pl.BlockSpec(memory_space=pltpu.VMEM)
    dma = pltpu.SemaphoreType.DMA
    return pl.pallas_call(
        functools.partial(kernel, rows, columns, 3),
        out_shape=(out,) * 4,
        in_specs=[anywhere] * 4 + [vmem] * 3,
        out_specs=(anywhere,) * 4,
        scratch_shapes=[
            pltpu.VMEM((4, chunk, width), BF16),
            pltpu.VMEM((2, 2, 2 * columns, 2, chunk, HD), BF16),
            pltpu.VMEM((2, 2, BLOCKS, 2, SLAB, HD), BF16),
            pltpu.VMEM((8, 128), F32),
            pltpu.VMEM((8, 128), F32),
            pltpu.VMEM((BLOCKS, 8, SLAB), F32),
            pltpu.VMEM((BLOCKS, SLAB, SLAB), F32),
            pltpu.VMEM((BLOCKS, SLAB, SLAB), BF16),
            pltpu.VMEM((2, BLOCKS, 8, SLAB), F32),
            pltpu.VMEM((2, BLOCKS, 8, SLAB), F32),
            pltpu.VMEM((2, 2, 2, SLAB, HD), BF16),
            pltpu.VMEM((2, 2, chunk, width), BF16),
            dma((4,)),
            dma((2, 2)),
            dma((2, 2)),
            dma,
            dma,
            dma((2, 2)),
            dma((2, 2, 2)),
            dma((2, 2, 3, 2)),
            dma((2, BLOCKS)),
            dma((2, BLOCKS)),
            dma((2,)),
            dma((2,)),
            dma((2, 2)),
        ],
        compiler_params=pltpu.CompilerParams(
            collective_id=0, has_side_effects=True, vmem_limit_bytes=48 * 1024 * 1024
        ),
        name="tiles",
    )(
        query, key, value, grad_out,
        query_scale.reshape(1, width), key_scale.reshape(1, width), neighbours,
    )


def solution(mesh):
    token = P(("slab", "head"), None)
    return jax.shard_map(
        local,
        mesh=mesh,
        in_specs=(token, token, token, token, P(), P(), P("slab", None)),
        out_specs=(token,) * 4,
        check_vma=False,
    )
```

```python
import functools

import jax
import jax.numpy as jnp
from jax import lax
from jax.experimental import pallas as pl
from jax.experimental.pallas import tpu as pltpu
from jax.sharding import PartitionSpec as P

HD = 128
TILE = 64
FT = 4
TW = 4
SLAB = TILE * TW
RING = 2 * FT
BLOCKS = 9
OUTER, INNER, BEYOND = 0, 1, 2
HIDDEN = -1e30
MESH = pl.DeviceIdType.MESH
BF16 = jnp.bfloat16
F32 = jnp.float32
KV, QD = 0, 1
VMEM_BYTES = 58 * 1024 * 1024


def dot_nn(a, b):
    return lax.dot_general(a, b, (((1,), (0,)), ((), ())), preferred_element_type=F32)


def dot_nt(a, b):
    return lax.dot_general(a, b, (((1,), (1,)), ((), ())), preferred_element_type=F32)


def dot_tn(a, b):
    return lax.dot_general(a, b, (((0,), (0,)), ((), ())), preferred_element_type=F32)


def by_key_tile(scores, rows):
    shaped = scores.reshape(TW, TILE, SLAB) + rows[:TW][:, None, :]
    return shaped.reshape(SLAB, SLAB)


def kernel(
    rows, columns, unroll,
    query, key, value, grad_out, query_scale_in, key_scale_in, neighbours_in, landed,
    raw, query_scale, key_scale, neighbours,
    stage, data, listed, lists, bias, scores, weights, stats, stats_sent, results,
    in_sem, a2a_send, a2a_recv, list_send, list_recv, halo_send, y_recv, r_recv,
    stat_send, stat_recv, far_send, far_recv, out_send, out_recv,
):
    loads = [
        pltpu.make_async_copy(source, target, in_sem.at[i])
        for i, (source, target) in enumerate((
            (key, raw.at[0]), (value, raw.at[1]), (query, raw.at[2]), (grad_out, raw.at[3]),
            (key_scale_in, key_scale), (query_scale_in, query_scale),
            (neighbours_in, neighbours),
        ))
    ]
    for load in (loads[4], *loads[:4], *loads[5:]):
        load.start()

    slab = lax.axis_index("slab")
    head = lax.axis_index("head")
    y_lo, r = slab // rows, slab % rows
    x, y_hi = head // 2, head % 2
    y = y_hi * FT + y_lo
    chunk = SLAB // (2 * columns)
    half = 1 - y_lo // 2
    far_y = (1 - y_lo // 2) * 2
    y_far = (far_y, far_y + 1, far_y + FT, far_y + FT + 1)
    frame_of = (3 * half, 1 + half, 2 - half)

    def quarter(at_y):
        return ((at_y + RING - 1) % RING) // 2

    def slot_of(at_y):
        return ((at_y % FT + 1) % FT) // 2

    my_head = x * 4 + quarter(y)
    y_partner = (y + RING - 1 + 2 * (y % 2)) % RING

    def device(to_y, to_r, to_x):
        return {"slab": (to_y % FT) * rows + to_r, "head": to_x * 2 + to_y // FT}

    r_at = ((r + rows - 1) % rows, r, (r + 1) % rows)
    x_at = tuple((x + step) % columns for step in range(columns))

    barrier = pltpu.get_barrier_semaphore()
    peers = [device(to_y, r, to_x) for to_y in y_far for to_x in x_at]
    peers += [device(y, r_at[0], x), device(y, r_at[2], x)]
    peers += [device(y_partner, to_r, x) for to_r in r_at]
    for peer in peers:
        pl.semaphore_signal(barrier, 1, device_id=peer, device_id_type=MESH)
    listed[...] = jnp.full(listed.shape, -2.0, F32)

    def put(kind, which, array):
        for piece in range(4 * columns):
            stage[kind, piece, which] = array[:, piece * HD : (piece + 1) * HD]

    loads[4].wait()
    loads[0].wait()
    put(KV, 0, (raw[0].astype(F32) * key_scale[...]).astype(BF16))
    loads[1].wait()
    put(KV, 1, raw[1])
    pl.semaphore_wait(barrier, len(peers))

    my_rows = pl.ds(pl.multiple_of(head * chunk, chunk), chunk)

    def send_heads(kind, places):
        for to_x in x_at:
            for to_y in places:
                pltpu.make_async_remote_copy(
                    src_ref=stage.at[kind, to_x * 4 + quarter(to_y)],
                    dst_ref=data.at[kind, slot_of(y), 1, :, my_rows, :],
                    send_sem=a2a_send.at[kind],
                    recv_sem=a2a_recv.at[kind, slot_of(y)],
                    device_id=device(to_y, r, to_x),
                    device_id_type=MESH,
                ).start()

    def wait_heads(kind, slot):
        whole = data.at[kind, slot, 1]
        pltpu.make_async_copy(whole, whole, a2a_recv.at[kind, slot]).wait()

    def y_copy(kind):
        return pltpu.make_async_remote_copy(
            src_ref=data.at[kind, INNER, 1],
            dst_ref=data.at[kind, BEYOND, 1],
            send_sem=halo_send.at[kind, 6],
            recv_sem=y_recv.at[kind],
            device_id=device(y_partner, r, x),
            device_id_type=MESH,
        )

    def r_copies(kind, slot):
        return [
            pltpu.make_async_remote_copy(
                src_ref=data.at[kind, slot, 1],
                dst_ref=data.at[kind, slot, 2 - side],
                send_sem=halo_send.at[kind, slot * 2 + side // 2],
                recv_sem=r_recv.at[kind, slot, side // 2],
                device_id=device(y, r_at[side], x),
                device_id_type=MESH,
            )
            for side in (0, 2)
        ]

    def spread(kind, slot):
        for copy in r_copies(kind, slot):
            copy.start()

    def forward(kind):
        y_copy(kind).wait_recv()
        spread(kind, BEYOND)

    def wait_rows(kind, slot):
        for copy in r_copies(kind, slot):
            copy.wait_recv()

    send_heads(KV, y_far)
    loads[6].wait()
    listed[0:TW, 0:27] = neighbours[...].astype(F32)
    for to_y in y_far:
        pltpu.make_async_remote_copy(
            src_ref=listed, dst_ref=lists.at[y_hi, slot_of(y)],
            send_sem=list_send, recv_sem=list_recv,
            device_id=device(to_y, r, x), device_id_type=MESH,
        ).start()

    loads[5].wait()
    factor = query_scale[...] * HD ** (-0.5)
    loads[2].wait()
    put(QD, 0, (raw[2].astype(F32) * factor).astype(BF16))
    loads[3].wait()
    put(QD, 1, raw[3])

    wait_heads(KV, INNER)
    y_copy(KV).start()
    spread(KV, INNER)
    send_heads(QD, y_far)
    wait_heads(KV, OUTER)
    spread(KV, OUTER)

    pltpu.make_async_copy(lists, lists, list_recv).wait()
    shape = (BLOCKS * 8, 128)
    line = lax.broadcasted_iota(jnp.int32, shape, 0)
    column = line % 8
    block_of = line // 8
    key_slot = block_of // 3
    key_frame = jnp.where(
        key_slot == 0, frame_of[0], jnp.where(key_slot == 1, frame_of[1], frame_of[2])
    )
    key_row = r + block_of % 3 - 1
    real = (column < TW) & (key_row >= 0) & (key_row < rows)
    ids = jnp.where(real, (key_frame * rows + key_row) * TW + column, -5).astype(F32)
    lane_tile = lax.broadcasted_iota(jnp.int32, (BLOCKS * 8, SLAB), 1) // TILE
    for slot in (OUTER, INNER):
        found = jnp.full((BLOCKS * 8, SLAB), HIDDEN, F32)
        for tile in range(TW):
            hit = jnp.max(
                jnp.where(lists[0, slot, tile : tile + 1, :] == ids, 0.0, HIDDEN),
                axis=1, keepdims=True,
            )
            found = jnp.where(lane_tile == tile, hit, found)
        bias[slot] = found.reshape(BLOCKS, 8, SLAB)

    forward(KV)
    wait_heads(QD, INNER)
    y_copy(QD).start()
    spread(QD, INNER)
    wait_heads(QD, OUTER)
    spread(QD, OUTER)

    def return_heads(kind, slot):
        columns_there = pl.ds(pl.multiple_of(my_head * HD, HD), HD)
        for to_x in x_at:
            for far_hi in range(2):
                to_y = frame_of[slot] + far_hi * FT
                token_chunk = to_x * 2 + far_hi
                part = pl.ds(pl.multiple_of(token_chunk * chunk, chunk), chunk)
                pltpu.make_async_remote_copy(
                    src_ref=results.at[kind, slot, :, part, :],
                    dst_ref=landed.at[kind, :, :, columns_there],
                    send_sem=out_send.at[kind],
                    recv_sem=out_recv.at[kind],
                    device_id=device(to_y, r, to_x),
                    device_id_type=MESH,
                ).start()

    def my_scale(scale):
        return scale[:, pl.ds(pl.multiple_of(my_head * HD, HD), HD)]

    def stat_copies(slot):
        return [
            pltpu.make_async_remote_copy(
                src_ref=stats_sent.at[slot, side, 0:2],
                dst_ref=stats.at[slot, 2 - side],
                send_sem=stat_send.at[slot, side // 2],
                recv_sem=stat_recv.at[slot, side // 2],
                device_id=device(y, r_at[side], x),
                device_id_type=MESH,
            )
            for side in (0, 2)
        ]

    def far_stat_copies():
        return [
            pltpu.make_async_remote_copy(
                src_ref=stats_sent.at[INNER, side, BEYOND],
                dst_ref=stats.at[BEYOND, 2 - side, INNER],
                send_sem=far_send.at[side],
                recv_sem=far_recv.at[side],
                device_id=device(y_partner, r_at[side], x),
                device_id_type=MESH,
            )
            for side in range(3)
        ]

    def query_side(slot, between):
        blocks = 9 if slot == INNER else 6
        queries = data[QD, slot, 1, 0]
        grads = data[QD, slot, 1, 1]

        def score(block, row_max):
            keys = data[KV, block // 3, block % 3, 0]
            part = by_key_tile(dot_nt(keys, queries), bias[slot, block])
            scores[block] = part
            return jnp.maximum(row_max, jnp.max(part, axis=0, keepdims=True))

        row_max = lax.fori_loop(
            0, blocks, score, jnp.full((1, SLAB), -3e38, F32), unroll=unroll
        )
        between()

        def attend(block, carry):
            total, attended = carry
            part = jnp.exp(scores[block] - row_max)
            low = part.astype(BF16)
            weights[block] = low
            total = total + jnp.sum(part, axis=0, keepdims=True)
            return total, attended + dot_tn(data[KV, block // 3, block % 3, 1], low)

        total, attended = lax.fori_loop(
            0, blocks, attend,
            (jnp.zeros((1, SLAB), F32), jnp.zeros((HD, SLAB), F32)), unroll=unroll,
        )
        inverse = 1.0 / total
        attended = (attended * inverse).astype(BF16).astype(F32)
        delta = jnp.sum(attended * grads.astype(F32).T, axis=0, keepdims=True)
        results[0, slot, 0] = attended.T.astype(BF16)
        log_total = row_max + jnp.log(total)
        line8 = lax.broadcasted_iota(jnp.int32, (8, SLAB), 0)
        for block in range(blocks):
            message = jnp.where(line8 == TW, delta, bias[slot, block] - log_total)
            if block % 3 == 1 and block < 6:
                stats[slot, 1, block // 3] = message
            else:
                stats_sent[slot, block % 3, block // 3] = message
        for copy in stat_copies(slot):
            copy.start()
        if slot == INNER:
            for copy in far_stat_copies():
                copy.start()
        delta_part = delta * inverse

        def slope(block, carry):
            grad_weights = dot_nt(data[KV, block // 3, block % 3, 1], grads)
            part = weights[block].astype(F32) * (grad_weights * inverse - delta_part)
            return carry + dot_tn(data[KV, block // 3, block % 3, 0], part.astype(BF16))

        grad_queries = lax.fori_loop(
            0, blocks, slope, jnp.zeros((HD, SLAB), F32), unroll=unroll
        )
        scale = my_scale(query_scale) * HD ** (-0.5)
        results[0, slot, 1] = (grad_queries.T * scale).astype(BF16)
        return_heads(0, slot)

    def key_side(slot):
        keys = data[KV, slot, 1, 0]
        values = data[KV, slot, 1, 1]

        def step(block, carry):
            grad_keys, grad_values = carry
            queries = data[QD, block // 3, block % 3, 0]
            grads = data[QD, block // 3, block % 3, 1]
            message = stats[block // 3, block % 3, slot]
            part = jnp.exp(by_key_tile(dot_nt(keys, queries), message))
            grad_weights = dot_nt(values, grads)
            slopes = (part * (grad_weights - message[TW : TW + 1])).astype(BF16)
            grad_values = grad_values + dot_nn(part.astype(BF16), grads)
            grad_keys = grad_keys + dot_nn(slopes, queries)
            return grad_keys, grad_values

        zero = jnp.zeros((SLAB, HD), F32)
        blocks = 9 if slot == INNER else 6
        grad_keys, grad_values = lax.fori_loop(0, blocks, step, (zero, zero), unroll=unroll)
        results[1, slot, 0] = (grad_keys * my_scale(key_scale)).astype(BF16)
        results[1, slot, 1] = grad_values.astype(BF16)
        return_heads(1, slot)

    wait_rows(KV, INNER)
    wait_rows(KV, OUTER)
    query_side(OUTER, lambda: forward(QD))
    wait_rows(KV, BEYOND)
    query_side(INNER, lambda: None)
    for slot in (OUTER, INNER):
        wait_rows(QD, slot)
        for copy in stat_copies(slot):
            copy.wait_recv()
    key_side(OUTER)
    wait_rows(QD, BEYOND)
    for copy in far_stat_copies():
        copy.wait_recv()
    key_side(INNER)

    for kind in range(2):
        pltpu.make_async_copy(landed.at[kind], landed.at[kind], out_recv.at[kind]).wait()
    sent = lists.at[0:2]
    pltpu.make_async_copy(sent, sent, list_send).wait()
    for kind in range(2):
        sent = stage.at[kind]
        pltpu.make_async_copy(sent, sent, a2a_send.at[kind]).wait()
        for slot in range(3):
            for copy in r_copies(kind, slot):
                copy.wait_send()
        y_copy(kind).wait_send()
        sent = results.at[kind]
        pltpu.make_async_copy(sent, sent, out_send.at[kind]).wait()
    for slot in (OUTER, INNER):
        for copy in stat_copies(slot):
            copy.wait_send()
    for copy in far_stat_copies():
        copy.wait_send()


def hand_out(landed, attention, grad_query, grad_key, grad_value, sems):
    targets = (attention, grad_query, grad_key, grad_value)
    copies = [
        pltpu.make_async_copy(landed.at[i // 2, i % 2], targets[i], sems.at[i]) for i in range(4)
    ]
    for copy in copies:
        copy.start()
    for copy in copies:
        copy.wait()


def local(query, key, value, grad_out, query_scale, key_scale, neighbours):
    rows = lax.axis_size("slab") // FT
    columns = lax.axis_size("head") // 2
    chunk, width = query.shape
    out = jax.ShapeDtypeStruct((chunk, width), BF16)
    hbm = pl.BlockSpec(memory_space=pltpu.HBM)
    dma = pltpu.SemaphoreType.DMA
    landed = pl.pallas_call(
        functools.partial(kernel, rows, columns, 3),
        out_shape=jax.ShapeDtypeStruct((2, 2, chunk, width), BF16),
        in_specs=[hbm] * 7,
        out_specs=hbm,
        scratch_shapes=[
            pltpu.VMEM((4, chunk, width), BF16),
            pltpu.VMEM((1, width), F32),
            pltpu.VMEM((1, width), F32),
            pltpu.VMEM(neighbours.shape, jnp.int32),
            pltpu.VMEM((2, 4 * columns, 2, chunk, HD), BF16),
            pltpu.VMEM((2, 3, 3, 2, SLAB, HD), BF16),
            pltpu.VMEM((8, 128), F32),
            pltpu.VMEM((2, 2, 8, 128), F32),
            pltpu.VMEM((2, BLOCKS, 8, SLAB), F32),
            pltpu.VMEM((BLOCKS, SLAB, SLAB), F32),
            pltpu.VMEM((BLOCKS, SLAB, SLAB), BF16),
            pltpu.VMEM((3, 3, 2, 8, SLAB), F32),
            pltpu.VMEM((2, 3, 3, 8, SLAB), F32),
            pltpu.VMEM((2, 2, 2, SLAB, HD), BF16),
            dma((7,)),
            dma((2,)),
            dma((2, 2)),
            dma,
            dma,
            dma((2, 7)),
            dma((2,)),
            dma((2, 3, 2)),
            dma((2, 2)),
            dma((2, 2)),
            dma((3,)),
            dma((3,)),
            dma((2,)),
            dma((2,)),
        ],
        compiler_params=pltpu.CompilerParams(
            collective_id=0, has_side_effects=True, vmem_limit_bytes=VMEM_BYTES
        ),
        name="tiles",
    )(
        query, key, value, grad_out,
        query_scale.reshape(1, width), key_scale.reshape(1, width), neighbours,
    )
    return pl.pallas_call(
        hand_out,
        out_shape=(out,) * 4,
        in_specs=[hbm],
        out_specs=(hbm,) * 4,
        scratch_shapes=[dma((4,))],
        compiler_params=pltpu.CompilerParams(vmem_limit_bytes=VMEM_BYTES),
        name="hand_out",
    )(landed)


def solution(mesh):
    token = P(("slab", "head"), None)
    return jax.shard_map(
        local,
        mesh=mesh,
        in_specs=(token, token, token, token, P(), P(), P("slab", None)),
        out_specs=(token,) * 4,
        check_vma=False,
    )
```

```python
import functools

import jax
import jax.numpy as jnp
from jax import lax
from jax.experimental import pallas as pl
from jax.experimental.pallas import tpu as pltpu
from jax.sharding import PartitionSpec as P

HD = 128
TILE = 64
FT = 4
TW = 4
SLAB = TILE * TW
RING = 2 * FT
BLOCKS = 9
OUTER, INNER, BEYOND = 0, 1, 2
HIDDEN = -1e30
MESH = pl.DeviceIdType.MESH
BF16 = jnp.bfloat16
F32 = jnp.float32
KV, QD = 0, 1
VMEM_BYTES = 58 * 1024 * 1024


def dot_nn(a, b):
    return lax.dot_general(a, b, (((1,), (0,)), ((), ())), preferred_element_type=F32)


def dot_nt(a, b):
    return lax.dot_general(a, b, (((1,), (1,)), ((), ())), preferred_element_type=F32)


def dot_tn(a, b):
    return lax.dot_general(a, b, (((0,), (0,)), ((), ())), preferred_element_type=F32)


def add_rows(scores, rows):
    shaped = scores.reshape(3, TILE, scores.shape[1]) + rows[:, None, :]
    return shaped.reshape(scores.shape)


def join(low, high, both):
    return jnp.concatenate(
        [low[:TILE], both(low[TILE:], high[: 2 * TILE]), high[2 * TILE :]], axis=0
    )


def fold(array, both):
    return both(both(array[:, :128], array[:, 128:256]), array[:, 256:])


def wide(column):
    return jnp.concatenate([column] * 3, axis=1)


def near(half):
    return slice(half * TILE, half * TILE + 3 * TILE)


def own(half):
    return slice(half * 2 * TILE, (half + 1) * 2 * TILE)


def kernel(
    rows, columns,
    query, key, value, grad_out, query_scale_in, key_scale_in, neighbours_in, landed,
    raw, query_scale, key_scale, neighbours,
    stage, data, listed, lists, bias, bias_rows, scores, weights, stats, stats_sent, results,
    in_sem, a2a_send, a2a_recv, list_send, list_recv, halo_send, y_recv, r_recv,
    stat_send, stat_recv, far_send, far_recv, out_send, out_recv,
):
    loads = [
        pltpu.make_async_copy(source, target, in_sem.at[i])
        for i, (source, target) in enumerate((
            (key, raw.at[0]), (value, raw.at[1]), (query, raw.at[2]), (grad_out, raw.at[3]),
            (key_scale_in, key_scale), (query_scale_in, query_scale),
            (neighbours_in, neighbours),
        ))
    ]
    for load in (loads[4], *loads[:4], *loads[5:]):
        load.start()

    slab = lax.axis_index("slab")
    head = lax.axis_index("head")
    y_lo, r = slab // rows, slab % rows
    x, y_hi = head // 2, head % 2
    y = y_hi * FT + y_lo
    chunk = SLAB // (2 * columns)
    half = 1 - y_lo // 2
    far_y = (1 - y_lo // 2) * 2
    y_far = (far_y, far_y + 1, far_y + FT, far_y + FT + 1)
    frame_of = (3 * half, 1 + half, 2 - half)

    def quarter(at_y):
        return ((at_y + RING - 1) % RING) // 2

    def slot_of(at_y):
        return ((at_y % FT + 1) % FT) // 2

    my_head = x * 4 + quarter(y)
    y_partner = (y + RING - 1 + 2 * (y % 2)) % RING

    def device(to_y, to_r, to_x):
        return {"slab": (to_y % FT) * rows + to_r, "head": to_x * 2 + to_y // FT}

    r_at = ((r + rows - 1) % rows, r, (r + 1) % rows)
    x_at = tuple((x + step) % columns for step in range(columns))

    barrier = pltpu.get_barrier_semaphore()
    peers = [device(to_y, r, to_x) for to_y in y_far for to_x in x_at]
    peers += [device(y, r_at[0], x), device(y, r_at[2], x)]
    peers += [device(y_partner, to_r, x) for to_r in r_at]
    for peer in peers:
        pl.semaphore_signal(barrier, 1, device_id=peer, device_id_type=MESH)
    listed[...] = jnp.full(listed.shape, -2.0, F32)

    def put(kind, which, array):
        for piece in range(4 * columns):
            stage[kind, piece, which] = array[:, piece * HD : (piece + 1) * HD]

    loads[4].wait()
    loads[0].wait()
    put(KV, 0, (raw[0].astype(F32) * key_scale[...]).astype(BF16))
    loads[1].wait()
    put(KV, 1, raw[1])
    pl.semaphore_wait(barrier, len(peers))

    my_rows = pl.ds(pl.multiple_of(head * chunk, chunk), chunk)

    def send_heads(kind, places):
        for to_x in x_at:
            for to_y in places:
                pltpu.make_async_remote_copy(
                    src_ref=stage.at[kind, to_x * 4 + quarter(to_y)],
                    dst_ref=data.at[kind, slot_of(y), 1, :, my_rows, :],
                    send_sem=a2a_send.at[kind],
                    recv_sem=a2a_recv.at[kind, slot_of(y)],
                    device_id=device(to_y, r, to_x),
                    device_id_type=MESH,
                ).start()

    def wait_heads(kind, slot):
        whole = data.at[kind, slot, 1]
        pltpu.make_async_copy(whole, whole, a2a_recv.at[kind, slot]).wait()

    def y_copy(kind):
        return pltpu.make_async_remote_copy(
            src_ref=data.at[kind, INNER, 1],
            dst_ref=data.at[kind, BEYOND, 1],
            send_sem=halo_send.at[kind, 6],
            recv_sem=y_recv.at[kind],
            device_id=device(y_partner, r, x),
            device_id_type=MESH,
        )

    def r_copies(kind, slot):
        return [
            pltpu.make_async_remote_copy(
                src_ref=data.at[kind, slot, 1],
                dst_ref=data.at[kind, slot, 2 - side],
                send_sem=halo_send.at[kind, slot * 2 + side // 2],
                recv_sem=r_recv.at[kind, slot, side // 2],
                device_id=device(y, r_at[side], x),
                device_id_type=MESH,
            )
            for side in (0, 2)
        ]

    def spread(kind, slot):
        for copy in r_copies(kind, slot):
            copy.start()

    def forward(kind):
        y_copy(kind).wait_recv()
        spread(kind, BEYOND)

    def wait_rows(kind, slot):
        for copy in r_copies(kind, slot):
            copy.wait_recv()

    send_heads(KV, y_far)
    loads[6].wait()
    listed[0:TW, 0:27] = neighbours[...].astype(F32)
    for to_y in y_far:
        pltpu.make_async_remote_copy(
            src_ref=listed, dst_ref=lists.at[y_hi, slot_of(y)],
            send_sem=list_send, recv_sem=list_recv,
            device_id=device(to_y, r, x), device_id_type=MESH,
        ).start()

    loads[5].wait()
    factor = query_scale[...] * HD ** (-0.5)
    loads[2].wait()
    put(QD, 0, (raw[2].astype(F32) * factor).astype(BF16))
    loads[3].wait()
    put(QD, 1, raw[3])

    wait_heads(KV, INNER)
    y_copy(KV).start()
    spread(KV, INNER)
    send_heads(QD, y_far)
    wait_heads(KV, OUTER)
    spread(KV, OUTER)

    pltpu.make_async_copy(lists, lists, list_recv).wait()
    shape = (BLOCKS * 8, 128)
    line = lax.broadcasted_iota(jnp.int32, shape, 0)
    column = line % 8
    block_of = line // 8
    key_slot = block_of // 3
    key_frame = jnp.where(
        key_slot == 0, frame_of[0], jnp.where(key_slot == 1, frame_of[1], frame_of[2])
    )
    key_row = r + block_of % 3 - 1
    real = (column < TW) & (key_row >= 0) & (key_row < rows)
    ids = jnp.where(real, (key_frame * rows + key_row) * TW + column, -5).astype(F32)
    lane_tile = lax.broadcasted_iota(jnp.int32, (BLOCKS * 8, SLAB), 1) // TILE
    lane = lax.broadcasted_iota(jnp.int32, (8, 128), 1)
    for slot in (OUTER, INNER):
        found = jnp.full((BLOCKS * 8, SLAB), HIDDEN, F32)
        for tile in range(TW):
            hit = jnp.max(
                jnp.where(lists[0, slot, tile : tile + 1, :] == ids, 0.0, HIDDEN),
                axis=1, keepdims=True,
            )
            found = jnp.where(lane_tile == tile, hit, found)
        bias[slot] = found.reshape(BLOCKS, 8, SLAB)
        turned = jnp.concatenate(
            [
                jnp.concatenate(
                    [found[:, tile * TILE : tile * TILE + 1] for tile in range(TW)]
                    + [jnp.full((BLOCKS * 8, 124), HIDDEN, F32)],
                    axis=1,
                ),
                jnp.full((56, 128), HIDDEN, F32),
            ],
            axis=0,
        ).T[:8]
        for key_block in range(BLOCKS):
            for side in range(2):
                at = key_block * 8 + side * 2
                bias_rows[slot, key_block // 3, side, :, pl.ds(key_block % 3 * 128, 128)] = jnp.where(
                    lane < TILE, turned[:, at : at + 1], turned[:, at + 1 : at + 2]
                )

    forward(KV)
    wait_heads(QD, INNER)
    y_copy(QD).start()
    spread(QD, INNER)
    wait_heads(QD, OUTER)
    spread(QD, OUTER)

    def return_heads(kind, slot):
        columns_there = pl.ds(pl.multiple_of(my_head * HD, HD), HD)
        for to_x in x_at:
            for far_hi in range(2):
                to_y = frame_of[slot] + far_hi * FT
                token_chunk = to_x * 2 + far_hi
                part = pl.ds(pl.multiple_of(token_chunk * chunk, chunk), chunk)
                pltpu.make_async_remote_copy(
                    src_ref=results.at[kind, slot, :, part, :],
                    dst_ref=landed.at[kind, :, :, columns_there],
                    send_sem=out_send.at[kind],
                    recv_sem=out_recv.at[kind],
                    device_id=device(to_y, r, to_x),
                    device_id_type=MESH,
                ).start()

    def my_scale(scale):
        return scale[:, pl.ds(pl.multiple_of(my_head * HD, HD), HD)]

    def stat_copies(slot):
        return [
            pltpu.make_async_remote_copy(
                src_ref=stats_sent.at[slot, side, 0:2],
                dst_ref=stats.at[slot, 2 - side],
                send_sem=stat_send.at[slot, side // 2],
                recv_sem=stat_recv.at[slot, side // 2],
                device_id=device(y, r_at[side], x),
                device_id_type=MESH,
            )
            for side in (0, 2)
        ]

    def far_stat_copies():
        return [
            pltpu.make_async_remote_copy(
                src_ref=stats_sent.at[INNER, side, BEYOND],
                dst_ref=stats.at[BEYOND, 2 - side, INNER],
                send_sem=far_send.at[side],
                recv_sem=far_recv.at[side],
                device_id=device(y_partner, r_at[side], x),
                device_id_type=MESH,
            )
            for side in range(3)
        ]

    def rows_of(kind, slot, which, side):
        return jnp.concatenate(
            [data[kind, slot, row, which, own(side), :] for row in range(3)], axis=0
        )

    def query_side(slot, arrive, between):
        key_slots = (INNER, OUTER) if slot == OUTER else (INNER, OUTER, BEYOND)
        parts = [(key_slot, side) for key_slot in key_slots for side in range(2)]
        peak = [jnp.full((3 * TILE, 128), -3e38, F32) for side in range(2)]
        for key_slot, side in parts:
            if side == 0:
                arrive(key_slot)
            part = add_rows(
                dot_nt(data[QD, slot, 1, 0, near(side), :], rows_of(KV, key_slot, 0, side)),
                bias_rows[slot, key_slot, side, side : side + 3, :],
            )
            scores[key_slot, side] = part
            peak[side] = jnp.maximum(peak[side], fold(part, jnp.maximum))
        row_max = jnp.max(join(*peak, jnp.maximum), axis=1, keepdims=True)
        between()

        row_wide = jnp.broadcast_to(row_max, (SLAB, 128))
        totals = [jnp.zeros((3 * TILE, 128), F32) for side in range(2)]
        sums = [jnp.zeros((3 * TILE, HD), F32) for side in range(2)]
        for key_slot, side in parts:
            part = jnp.exp(scores[key_slot, side] - wide(row_wide[near(side)]))
            low = part.astype(BF16)
            weights[key_slot, side] = low
            totals[side] = totals[side] + fold(part, jnp.add)
            sums[side] = sums[side] + dot_nn(low, rows_of(KV, key_slot, 1, side))
        total = jnp.sum(join(*totals, jnp.add), axis=1, keepdims=True)
        inverse = jnp.broadcast_to(1.0 / total, (SLAB, 128))
        attended = (join(*sums, jnp.add) * inverse).astype(BF16)
        results[0, slot, 0] = attended
        grads = data[QD, slot, 1, 1].astype(F32)
        delta = jnp.sum(attended.astype(F32) * grads, axis=1, keepdims=True)
        log_total = row_max + jnp.log(total)
        lane = lax.broadcasted_iota(jnp.int32, (SLAB, 128), 1)
        turned = jnp.where(lane == 0, log_total, delta).T
        log_row, delta_row = turned[0:1], turned[1:2]
        line8 = lax.broadcasted_iota(jnp.int32, (8, SLAB), 0)
        for key_slot in key_slots:
            for row in range(3):
                message = jnp.where(
                    line8 == TW, delta_row, bias[slot, key_slot * 3 + row] - log_row
                )
                if row == 1 and key_slot != BEYOND:
                    stats[slot, 1, key_slot] = message
                else:
                    stats_sent[slot, row, key_slot] = message
        for copy in stat_copies(slot):
            copy.start()
        if slot == INNER:
            for copy in far_stat_copies():
                copy.start()
        delta_part = delta * inverse

        sums = [jnp.zeros((3 * TILE, HD), F32) for side in range(2)]
        for key_slot, side in parts:
            grad_weights = dot_nt(
                data[QD, slot, 1, 1, near(side), :], rows_of(KV, key_slot, 1, side)
            )
            part = weights[key_slot, side].astype(F32) * (
                grad_weights * wide(inverse[near(side)]) - wide(delta_part[near(side)])
            )
            sums[side] = sums[side] + dot_nn(part.astype(BF16), rows_of(KV, key_slot, 0, side))
        scale = my_scale(query_scale) * HD ** (-0.5)
        results[0, slot, 1] = (join(*sums, jnp.add) * scale).astype(BF16)
        return_heads(0, slot)

    def key_side(slot, arrive):
        query_slots = (INNER, OUTER) if slot == OUTER else (INNER, OUTER, BEYOND)
        key_sums = [jnp.zeros((3 * TILE, HD), F32) for side in range(2)]
        value_sums = [jnp.zeros((3 * TILE, HD), F32) for side in range(2)]
        for query_slot in query_slots:
            arrive(query_slot)
            for side in range(2):
                message = jnp.concatenate(
                    [stats[query_slot, row, slot, :, own(side)] for row in range(3)], axis=1
                )
                queries = rows_of(QD, query_slot, 0, side)
                grads = rows_of(QD, query_slot, 1, side)
                part = jnp.exp(add_rows(
                    dot_nt(data[KV, slot, 1, 0, near(side), :], queries),
                    message[side : side + 3],
                ))
                grad_weights = dot_nt(data[KV, slot, 1, 1, near(side), :], grads)
                slopes = (part * (grad_weights - message[TW : TW + 1])).astype(BF16)
                value_sums[side] = value_sums[side] + dot_nn(part.astype(BF16), grads)
                key_sums[side] = key_sums[side] + dot_nn(slopes, queries)
        grad_keys = join(*key_sums, jnp.add)
        results[1, slot, 0] = (grad_keys * my_scale(key_scale)).astype(BF16)
        results[1, slot, 1] = join(*value_sums, jnp.add).astype(BF16)
        return_heads(1, slot)

    def beyond_arrives(key_slot):
        if key_slot == BEYOND:
            wait_rows(KV, BEYOND)

    def queries_arrive(query_slot):
        if query_slot == BEYOND:
            wait_rows(QD, BEYOND)
            for copy in far_stat_copies():
                copy.wait_recv()

    query_side(OUTER, lambda key_slot: wait_rows(KV, key_slot), lambda: forward(QD))
    query_side(INNER, beyond_arrives, lambda: None)
    for slot in (INNER, OUTER):
        wait_rows(QD, slot)
        for copy in stat_copies(slot):
            copy.wait_recv()
    key_side(OUTER, lambda query_slot: None)
    key_side(INNER, queries_arrive)

    for kind in range(2):
        pltpu.make_async_copy(landed.at[kind], landed.at[kind], out_recv.at[kind]).wait()
    sent = lists.at[0:2]
    pltpu.make_async_copy(sent, sent, list_send).wait()
    for kind in range(2):
        sent = stage.at[kind]
        pltpu.make_async_copy(sent, sent, a2a_send.at[kind]).wait()
        for slot in range(3):
            for copy in r_copies(kind, slot):
                copy.wait_send()
        y_copy(kind).wait_send()
        sent = results.at[kind]
        pltpu.make_async_copy(sent, sent, out_send.at[kind]).wait()
    for slot in (OUTER, INNER):
        for copy in stat_copies(slot):
            copy.wait_send()
    for copy in far_stat_copies():
        copy.wait_send()


def hand_out(landed, attention, grad_query, grad_key, grad_value, held, sems):
    targets = (attention, grad_query, grad_key, grad_value)
    loads = [
        pltpu.make_async_copy(landed.at[i // 2, i % 2], held.at[i], sems.at[0, i])
        for i in range(4)
    ]
    stores = [pltpu.make_async_copy(held.at[i], targets[i], sems.at[1, i]) for i in range(4)]
    for load in loads:
        load.start()
    for load, store in zip(loads, stores):
        load.wait()
        store.start()
    for store in stores:
        store.wait()


def local(query, key, value, grad_out, query_scale, key_scale, neighbours):
    rows = lax.axis_size("slab") // FT
    columns = lax.axis_size("head") // 2
    chunk, width = query.shape
    out = jax.ShapeDtypeStruct((chunk, width), BF16)
    hbm = pl.BlockSpec(memory_space=pltpu.HBM)
    dma = pltpu.SemaphoreType.DMA
    landed = pl.pallas_call(
        functools.partial(kernel, rows, columns),
        out_shape=jax.ShapeDtypeStruct((2, 2, chunk, width), BF16),
        in_specs=[hbm] * 7,
        out_specs=hbm,
        scratch_shapes=[
            pltpu.VMEM((4, chunk, width), BF16),
            pltpu.VMEM((1, width), F32),
            pltpu.VMEM((1, width), F32),
            pltpu.VMEM(neighbours.shape, jnp.int32),
            pltpu.VMEM((2, 4 * columns, 2, chunk, HD), BF16),
            pltpu.VMEM((2, 3, 3, 2, SLAB, HD), BF16),
            pltpu.VMEM((8, 128), F32),
            pltpu.VMEM((2, 2, 8, 128), F32),
            pltpu.VMEM((2, BLOCKS, 8, SLAB), F32),
            pltpu.VMEM((2, 3, 2, 8, 3 * 128), F32),
            pltpu.VMEM((3, 2, 3 * TILE, 3 * 128), F32),
            pltpu.VMEM((3, 2, 3 * TILE, 3 * 128), BF16),
            pltpu.VMEM((3, 3, 2, 8, SLAB), F32),
            pltpu.VMEM((2, 3, 3, 8, SLAB), F32),
            pltpu.VMEM((2, 2, 2, SLAB, HD), BF16),
            dma((7,)),
            dma((2,)),
            dma((2, 2)),
            dma,
            dma,
            dma((2, 7)),
            dma((2,)),
            dma((2, 3, 2)),
            dma((2, 2)),
            dma((2, 2)),
            dma((3,)),
            dma((3,)),
            dma((2,)),
            dma((2,)),
        ],
        compiler_params=pltpu.CompilerParams(
            collective_id=0, has_side_effects=True, vmem_limit_bytes=VMEM_BYTES
        ),
        name="tiles",
    )(
        query, key, value, grad_out,
        query_scale.reshape(1, width), key_scale.reshape(1, width), neighbours,
    )
    return pl.pallas_call(
        hand_out,
        out_shape=(out,) * 4,
        in_specs=[hbm],
        out_specs=(hbm,) * 4,
        scratch_shapes=[pltpu.VMEM((4, chunk, width), BF16), dma((2, 4))],
        compiler_params=pltpu.CompilerParams(vmem_limit_bytes=VMEM_BYTES),
        name="hand_out",
    )(landed)


def solution(mesh):
    token = P(("slab", "head"), None)
    return jax.shard_map(
        local,
        mesh=mesh,
        in_specs=(token, token, token, token, P(), P(), P("slab", None)),
        out_specs=(token,) * 4,
        check_vma=False,
    )
```

```python
import functools

import jax
import jax.numpy as jnp
from jax import lax
from jax.experimental import pallas as pl
from jax.experimental.pallas import tpu as pltpu
from jax.sharding import PartitionSpec as P

HD = 128
TILE = 64
FT = 4
TW = 4
SLAB = TILE * TW
RING = 2 * FT
BLOCKS = 9
OUTER, INNER, BEYOND = 0, 1, 2
HIDDEN = -1e30
MESH = pl.DeviceIdType.MESH
BF16 = jnp.bfloat16
F32 = jnp.float32
KV, QD = 0, 1
VMEM_BYTES = 58 * 1024 * 1024


def dot_nn(a, b):
    return lax.dot_general(a, b, (((1,), (0,)), ((), ())), preferred_element_type=F32)


def dot_nt(a, b):
    return lax.dot_general(a, b, (((1,), (1,)), ((), ())), preferred_element_type=F32)


def dot_tn(a, b):
    return lax.dot_general(a, b, (((0,), (0,)), ((), ())), preferred_element_type=F32)


def add_rows(scores, rows):
    shaped = scores.reshape(3, TILE, scores.shape[1]) + rows[:, None, :]
    return shaped.reshape(scores.shape)


def join(low, high, both):
    return jnp.concatenate(
        [low[:TILE], both(low[TILE:], high[: 2 * TILE]), high[2 * TILE :]], axis=0
    )


def fold(array, both):
    return both(both(array[:, :128], array[:, 128:256]), array[:, 256:])


def wide(column):
    return jnp.concatenate([column] * 3, axis=1)


def near(half):
    return slice(half * TILE, half * TILE + 3 * TILE)


def own(half):
    return slice(half * 2 * TILE, (half + 1) * 2 * TILE)


def kernel(
    rows, columns,
    query, key, value, grad_out, query_scale_in, key_scale_in, neighbours_in, landed,
    raw, query_scale, key_scale, neighbours,
    stage, data, listed, lists, bias, bias_rows, scores, weights, stats, stats_sent, results,
    in_sem, a2a_send, a2a_recv, list_send, list_recv, halo_send, y_recv, r_recv,
    stat_send, stat_recv, far_send, far_recv, out_send, out_recv,
):
    loads = [
        pltpu.make_async_copy(source, target, in_sem.at[i])
        for i, (source, target) in enumerate((
            (key, raw.at[0]), (value, raw.at[1]), (query, raw.at[2]), (grad_out, raw.at[3]),
            (key_scale_in, key_scale), (query_scale_in, query_scale),
            (neighbours_in, neighbours),
        ))
    ]
    for load in (loads[4], *loads[:4], *loads[5:]):
        load.start()

    slab = lax.axis_index("slab")
    head = lax.axis_index("head")
    y_lo, r = slab // rows, slab % rows
    x, y_hi = head // 2, head % 2
    y = y_hi * FT + y_lo
    chunk = SLAB // (2 * columns)
    half = 1 - y_lo // 2
    far_y = (1 - y_lo // 2) * 2
    y_far = (far_y, far_y + 1, far_y + FT, far_y + FT + 1)
    frame_of = (3 * half, 1 + half, 2 - half)

    def quarter(at_y):
        return ((at_y + RING - 1) % RING) // 2

    def slot_of(at_y):
        return ((at_y % FT + 1) % FT) // 2

    my_head = x * 4 + quarter(y)
    y_partner = (y + RING - 1 + 2 * (y % 2)) % RING

    def device(to_y, to_r, to_x):
        return {"slab": (to_y % FT) * rows + to_r, "head": to_x * 2 + to_y // FT}

    r_at = ((r + rows - 1) % rows, r, (r + 1) % rows)
    x_at = tuple((x + step) % columns for step in range(columns))

    def at_side(side):
        return pl.when(r < rows - 1) if side == 2 else pl.when(r >= 1 - side)

    barrier = pltpu.get_barrier_semaphore()

    def greet(peers):
        for peer in peers:
            pl.semaphore_signal(barrier, 1, device_id=peer, device_id_type=MESH)

    greet([device(to_y, r, to_x) for to_y in y_far for to_x in x_at])
    greet([device(y_partner, r, x)])
    for side in (0, 2):
        @at_side(side)
        def _():
            greet([device(y, r_at[side], x), device(y_partner, r_at[side], x)])

    for side in (0, 2):
        @pl.when(r == (rows - 1 if side == 2 else 0))
        def _():
            data[:, :, side] = jnp.zeros((2, 3, 2, SLAB, HD), BF16)
            stats[:, side] = jnp.full((3, 2, 8, SLAB), HIDDEN, F32)

    listed[...] = jnp.full(listed.shape, -2.0, F32)

    def put(kind, which, array):
        for piece in range(4 * columns):
            stage[kind, piece, which] = array[:, piece * HD : (piece + 1) * HD]

    loads[4].wait()
    loads[0].wait()
    put(KV, 0, (raw[0].astype(F32) * key_scale[...]).astype(BF16))
    loads[1].wait()
    put(KV, 1, raw[1])
    row_sides = (r + rows - 1) // rows + (2 * rows - 2 - r) // rows
    pl.semaphore_wait(barrier, 4 * columns + 1 + 2 * row_sides)

    my_rows = pl.ds(pl.multiple_of(head * chunk, chunk), chunk)

    def send_heads(kind, places):
        for to_x in x_at:
            for to_y in places:
                pltpu.make_async_remote_copy(
                    src_ref=stage.at[kind, to_x * 4 + quarter(to_y)],
                    dst_ref=data.at[kind, slot_of(y), 1, :, my_rows, :],
                    send_sem=a2a_send.at[kind],
                    recv_sem=a2a_recv.at[kind, slot_of(y)],
                    device_id=device(to_y, r, to_x),
                    device_id_type=MESH,
                ).start()

    def wait_heads(kind, slot):
        whole = data.at[kind, slot, 1]
        pltpu.make_async_copy(whole, whole, a2a_recv.at[kind, slot]).wait()

    def y_copy(kind):
        return pltpu.make_async_remote_copy(
            src_ref=data.at[kind, INNER, 1],
            dst_ref=data.at[kind, BEYOND, 1],
            send_sem=halo_send.at[kind, 6],
            recv_sem=y_recv.at[kind],
            device_id=device(y_partner, r, x),
            device_id_type=MESH,
        )

    def start_rows(copies):
        for side, copy in copies.items():
            at_side(side)(copy.start)

    def sent_rows(copies):
        for side, copy in copies.items():
            at_side(side)(copy.wait_send)

    def came_rows(copies):
        for side, copy in copies.items():
            at_side(2 - side)(copy.wait_recv)

    def r_copies(kind, slot):
        return {
            side: pltpu.make_async_remote_copy(
                src_ref=data.at[kind, slot, 1],
                dst_ref=data.at[kind, slot, 2 - side],
                send_sem=halo_send.at[kind, slot * 2 + side // 2],
                recv_sem=r_recv.at[kind, slot, side // 2],
                device_id=device(y, r_at[side], x),
                device_id_type=MESH,
            )
            for side in (0, 2)
        }

    def spread(kind, slot):
        start_rows(r_copies(kind, slot))

    def forward(kind):
        y_copy(kind).wait_recv()
        spread(kind, BEYOND)

    def wait_rows(kind, slot):
        came_rows(r_copies(kind, slot))

    send_heads(KV, y_far)
    loads[6].wait()
    listed[0:TW, 0:27] = neighbours[...].astype(F32)
    for to_y in y_far:
        pltpu.make_async_remote_copy(
            src_ref=listed, dst_ref=lists.at[y_hi, slot_of(y)],
            send_sem=list_send, recv_sem=list_recv,
            device_id=device(to_y, r, x), device_id_type=MESH,
        ).start()

    loads[5].wait()
    factor = query_scale[...] * HD ** (-0.5)
    loads[2].wait()
    put(QD, 0, (raw[2].astype(F32) * factor).astype(BF16))
    loads[3].wait()
    put(QD, 1, raw[3])

    send_heads(QD, y_far)
    wait_heads(KV, INNER)
    y_copy(KV).start()
    spread(KV, INNER)
    wait_heads(KV, OUTER)
    spread(KV, OUTER)

    pltpu.make_async_copy(lists, lists, list_recv).wait()
    shape = (BLOCKS * 8, 128)
    line = lax.broadcasted_iota(jnp.int32, shape, 0)
    column = line % 8
    block_of = line // 8
    key_slot = block_of // 3
    key_frame = jnp.where(
        key_slot == 0, frame_of[0], jnp.where(key_slot == 1, frame_of[1], frame_of[2])
    )
    key_row = r + block_of % 3 - 1
    real = (column < TW) & (key_row >= 0) & (key_row < rows)
    ids = jnp.where(real, (key_frame * rows + key_row) * TW + column, -5).astype(F32)
    lane_tile = lax.broadcasted_iota(jnp.int32, (BLOCKS * 8, SLAB), 1) // TILE
    lane = lax.broadcasted_iota(jnp.int32, (8, 128), 1)
    for slot in (OUTER, INNER):
        found = jnp.full((BLOCKS * 8, SLAB), HIDDEN, F32)
        for tile in range(TW):
            hit = jnp.max(
                jnp.where(lists[0, slot, tile : tile + 1, :] == ids, 0.0, HIDDEN),
                axis=1, keepdims=True,
            )
            found = jnp.where(lane_tile == tile, hit, found)
        bias[slot] = found.reshape(BLOCKS, 8, SLAB)
        turned = jnp.concatenate(
            [
                jnp.concatenate(
                    [found[:, tile * TILE : tile * TILE + 1] for tile in range(TW)]
                    + [jnp.full((BLOCKS * 8, 124), HIDDEN, F32)],
                    axis=1,
                ),
                jnp.full((56, 128), HIDDEN, F32),
            ],
            axis=0,
        ).T[:8]
        for key_block in range(BLOCKS):
            for side in range(2):
                at = key_block * 8 + side * 2
                bias_rows[slot, key_block // 3, side, :, pl.ds(key_block % 3 * 128, 128)] = jnp.where(
                    lane < TILE, turned[:, at : at + 1], turned[:, at + 1 : at + 2]
                )

    forward(KV)
    wait_heads(QD, INNER)
    y_copy(QD).start()
    spread(QD, INNER)
    wait_heads(QD, OUTER)
    spread(QD, OUTER)

    def return_heads(kind, slot):
        for to_x in x_at:
            for far_hi in range(2):
                to_y = frame_of[slot] + far_hi * FT
                token_chunk = to_x * 2 + far_hi
                part = pl.ds(pl.multiple_of(token_chunk * chunk, chunk), chunk)
                pltpu.make_async_remote_copy(
                    src_ref=results.at[kind, slot, :, part, :],
                    dst_ref=landed.at[kind, my_head],
                    send_sem=out_send.at[kind],
                    recv_sem=out_recv.at[kind],
                    device_id=device(to_y, r, to_x),
                    device_id_type=MESH,
                ).start()

    def my_scale(scale):
        return scale[:, pl.ds(pl.multiple_of(my_head * HD, HD), HD)]

    def stat_copies(slot):
        return {
            side: pltpu.make_async_remote_copy(
                src_ref=stats_sent.at[slot, side, 0:2],
                dst_ref=stats.at[slot, 2 - side],
                send_sem=stat_send.at[slot, side // 2],
                recv_sem=stat_recv.at[slot, side // 2],
                device_id=device(y, r_at[side], x),
                device_id_type=MESH,
            )
            for side in (0, 2)
        }

    def far_stat_copies():
        return {
            side: pltpu.make_async_remote_copy(
                src_ref=stats_sent.at[INNER, side, BEYOND],
                dst_ref=stats.at[BEYOND, 2 - side, INNER],
                send_sem=far_send.at[side],
                recv_sem=far_recv.at[side],
                device_id=device(y_partner, r_at[side], x),
                device_id_type=MESH,
            )
            for side in range(3)
        }

    def rows_of(kind, slot, which, side):
        return jnp.concatenate(
            [data[kind, slot, row, which, own(side), :] for row in range(3)], axis=0
        )

    def query_side(slot, arrive, between):
        key_slots = (INNER, OUTER) if slot == OUTER else (INNER, OUTER, BEYOND)
        parts = [(key_slot, side) for key_slot in key_slots for side in range(2)]
        peak = [jnp.full((3 * TILE, 128), -3e38, F32) for side in range(2)]
        for key_slot, side in parts:
            if side == 0:
                arrive(key_slot)
            part = add_rows(
                dot_nt(data[QD, slot, 1, 0, near(side), :], rows_of(KV, key_slot, 0, side)),
                bias_rows[slot, key_slot, side, side : side + 3, :],
            )
            scores[key_slot, side] = part
            peak[side] = jnp.maximum(peak[side], fold(part, jnp.maximum))
        row_max = jnp.max(join(*peak, jnp.maximum), axis=1, keepdims=True)
        between()

        row_wide = jnp.broadcast_to(row_max, (SLAB, 128))
        totals = [jnp.zeros((3 * TILE, 128), F32) for side in range(2)]
        sums = [jnp.zeros((3 * TILE, HD), F32) for side in range(2)]
        for key_slot, side in parts:
            part = jnp.exp(scores[key_slot, side] - wide(row_wide[near(side)]))
            low = part.astype(BF16)
            weights[key_slot, side] = low
            totals[side] = totals[side] + fold(part, jnp.add)
            sums[side] = sums[side] + dot_nn(low, rows_of(KV, key_slot, 1, side))
        total = jnp.sum(join(*totals, jnp.add), axis=1, keepdims=True)
        inverse = jnp.broadcast_to(1.0 / total, (SLAB, 128))
        attended = (join(*sums, jnp.add) * inverse).astype(BF16)
        results[0, slot, 0] = attended
        grads = data[QD, slot, 1, 1].astype(F32)
        delta = jnp.sum(attended.astype(F32) * grads, axis=1, keepdims=True)
        log_total = row_max + jnp.log(total)
        lane = lax.broadcasted_iota(jnp.int32, (SLAB, 128), 1)
        turned = jnp.where(lane == 0, log_total, delta).T
        log_row, delta_row = turned[0:1], turned[1:2]
        line8 = lax.broadcasted_iota(jnp.int32, (8, SLAB), 0)
        for key_slot in key_slots:
            for row in range(3):
                message = jnp.where(
                    line8 == TW, delta_row, bias[slot, key_slot * 3 + row] - log_row
                )
                if row == 1 and key_slot != BEYOND:
                    stats[slot, 1, key_slot] = message
                else:
                    stats_sent[slot, row, key_slot] = message
        start_rows(stat_copies(slot))
        if slot == INNER:
            start_rows(far_stat_copies())
        delta_part = delta * inverse

        sums = [jnp.zeros((3 * TILE, HD), F32) for side in range(2)]
        for key_slot, side in parts:
            grad_weights = dot_nt(
                data[QD, slot, 1, 1, near(side), :], rows_of(KV, key_slot, 1, side)
            )
            part = weights[key_slot, side].astype(F32) * (
                grad_weights * wide(inverse[near(side)]) - wide(delta_part[near(side)])
            )
            sums[side] = sums[side] + dot_nn(part.astype(BF16), rows_of(KV, key_slot, 0, side))
        scale = my_scale(query_scale) * HD ** (-0.5)
        results[0, slot, 1] = (join(*sums, jnp.add) * scale).astype(BF16)
        return_heads(0, slot)

    def key_side(slot, arrive):
        query_slots = (INNER, OUTER) if slot == OUTER else (INNER, OUTER, BEYOND)
        key_sums = [jnp.zeros((3 * TILE, HD), F32) for side in range(2)]
        value_sums = [jnp.zeros((3 * TILE, HD), F32) for side in range(2)]
        for query_slot in query_slots:
            arrive(query_slot)
            for side in range(2):
                message = jnp.concatenate(
                    [stats[query_slot, row, slot, :, own(side)] for row in range(3)], axis=1
                )
                queries = rows_of(QD, query_slot, 0, side)
                grads = rows_of(QD, query_slot, 1, side)
                part = jnp.exp(add_rows(
                    dot_nt(data[KV, slot, 1, 0, near(side), :], queries),
                    message[side : side + 3],
                ))
                grad_weights = dot_nt(data[KV, slot, 1, 1, near(side), :], grads)
                slopes = (part * (grad_weights - message[TW : TW + 1])).astype(BF16)
                value_sums[side] = value_sums[side] + dot_nn(part.astype(BF16), grads)
                key_sums[side] = key_sums[side] + dot_nn(slopes, queries)
        grad_keys = join(*key_sums, jnp.add)
        results[1, slot, 0] = (grad_keys * my_scale(key_scale)).astype(BF16)
        results[1, slot, 1] = join(*value_sums, jnp.add).astype(BF16)
        return_heads(1, slot)

    def beyond_arrives(key_slot):
        if key_slot == BEYOND:
            wait_rows(KV, BEYOND)

    def queries_arrive(query_slot):
        if query_slot == BEYOND:
            wait_rows(QD, BEYOND)
            came_rows(far_stat_copies())

    query_side(OUTER, lambda key_slot: wait_rows(KV, key_slot), lambda: forward(QD))
    query_side(INNER, beyond_arrives, lambda: None)
    for slot in (INNER, OUTER):
        wait_rows(QD, slot)
        came_rows(stat_copies(slot))
    key_side(OUTER, lambda query_slot: None)
    key_side(INNER, queries_arrive)

    for kind in range(2):
        pltpu.make_async_copy(landed.at[kind], landed.at[kind], out_recv.at[kind]).wait()
    sent = lists.at[0:2]
    pltpu.make_async_copy(sent, sent, list_send).wait()
    for kind in range(2):
        sent = stage.at[kind]
        pltpu.make_async_copy(sent, sent, a2a_send.at[kind]).wait()
        for slot in range(3):
            sent_rows(r_copies(kind, slot))
        y_copy(kind).wait_send()
        sent = results.at[kind]
        pltpu.make_async_copy(sent, sent, out_send.at[kind]).wait()
    for slot in (OUTER, INNER):
        sent_rows(stat_copies(slot))
    sent_rows(far_stat_copies())


def hand_out(landed, attention, grad_query, grad_key, grad_value, pieces, held, sems):
    targets = (attention, grad_query, grad_key, grad_value)
    loads = [
        pltpu.make_async_copy(landed.at[kind], pieces.at[kind], sems.at[0, kind])
        for kind in range(2)
    ]
    stores = [pltpu.make_async_copy(held.at[i], targets[i], sems.at[1, i]) for i in range(4)]
    for load in loads:
        load.start()
    for i in range(4):
        if i % 2 == 0:
            loads[i // 2].wait()
        for head in range(landed.shape[1]):
            held[i, :, head * HD : (head + 1) * HD] = pieces[i // 2, head, i % 2]
        stores[i].start()
    for store in stores:
        store.wait()


def local(query, key, value, grad_out, query_scale, key_scale, neighbours):
    rows = lax.axis_size("slab") // FT
    columns = lax.axis_size("head") // 2
    chunk, width = query.shape
    out = jax.ShapeDtypeStruct((chunk, width), BF16)
    landing = (2, width // HD, 2, chunk, HD)
    hbm = pl.BlockSpec(memory_space=pltpu.HBM)
    dma = pltpu.SemaphoreType.DMA
    landed = pl.pallas_call(
        functools.partial(kernel, rows, columns),
        out_shape=jax.ShapeDtypeStruct(landing, BF16),
        in_specs=[hbm] * 7,
        out_specs=hbm,
        scratch_shapes=[
            pltpu.VMEM((4, chunk, width), BF16),
            pltpu.VMEM((1, width), F32),
            pltpu.VMEM((1, width), F32),
            pltpu.VMEM(neighbours.shape, jnp.int32),
            pltpu.VMEM((2, 4 * columns, 2, chunk, HD), BF16),
            pltpu.VMEM((2, 3, 3, 2, SLAB, HD), BF16),
            pltpu.VMEM((8, 128), F32),
            pltpu.VMEM((2, 2, 8, 128), F32),
            pltpu.VMEM((2, BLOCKS, 8, SLAB), F32),
            pltpu.VMEM((2, 3, 2, 8, 3 * 128), F32),
            pltpu.VMEM((3, 2, 3 * TILE, 3 * 128), F32),
            pltpu.VMEM((3, 2, 3 * TILE, 3 * 128), BF16),
            pltpu.VMEM((3, 3, 2, 8, SLAB), F32),
            pltpu.VMEM((2, 3, 3, 8, SLAB), F32),
            pltpu.VMEM((2, 2, 2, SLAB, HD), BF16),
            dma((7,)),
            dma((2,)),
            dma((2, 2)),
            dma,
            dma,
            dma((2, 7)),
            dma((2,)),
            dma((2, 3, 2)),
            dma((2, 2)),
            dma((2, 2)),
            dma((3,)),
            dma((3,)),
            dma((2,)),
            dma((2,)),
        ],
        compiler_params=pltpu.CompilerParams(
            collective_id=0, has_side_effects=True, vmem_limit_bytes=VMEM_BYTES
        ),
        name="tiles",
    )(
        query, key, value, grad_out,
        query_scale.reshape(1, width), key_scale.reshape(1, width), neighbours,
    )
    return pl.pallas_call(
        hand_out,
        out_shape=(out,) * 4,
        in_specs=[hbm],
        out_specs=(hbm,) * 4,
        scratch_shapes=[
            pltpu.VMEM(landing, BF16), pltpu.VMEM((4, chunk, width), BF16), dma((2, 4)),
        ],
        compiler_params=pltpu.CompilerParams(vmem_limit_bytes=VMEM_BYTES),
        name="hand_out",
    )(landed)


def solution(mesh):
    token = P(("slab", "head"), None)
    return jax.shard_map(
        local,
        mesh=mesh,
        in_specs=(token, token, token, token, P(), P(), P("slab", None)),
        out_specs=(token,) * 4,
        check_vma=False,
    )
```

```python
import functools

import jax
import jax.numpy as jnp
from jax import lax
from jax.experimental import pallas as pl
from jax.experimental.pallas import tpu as pltpu
from jax.sharding import PartitionSpec as P

HD = 128
TILE = 64
FT = 4
TW = 4
SLAB = TILE * TW
RING = 2 * FT
BLOCKS = 9
OUTER, INNER, BEYOND = 0, 1, 2
HIDDEN = -1e30
MESH = pl.DeviceIdType.MESH
BF16 = jnp.bfloat16
F32 = jnp.float32
KV, QD = 0, 1
VMEM_BYTES = 58 * 1024 * 1024


def dot_nn(a, b):
    return lax.dot_general(a, b, (((1,), (0,)), ((), ())), preferred_element_type=F32)


def dot_nt(a, b):
    return lax.dot_general(a, b, (((1,), (1,)), ((), ())), preferred_element_type=F32)


def dot_tn(a, b):
    return lax.dot_general(a, b, (((0,), (0,)), ((), ())), preferred_element_type=F32)


def add_rows(scores, rows):
    shaped = scores.reshape(3, TILE, scores.shape[1]) + rows[:, None, :]
    return shaped.reshape(scores.shape)


def join(low, high, both):
    return jnp.concatenate(
        [low[:TILE], both(low[TILE:], high[: 2 * TILE]), high[2 * TILE :]], axis=0
    )


def fold(array, both):
    return both(both(array[:, :128], array[:, 128:256]), array[:, 256:])


def wide(column):
    return jnp.concatenate([column] * 3, axis=1)


def near(half):
    return slice(half * TILE, half * TILE + 3 * TILE)


def own(half):
    return slice(half * 2 * TILE, (half + 1) * 2 * TILE)


def kernel(
    rows, columns,
    query, key, value, grad_out, query_scale_in, key_scale_in, neighbours_in, landed,
    raw, query_scale, key_scale, neighbours,
    stage, data, listed, lists, bias, bias_rows, scores, weights, stats, stats_sent, results,
    in_sem, a2a_send, a2a_recv, list_send, list_recv, halo_send, y_recv, r_recv,
    stat_send, stat_recv, far_send, far_recv, out_send, out_recv,
):
    loads = [
        pltpu.make_async_copy(source, target, in_sem.at[i])
        for i, (source, target) in enumerate((
            (key, raw.at[0]), (value, raw.at[1]), (query, raw.at[2]), (grad_out, raw.at[3]),
            (key_scale_in, key_scale), (query_scale_in, query_scale),
            (neighbours_in, neighbours),
        ))
    ]
    for load in (loads[4], *loads[:4], *loads[5:]):
        load.start()

    slab = lax.axis_index("slab")
    head = lax.axis_index("head")
    y_lo, r = slab // rows, slab % rows
    x, y_hi = head // 2, head % 2
    y = y_hi * FT + y_lo
    chunk = SLAB // (2 * columns)
    half = 1 - y_lo // 2
    far_y = (1 - y_lo // 2) * 2
    y_far = (far_y, far_y + 1, far_y + FT, far_y + FT + 1)
    frame_of = (3 * half, 1 + half, 2 - half)

    def quarter(at_y):
        return ((at_y + RING - 1) % RING) // 2

    def slot_of(at_y):
        return ((at_y % FT + 1) % FT) // 2

    my_head = x * 4 + quarter(y)
    y_partner = (y + RING - 1 + 2 * (y % 2)) % RING

    def device(to_y, to_r, to_x):
        return {"slab": (to_y % FT) * rows + to_r, "head": to_x * 2 + to_y // FT}

    r_at = ((r + rows - 1) % rows, r, (r + 1) % rows)
    x_at = tuple((x + step) % columns for step in range(columns))

    def at_side(side):
        return pl.when(r < rows - 1) if side == 2 else pl.when(r >= 1 - side)

    barrier = pltpu.get_barrier_semaphore()

    def greet(peers):
        for peer in peers:
            pl.semaphore_signal(barrier, 1, device_id=peer, device_id_type=MESH)

    greet([device(to_y, r, to_x) for to_y in y_far for to_x in x_at])
    greet([device(y_partner, r, x)])
    for side in (0, 2):
        @at_side(side)
        def _():
            greet([device(y, r_at[side], x), device(y_partner, r_at[side], x)])

    listed[...] = jnp.full(listed.shape, -2.0, F32)

    def put(kind, which, array):
        for piece in range(4 * columns):
            stage[kind, piece, which] = array[:, piece * HD : (piece + 1) * HD]

    loads[4].wait()
    loads[0].wait()
    put(KV, 0, (raw[0].astype(F32) * key_scale[...]).astype(BF16))
    loads[1].wait()
    put(KV, 1, raw[1])
    row_sides = (r + rows - 1) // rows + (2 * rows - 2 - r) // rows
    pl.semaphore_wait(barrier, 4 * columns + 1 + 2 * row_sides)

    my_rows = pl.ds(pl.multiple_of(head * chunk, chunk), chunk)

    def send_heads(kind, places):
        for to_x in x_at:
            for to_y in places:
                pltpu.make_async_remote_copy(
                    src_ref=stage.at[kind, to_x * 4 + quarter(to_y)],
                    dst_ref=data.at[kind, slot_of(y), 1, :, my_rows, :],
                    send_sem=a2a_send.at[kind],
                    recv_sem=a2a_recv.at[kind, slot_of(y)],
                    device_id=device(to_y, r, to_x),
                    device_id_type=MESH,
                ).start()

    def wait_heads(kind, slot):
        whole = data.at[kind, slot, 1]
        pltpu.make_async_copy(whole, whole, a2a_recv.at[kind, slot]).wait()

    def y_copy(kind):
        return pltpu.make_async_remote_copy(
            src_ref=data.at[kind, INNER, 1],
            dst_ref=data.at[kind, BEYOND, 1],
            send_sem=halo_send.at[kind, 6],
            recv_sem=y_recv.at[kind],
            device_id=device(y_partner, r, x),
            device_id_type=MESH,
        )

    def start_rows(copies):
        for side, copy in copies.items():
            at_side(side)(copy.start)

    def sent_rows(copies):
        for side, copy in copies.items():
            at_side(side)(copy.wait_send)

    def came_rows(copies):
        for side, copy in copies.items():
            at_side(2 - side)(copy.wait_recv)

    def r_copies(kind, slot):
        return {
            side: pltpu.make_async_remote_copy(
                src_ref=data.at[kind, slot, 1],
                dst_ref=data.at[kind, slot, 2 - side],
                send_sem=halo_send.at[kind, slot * 2 + side // 2],
                recv_sem=r_recv.at[kind, slot, side // 2],
                device_id=device(y, r_at[side], x),
                device_id_type=MESH,
            )
            for side in (0, 2)
        }

    def spread(kind, slot):
        start_rows(r_copies(kind, slot))

    def forward(kind):
        y_copy(kind).wait_recv()
        spread(kind, BEYOND)

    def wait_rows(kind, slot):
        came_rows(r_copies(kind, slot))

    send_heads(KV, y_far)
    loads[6].wait()
    listed[0:TW, 0:27] = neighbours[...].astype(F32)
    for to_y in y_far:
        pltpu.make_async_remote_copy(
            src_ref=listed, dst_ref=lists.at[y_hi, slot_of(y)],
            send_sem=list_send, recv_sem=list_recv,
            device_id=device(to_y, r, x), device_id_type=MESH,
        ).start()

    loads[5].wait()
    factor = query_scale[...] * HD ** (-0.5)
    loads[2].wait()
    put(QD, 0, (raw[2].astype(F32) * factor).astype(BF16))
    loads[3].wait()
    put(QD, 1, raw[3])

    send_heads(QD, y_far)

    for side in (0, 2):
        @pl.when(r == (rows - 1 if side == 2 else 0))
        def _():
            data[:, :, side] = jnp.zeros((2, 3, 2, SLAB, HD), BF16)
            stats[:, side] = jnp.full((3, 2, 8, SLAB), HIDDEN, F32)

    wait_heads(KV, INNER)
    y_copy(KV).start()
    spread(KV, INNER)
    wait_heads(KV, OUTER)
    spread(KV, OUTER)

    pltpu.make_async_copy(lists, lists, list_recv).wait()
    shape = (BLOCKS * 8, 128)
    line = lax.broadcasted_iota(jnp.int32, shape, 0)
    column = line % 8
    block_of = line // 8
    key_slot = block_of // 3
    key_frame = jnp.where(
        key_slot == 0, frame_of[0], jnp.where(key_slot == 1, frame_of[1], frame_of[2])
    )
    key_row = r + block_of % 3 - 1
    real = (column < TW) & (key_row >= 0) & (key_row < rows)
    ids = jnp.where(real, (key_frame * rows + key_row) * TW + column, -5).astype(F32)
    lane_tile = lax.broadcasted_iota(jnp.int32, (BLOCKS * 8, SLAB), 1) // TILE
    lane = lax.broadcasted_iota(jnp.int32, (8, 128), 1)
    for slot in (OUTER, INNER):
        found = jnp.full((BLOCKS * 8, SLAB), HIDDEN, F32)
        for tile in range(TW):
            hit = jnp.max(
                jnp.where(lists[0, slot, tile : tile + 1, :] == ids, 0.0, HIDDEN),
                axis=1, keepdims=True,
            )
            found = jnp.where(lane_tile == tile, hit, found)
        bias[slot] = found.reshape(BLOCKS, 8, SLAB)
        turned = jnp.concatenate(
            [
                jnp.concatenate(
                    [found[:, tile * TILE : tile * TILE + 1] for tile in range(TW)]
                    + [jnp.full((BLOCKS * 8, 124), HIDDEN, F32)],
                    axis=1,
                ),
                jnp.full((56, 128), HIDDEN, F32),
            ],
            axis=0,
        ).T[:8]
        for key_block in range(BLOCKS):
            for side in range(2):
                at = key_block * 8 + side * 2
                bias_rows[slot, key_block // 3, side, :, pl.ds(key_block % 3 * 128, 128)] = jnp.where(
                    lane < TILE, turned[:, at : at + 1], turned[:, at + 1 : at + 2]
                )

    wait_heads(QD, INNER)
    y_copy(QD).start()
    spread(QD, INNER)
    wait_heads(QD, OUTER)
    spread(QD, OUTER)

    def return_heads(kind, slot):
        for to_x in x_at:
            for far_hi in range(2):
                to_y = frame_of[slot] + far_hi * FT
                token_chunk = to_x * 2 + far_hi
                part = pl.ds(pl.multiple_of(token_chunk * chunk, chunk), chunk)
                pltpu.make_async_remote_copy(
                    src_ref=results.at[kind, slot, :, part, :],
                    dst_ref=landed.at[kind, my_head],
                    send_sem=out_send.at[kind],
                    recv_sem=out_recv.at[kind],
                    device_id=device(to_y, r, to_x),
                    device_id_type=MESH,
                ).start()

    def my_scale(scale):
        return scale[:, pl.ds(pl.multiple_of(my_head * HD, HD), HD)]

    def stat_copies(slot):
        return {
            side: pltpu.make_async_remote_copy(
                src_ref=stats_sent.at[slot, side, 0:2],
                dst_ref=stats.at[slot, 2 - side],
                send_sem=stat_send.at[slot, side // 2],
                recv_sem=stat_recv.at[slot, side // 2],
                device_id=device(y, r_at[side], x),
                device_id_type=MESH,
            )
            for side in (0, 2)
        }

    def far_stat_copies():
        return {
            side: pltpu.make_async_remote_copy(
                src_ref=stats_sent.at[INNER, side, BEYOND],
                dst_ref=stats.at[BEYOND, 2 - side, INNER],
                send_sem=far_send.at[side],
                recv_sem=far_recv.at[side],
                device_id=device(y_partner, r_at[side], x),
                device_id_type=MESH,
            )
            for side in range(3)
        }

    def rows_of(kind, slot, which, side):
        return jnp.concatenate(
            [data[kind, slot, row, which, own(side), :] for row in range(3)], axis=0
        )

    def query_side(slot, arrive, between):
        key_slots = (INNER, OUTER) if slot == OUTER else (INNER, OUTER, BEYOND)
        parts = [(key_slot, side) for key_slot in key_slots for side in range(2)]
        peak = [jnp.full((3 * TILE, 128), -3e38, F32) for side in range(2)]
        for key_slot, side in parts:
            if side == 0:
                arrive(key_slot)
            part = add_rows(
                dot_nt(data[QD, slot, 1, 0, near(side), :], rows_of(KV, key_slot, 0, side)),
                bias_rows[slot, key_slot, side, side : side + 3, :],
            )
            scores[key_slot, side] = part
            peak[side] = jnp.maximum(peak[side], fold(part, jnp.maximum))
        row_max = jnp.max(join(*peak, jnp.maximum), axis=1, keepdims=True)
        between()

        row_wide = jnp.broadcast_to(row_max, (SLAB, 128))
        totals = [jnp.zeros((3 * TILE, 128), F32) for side in range(2)]
        sums = [jnp.zeros((3 * TILE, HD), F32) for side in range(2)]
        for key_slot, side in parts:
            part = jnp.exp(scores[key_slot, side] - wide(row_wide[near(side)]))
            low = part.astype(BF16)
            weights[key_slot, side] = low
            totals[side] = totals[side] + fold(part, jnp.add)
            sums[side] = sums[side] + dot_nn(low, rows_of(KV, key_slot, 1, side))
        total = jnp.sum(join(*totals, jnp.add), axis=1, keepdims=True)
        inverse = jnp.broadcast_to(1.0 / total, (SLAB, 128))
        attended = (join(*sums, jnp.add) * inverse).astype(BF16)
        results[0, slot, 0] = attended
        grads = data[QD, slot, 1, 1].astype(F32)
        delta = jnp.sum(attended.astype(F32) * grads, axis=1, keepdims=True)
        log_total = row_max + jnp.log(total)
        lane = lax.broadcasted_iota(jnp.int32, (SLAB, 128), 1)
        turned = jnp.where(lane == 0, log_total, delta).T
        log_row, delta_row = turned[0:1], turned[1:2]
        line8 = lax.broadcasted_iota(jnp.int32, (8, SLAB), 0)
        for key_slot in key_slots:
            for row in range(3):
                message = jnp.where(
                    line8 == TW, delta_row, bias[slot, key_slot * 3 + row] - log_row
                )
                if row == 1 and key_slot != BEYOND:
                    stats[slot, 1, key_slot] = message
                else:
                    stats_sent[slot, row, key_slot] = message
        start_rows(stat_copies(slot))
        if slot == INNER:
            start_rows(far_stat_copies())
        delta_part = delta * inverse

        sums = [jnp.zeros((3 * TILE, HD), F32) for side in range(2)]
        for key_slot, side in parts:
            grad_weights = dot_nt(
                data[QD, slot, 1, 1, near(side), :], rows_of(KV, key_slot, 1, side)
            )
            part = weights[key_slot, side].astype(F32) * (
                grad_weights * wide(inverse[near(side)]) - wide(delta_part[near(side)])
            )
            sums[side] = sums[side] + dot_nn(part.astype(BF16), rows_of(KV, key_slot, 0, side))
        scale = my_scale(query_scale) * HD ** (-0.5)
        results[0, slot, 1] = (join(*sums, jnp.add) * scale).astype(BF16)
        return_heads(0, slot)

    def key_side(slot, arrive):
        query_slots = (OUTER, INNER) if slot == OUTER else (OUTER, INNER, BEYOND)
        key_sums = [jnp.zeros((3 * TILE, HD), F32) for side in range(2)]
        value_sums = [jnp.zeros((3 * TILE, HD), F32) for side in range(2)]
        for query_slot in query_slots:
            arrive(query_slot)
            for side in range(2):
                message = jnp.concatenate(
                    [stats[query_slot, row, slot, :, own(side)] for row in range(3)], axis=1
                )
                queries = rows_of(QD, query_slot, 0, side)
                grads = rows_of(QD, query_slot, 1, side)
                part = jnp.exp(add_rows(
                    dot_nt(data[KV, slot, 1, 0, near(side), :], queries),
                    message[side : side + 3],
                ))
                grad_weights = dot_nt(data[KV, slot, 1, 1, near(side), :], grads)
                slopes = (part * (grad_weights - message[TW : TW + 1])).astype(BF16)
                value_sums[side] = value_sums[side] + dot_nn(part.astype(BF16), grads)
                key_sums[side] = key_sums[side] + dot_nn(slopes, queries)
        grad_keys = join(*key_sums, jnp.add)
        results[1, slot, 0] = (grad_keys * my_scale(key_scale)).astype(BF16)
        results[1, slot, 1] = join(*value_sums, jnp.add).astype(BF16)
        return_heads(1, slot)

    def beyond_arrives(key_slot):
        if key_slot == BEYOND:
            wait_rows(KV, BEYOND)

    def pair_arrives(query_slot):
        wait_rows(QD, query_slot)
        came_rows(stat_copies(query_slot))

    def beyond_queries_arrive(query_slot):
        if query_slot == BEYOND:
            wait_rows(QD, BEYOND)
            came_rows(far_stat_copies())

    query_side(OUTER, lambda key_slot: wait_rows(KV, key_slot), lambda: forward(KV))
    query_side(INNER, beyond_arrives, lambda: forward(QD))
    key_side(OUTER, pair_arrives)
    key_side(INNER, beyond_queries_arrive)

    for kind in range(2):
        pltpu.make_async_copy(landed.at[kind], landed.at[kind], out_recv.at[kind]).wait()
    sent = lists.at[0:2]
    pltpu.make_async_copy(sent, sent, list_send).wait()
    for kind in range(2):
        sent = stage.at[kind]
        pltpu.make_async_copy(sent, sent, a2a_send.at[kind]).wait()
        for slot in range(3):
            sent_rows(r_copies(kind, slot))
        y_copy(kind).wait_send()
        sent = results.at[kind]
        pltpu.make_async_copy(sent, sent, out_send.at[kind]).wait()
    for slot in (OUTER, INNER):
        sent_rows(stat_copies(slot))
    sent_rows(far_stat_copies())


def hand_out(landed, attention, grad_query, grad_key, grad_value, pieces, held, sems):
    targets = (attention, grad_query, grad_key, grad_value)
    loads = [
        pltpu.make_async_copy(landed.at[kind], pieces.at[kind], sems.at[0, kind])
        for kind in range(2)
    ]
    stores = [pltpu.make_async_copy(held.at[i], targets[i], sems.at[1, i]) for i in range(4)]
    for load in loads:
        load.start()
    for i in range(4):
        if i % 2 == 0:
            loads[i // 2].wait()
        for head in range(landed.shape[1]):
            held[i, :, head * HD : (head + 1) * HD] = pieces[i // 2, head, i % 2]
        stores[i].start()
    for store in stores:
        store.wait()


def local(query, key, value, grad_out, query_scale, key_scale, neighbours):
    rows = lax.axis_size("slab") // FT
    columns = lax.axis_size("head") // 2
    chunk, width = query.shape
    out = jax.ShapeDtypeStruct((chunk, width), BF16)
    landing = (2, width // HD, 2, chunk, HD)
    hbm = pl.BlockSpec(memory_space=pltpu.HBM)
    dma = pltpu.SemaphoreType.DMA
    landed = pl.pallas_call(
        functools.partial(kernel, rows, columns),
        out_shape=jax.ShapeDtypeStruct(landing, BF16),
        in_specs=[hbm] * 7,
        out_specs=hbm,
        scratch_shapes=[
            pltpu.VMEM((4, chunk, width), BF16),
            pltpu.VMEM((1, width), F32),
            pltpu.VMEM((1, width), F32),
            pltpu.VMEM(neighbours.shape, jnp.int32),
            pltpu.VMEM((2, 4 * columns, 2, chunk, HD), BF16),
            pltpu.VMEM((2, 3, 3, 2, SLAB, HD), BF16),
            pltpu.VMEM((8, 128), F32),
            pltpu.VMEM((2, 2, 8, 128), F32),
            pltpu.VMEM((2, BLOCKS, 8, SLAB), F32),
            pltpu.VMEM((2, 3, 2, 8, 3 * 128), F32),
            pltpu.VMEM((3, 2, 3 * TILE, 3 * 128), F32),
            pltpu.VMEM((3, 2, 3 * TILE, 3 * 128), BF16),
            pltpu.VMEM((3, 3, 2, 8, SLAB), F32),
            pltpu.VMEM((2, 3, 3, 8, SLAB), F32),
            pltpu.VMEM((2, 2, 2, SLAB, HD), BF16),
            dma((7,)),
            dma((2,)),
            dma((2, 2)),
            dma,
            dma,
            dma((2, 7)),
            dma((2,)),
            dma((2, 3, 2)),
            dma((2, 2)),
            dma((2, 2)),
            dma((3,)),
            dma((3,)),
            dma((2,)),
            dma((2,)),
        ],
        compiler_params=pltpu.CompilerParams(
            collective_id=0, has_side_effects=True, vmem_limit_bytes=VMEM_BYTES
        ),
        name="tiles",
    )(
        query, key, value, grad_out,
        query_scale.reshape(1, width), key_scale.reshape(1, width), neighbours,
    )
    return pl.pallas_call(
        hand_out,
        out_shape=(out,) * 4,
        in_specs=[hbm],
        out_specs=(hbm,) * 4,
        scratch_shapes=[
            pltpu.VMEM(landing, BF16), pltpu.VMEM((4, chunk, width), BF16), dma((2, 4)),
        ],
        compiler_params=pltpu.CompilerParams(vmem_limit_bytes=VMEM_BYTES),
        name="hand_out",
    )(landed)


def solution(mesh):
    token = P(("slab", "head"), None)
    return jax.shard_map(
        local,
        mesh=mesh,
        in_specs=(token, token, token, token, P(), P(), P("slab", None)),
        out_specs=(token,) * 4,
        check_vma=False,
    )
```

```python
import functools

import jax
import jax.numpy as jnp
from jax import lax
from jax.experimental import pallas as pl
from jax.experimental.pallas import tpu as pltpu
from jax.sharding import PartitionSpec as P

HD = 128
TILE = 64
FT = 4
TW = 4
SLAB = TILE * TW
RING = 2 * FT
BLOCKS = 9
OUTER, INNER, BEYOND = 0, 1, 2
HIDDEN = -1e30
MESH = pl.DeviceIdType.MESH
BF16 = jnp.bfloat16
F32 = jnp.float32
KV, QD = 0, 1
VMEM_BYTES = 58 * 1024 * 1024


def dot_nn(a, b):
    return lax.dot_general(a, b, (((1,), (0,)), ((), ())), preferred_element_type=F32)


def dot_nt(a, b):
    return lax.dot_general(a, b, (((1,), (1,)), ((), ())), preferred_element_type=F32)


def dot_tn(a, b):
    return lax.dot_general(a, b, (((0,), (0,)), ((), ())), preferred_element_type=F32)


def add_rows(scores, rows):
    shaped = scores.reshape(3, TILE, scores.shape[1]) + rows[:, None, :]
    return shaped.reshape(scores.shape)


def join(low, high, both):
    return jnp.concatenate(
        [low[:TILE], both(low[TILE:], high[: 2 * TILE]), high[2 * TILE :]], axis=0
    )


def fold(array, both):
    return both(both(array[:, :128], array[:, 128:256]), array[:, 256:])


def wide(column):
    return jnp.concatenate([column] * 3, axis=1)


def near(half):
    return slice(half * TILE, half * TILE + 3 * TILE)


def own(half):
    return slice(half * 2 * TILE, (half + 1) * 2 * TILE)


def kernel(
    rows, columns,
    query, key, value, grad_out, query_scale_in, key_scale_in, neighbours_in, landed,
    raw, query_scale, key_scale, neighbours,
    stage, data, listed, lists, bias, bias_rows, scores, weights, stats, stats_sent, results,
    in_sem, a2a_send, a2a_recv, list_send, list_recv, halo_send, y_recv, r_recv,
    stat_send, stat_recv, far_send, far_recv, out_send, out_recv,
):
    loads = [
        pltpu.make_async_copy(source, target, in_sem.at[i])
        for i, (source, target) in enumerate((
            (key, raw.at[0]), (value, raw.at[1]), (query, raw.at[2]), (grad_out, raw.at[3]),
            (key_scale_in, key_scale), (query_scale_in, query_scale),
            (neighbours_in, neighbours),
        ))
    ]
    for load in (loads[4], *loads[:4], *loads[5:]):
        load.start()

    slab = lax.axis_index("slab")
    head = lax.axis_index("head")
    y_lo, r = slab // rows, slab % rows
    x, y_hi = head // 2, head % 2
    y = y_hi * FT + y_lo
    chunk = SLAB // (2 * columns)
    half = 1 - y_lo // 2
    far_y = (1 - y_lo // 2) * 2
    y_far = (far_y, far_y + 1, far_y + FT, far_y + FT + 1)
    frame_of = (3 * half, 1 + half, 2 - half)

    def quarter(at_y):
        return ((at_y + RING - 1) % RING) // 2

    def slot_of(at_y):
        return ((at_y % FT + 1) % FT) // 2

    my_head = x * 4 + quarter(y)
    y_partner = (y + RING - 1 + 2 * (y % 2)) % RING

    def device(to_y, to_r, to_x):
        return {"slab": (to_y % FT) * rows + to_r, "head": to_x * 2 + to_y // FT}

    r_at = ((r + rows - 1) % rows, r, (r + 1) % rows)
    x_at = tuple((x + step) % columns for step in range(columns))

    def at_side(side):
        return pl.when(r < rows - 1) if side == 2 else pl.when(r >= 1 - side)

    barrier = pltpu.get_barrier_semaphore()

    def greet(peers):
        for peer in peers:
            pl.semaphore_signal(barrier, 1, device_id=peer, device_id_type=MESH)

    greet([device(to_y, r, to_x) for to_y in y_far for to_x in x_at])
    greet([device(y_partner, r, x)])
    for side in (0, 2):
        @at_side(side)
        def _():
            greet([device(y, r_at[side], x), device(y_partner, r_at[side], x)])

    listed[...] = jnp.full(listed.shape, -2.0, F32)

    def put(kind, which, array):
        for piece in range(4 * columns):
            stage[kind, piece, which] = array[:, piece * HD : (piece + 1) * HD]

    loads[4].wait()
    loads[0].wait()
    put(KV, 0, (raw[0].astype(F32) * key_scale[...]).astype(BF16))
    loads[1].wait()
    put(KV, 1, raw[1])
    row_sides = (r + rows - 1) // rows + (2 * rows - 2 - r) // rows
    pl.semaphore_wait(barrier, 4 * columns + 1 + 2 * row_sides)

    my_rows = pl.ds(pl.multiple_of(head * chunk, chunk), chunk)

    def send_heads(kind, places):
        for to_x in x_at:
            for to_y in places:
                pltpu.make_async_remote_copy(
                    src_ref=stage.at[kind, to_x * 4 + quarter(to_y)],
                    dst_ref=data.at[kind, slot_of(y), 1, :, my_rows, :],
                    send_sem=a2a_send.at[kind],
                    recv_sem=a2a_recv.at[kind, slot_of(y)],
                    device_id=device(to_y, r, to_x),
                    device_id_type=MESH,
                ).start()

    def wait_heads(kind, slot):
        whole = data.at[kind, slot, 1]
        pltpu.make_async_copy(whole, whole, a2a_recv.at[kind, slot]).wait()

    def y_copy(kind):
        return pltpu.make_async_remote_copy(
            src_ref=data.at[kind, INNER, 1],
            dst_ref=data.at[kind, BEYOND, 1],
            send_sem=halo_send.at[kind, 6],
            recv_sem=y_recv.at[kind],
            device_id=device(y_partner, r, x),
            device_id_type=MESH,
        )

    def start_rows(copies):
        for side, copy in copies.items():
            at_side(side)(copy.start)

    def sent_rows(copies):
        for side, copy in copies.items():
            at_side(side)(copy.wait_send)

    def came_rows(copies):
        for side, copy in copies.items():
            at_side(2 - side)(copy.wait_recv)

    def r_copies(kind, slot):
        return {
            side: pltpu.make_async_remote_copy(
                src_ref=data.at[kind, slot, 1],
                dst_ref=data.at[kind, slot, 2 - side],
                send_sem=halo_send.at[kind, slot * 2 + side // 2],
                recv_sem=r_recv.at[kind, slot, side // 2],
                device_id=device(y, r_at[side], x),
                device_id_type=MESH,
            )
            for side in (0, 2)
        }

    def spread(kind, slot):
        start_rows(r_copies(kind, slot))

    def forward(kind):
        y_copy(kind).wait_recv()
        spread(kind, BEYOND)

    def wait_rows(kind, slot):
        came_rows(r_copies(kind, slot))

    send_heads(KV, y_far)
    loads[6].wait()
    listed[0:TW, 0:27] = neighbours[...].astype(F32)
    for to_y in y_far:
        pltpu.make_async_remote_copy(
            src_ref=listed, dst_ref=lists.at[y_hi, slot_of(y)],
            send_sem=list_send, recv_sem=list_recv,
            device_id=device(to_y, r, x), device_id_type=MESH,
        ).start()

    loads[5].wait()
    factor = query_scale[...] * HD ** (-0.5)
    loads[2].wait()
    put(QD, 0, (raw[2].astype(F32) * factor).astype(BF16))
    loads[3].wait()
    put(QD, 1, raw[3])

    send_heads(QD, y_far)

    for side in (0, 2):
        @pl.when(r == (rows - 1 if side == 2 else 0))
        def _():
            data[:, :, side] = jnp.zeros((2, 3, 2, SLAB, HD), BF16)
            stats[:, side] = jnp.full((3, 2, 8, SLAB), HIDDEN, F32)

    wait_heads(KV, INNER)
    y_copy(KV).start()
    spread(KV, INNER)
    wait_heads(KV, OUTER)
    spread(KV, OUTER)

    pltpu.make_async_copy(lists, lists, list_recv).wait()
    shape = (BLOCKS * 8, 128)
    line = lax.broadcasted_iota(jnp.int32, shape, 0)
    column = line % 8
    block_of = line // 8
    key_slot = block_of // 3
    key_frame = jnp.where(
        key_slot == 0, frame_of[0], jnp.where(key_slot == 1, frame_of[1], frame_of[2])
    )
    key_row = r + block_of % 3 - 1
    real = (column < TW) & (key_row >= 0) & (key_row < rows)
    ids = jnp.where(real, (key_frame * rows + key_row) * TW + column, -5).astype(F32)
    lane_tile = lax.broadcasted_iota(jnp.int32, (BLOCKS * 8, SLAB), 1) // TILE
    lane = lax.broadcasted_iota(jnp.int32, (8, 128), 1)
    for slot in (OUTER, INNER):
        found = jnp.full((BLOCKS * 8, SLAB), HIDDEN, F32)
        for tile in range(TW):
            hit = jnp.max(
                jnp.where(lists[0, slot, tile : tile + 1, :] == ids, 0.0, HIDDEN),
                axis=1, keepdims=True,
            )
            found = jnp.where(lane_tile == tile, hit, found)
        bias[slot] = found.reshape(BLOCKS, 8, SLAB)
        turned = jnp.concatenate(
            [
                jnp.concatenate(
                    [found[:, tile * TILE : tile * TILE + 1] for tile in range(TW)]
                    + [jnp.full((BLOCKS * 8, 124), HIDDEN, F32)],
                    axis=1,
                ),
                jnp.full((56, 128), HIDDEN, F32),
            ],
            axis=0,
        ).T[:8]
        for key_block in range(BLOCKS):
            for side in range(2):
                at = key_block * 8 + side * 2
                bias_rows[slot, key_block // 3, side, :, pl.ds(key_block % 3 * 128, 128)] = jnp.where(
                    lane < TILE, turned[:, at : at + 1], turned[:, at + 1 : at + 2]
                )

    wait_heads(QD, INNER)
    y_copy(QD).start()
    spread(QD, INNER)
    wait_heads(QD, OUTER)

    def return_heads(kind, slot):
        for to_x in x_at:
            for far_hi in range(2):
                to_y = frame_of[slot] + far_hi * FT
                token_chunk = to_x * 2 + far_hi
                part = pl.ds(pl.multiple_of(token_chunk * chunk, chunk), chunk)
                pltpu.make_async_remote_copy(
                    src_ref=results.at[kind, slot, :, part, :],
                    dst_ref=landed.at[kind, my_head],
                    send_sem=out_send.at[kind],
                    recv_sem=out_recv.at[kind],
                    device_id=device(to_y, r, to_x),
                    device_id_type=MESH,
                ).start()

    def my_scale(scale):
        return scale[:, pl.ds(pl.multiple_of(my_head * HD, HD), HD)]

    def stat_copies(slot):
        return {
            side: pltpu.make_async_remote_copy(
                src_ref=stats_sent.at[slot, side, 0:2],
                dst_ref=stats.at[slot, 2 - side],
                send_sem=stat_send.at[slot, side // 2],
                recv_sem=stat_recv.at[slot, side // 2],
                device_id=device(y, r_at[side], x),
                device_id_type=MESH,
            )
            for side in (0, 2)
        }

    def far_stat_copies():
        return {
            side: pltpu.make_async_remote_copy(
                src_ref=stats_sent.at[INNER, side, BEYOND],
                dst_ref=stats.at[BEYOND, 2 - side, INNER],
                send_sem=far_send.at[side],
                recv_sem=far_recv.at[side],
                device_id=device(y_partner, r_at[side], x),
                device_id_type=MESH,
            )
            for side in range(3)
        }

    def rows_of(kind, slot, which, side):
        return jnp.concatenate(
            [data[kind, slot, row, which, own(side), :] for row in range(3)], axis=0
        )

    def query_side(slot, arrive, between):
        key_slots = (INNER, OUTER) if slot == OUTER else (INNER, OUTER, BEYOND)
        parts = [(key_slot, side) for key_slot in key_slots for side in range(2)]
        peak = [jnp.full((3 * TILE, 128), -3e38, F32) for side in range(2)]
        for key_slot, side in parts:
            if side == 0:
                arrive(key_slot)
            part = add_rows(
                dot_nt(data[QD, slot, 1, 0, near(side), :], rows_of(KV, key_slot, 0, side)),
                bias_rows[slot, key_slot, side, side : side + 3, :],
            )
            scores[key_slot, side] = part
            peak[side] = jnp.maximum(peak[side], fold(part, jnp.maximum))
        row_max = jnp.max(join(*peak, jnp.maximum), axis=1, keepdims=True)
        between()

        row_wide = jnp.broadcast_to(row_max, (SLAB, 128))
        totals = [jnp.zeros((3 * TILE, 128), F32) for side in range(2)]
        sums = [jnp.zeros((3 * TILE, HD), F32) for side in range(2)]
        for key_slot, side in parts:
            part = jnp.exp(scores[key_slot, side] - wide(row_wide[near(side)]))
            low = part.astype(BF16)
            weights[key_slot, side] = low
            totals[side] = totals[side] + fold(part, jnp.add)
            sums[side] = sums[side] + dot_nn(low, rows_of(KV, key_slot, 1, side))
        total = jnp.sum(join(*totals, jnp.add), axis=1, keepdims=True)
        inverse = jnp.broadcast_to(1.0 / total, (SLAB, 128))
        attended = (join(*sums, jnp.add) * inverse).astype(BF16)
        results[0, slot, 0] = attended
        grads = data[QD, slot, 1, 1].astype(F32)
        delta = jnp.sum(attended.astype(F32) * grads, axis=1, keepdims=True)
        log_total = row_max + jnp.log(total)
        lane = lax.broadcasted_iota(jnp.int32, (SLAB, 128), 1)
        turned = jnp.where(lane == 0, log_total, delta).T
        log_row, delta_row = turned[0:1], turned[1:2]
        line8 = lax.broadcasted_iota(jnp.int32, (8, SLAB), 0)
        for key_slot in key_slots:
            for row in range(3):
                message = jnp.where(
                    line8 == TW, delta_row, bias[slot, key_slot * 3 + row] - log_row
                )
                if row == 1 and key_slot != BEYOND:
                    stats[slot, 1, key_slot] = message
                else:
                    stats_sent[slot, row, key_slot] = message
        start_rows(stat_copies(slot))
        if slot == INNER:
            start_rows(far_stat_copies())
        delta_part = delta * inverse

        sums = [jnp.zeros((3 * TILE, HD), F32) for side in range(2)]
        for key_slot, side in parts:
            grad_weights = dot_nt(
                data[QD, slot, 1, 1, near(side), :], rows_of(KV, key_slot, 1, side)
            )
            part = weights[key_slot, side].astype(F32) * (
                grad_weights * wide(inverse[near(side)]) - wide(delta_part[near(side)])
            )
            sums[side] = sums[side] + dot_nn(part.astype(BF16), rows_of(KV, key_slot, 0, side))
        scale = my_scale(query_scale) * HD ** (-0.5)
        results[0, slot, 1] = (join(*sums, jnp.add) * scale).astype(BF16)
        return_heads(0, slot)

    def key_side(slot, arrive):
        query_slots = (OUTER, INNER) if slot == OUTER else (OUTER, INNER, BEYOND)
        key_sums = [jnp.zeros((3 * TILE, HD), F32) for side in range(2)]
        value_sums = [jnp.zeros((3 * TILE, HD), F32) for side in range(2)]
        for query_slot in query_slots:
            arrive(query_slot)
            for side in range(2):
                message = jnp.concatenate(
                    [stats[query_slot, row, slot, :, own(side)] for row in range(3)], axis=1
                )
                queries = rows_of(QD, query_slot, 0, side)
                grads = rows_of(QD, query_slot, 1, side)
                part = jnp.exp(add_rows(
                    dot_nt(data[KV, slot, 1, 0, near(side), :], queries),
                    message[side : side + 3],
                ))
                grad_weights = dot_nt(data[KV, slot, 1, 1, near(side), :], grads)
                slopes = (part * (grad_weights - message[TW : TW + 1])).astype(BF16)
                value_sums[side] = value_sums[side] + dot_nn(part.astype(BF16), grads)
                key_sums[side] = key_sums[side] + dot_nn(slopes, queries)
        grad_keys = join(*key_sums, jnp.add)
        results[1, slot, 0] = (grad_keys * my_scale(key_scale)).astype(BF16)
        results[1, slot, 1] = join(*value_sums, jnp.add).astype(BF16)
        return_heads(1, slot)

    def beyond_arrives(key_slot):
        if key_slot == BEYOND:
            wait_rows(KV, BEYOND)

    def pair_arrives(query_slot):
        wait_rows(QD, query_slot)
        came_rows(stat_copies(query_slot))

    def beyond_queries_arrive(query_slot):
        if query_slot == BEYOND:
            wait_rows(QD, BEYOND)
            came_rows(far_stat_copies())

    def forward_first():
        forward(KV)
        spread(QD, OUTER)

    query_side(OUTER, lambda key_slot: wait_rows(KV, key_slot), forward_first)
    query_side(INNER, beyond_arrives, lambda: forward(QD))
    key_side(OUTER, pair_arrives)
    key_side(INNER, beyond_queries_arrive)

    for kind in range(2):
        pltpu.make_async_copy(landed.at[kind], landed.at[kind], out_recv.at[kind]).wait()
    sent = lists.at[0:2]
    pltpu.make_async_copy(sent, sent, list_send).wait()
    for kind in range(2):
        sent = stage.at[kind]
        pltpu.make_async_copy(sent, sent, a2a_send.at[kind]).wait()
        for slot in range(3):
            sent_rows(r_copies(kind, slot))
        y_copy(kind).wait_send()
        sent = results.at[kind]
        pltpu.make_async_copy(sent, sent, out_send.at[kind]).wait()
    for slot in (OUTER, INNER):
        sent_rows(stat_copies(slot))
    sent_rows(far_stat_copies())


def hand_out(landed, attention, grad_query, grad_key, grad_value, pieces, held, sems):
    targets = (attention, grad_query, grad_key, grad_value)
    loads = [
        pltpu.make_async_copy(landed.at[kind], pieces.at[kind], sems.at[0, kind])
        for kind in range(2)
    ]
    stores = [pltpu.make_async_copy(held.at[i], targets[i], sems.at[1, i]) for i in range(4)]
    for load in loads:
        load.start()
    for i in range(4):
        if i % 2 == 0:
            loads[i // 2].wait()
        for head in range(landed.shape[1]):
            held[i, :, head * HD : (head + 1) * HD] = pieces[i // 2, head, i % 2]
        stores[i].start()
    for store in stores:
        store.wait()


def local(query, key, value, grad_out, query_scale, key_scale, neighbours):
    rows = lax.axis_size("slab") // FT
    columns = lax.axis_size("head") // 2
    chunk, width = query.shape
    out = jax.ShapeDtypeStruct((chunk, width), BF16)
    landing = (2, width // HD, 2, chunk, HD)
    hbm = pl.BlockSpec(memory_space=pltpu.HBM)
    dma = pltpu.SemaphoreType.DMA
    landed = pl.pallas_call(
        functools.partial(kernel, rows, columns),
        out_shape=jax.ShapeDtypeStruct(landing, BF16),
        in_specs=[hbm] * 7,
        out_specs=hbm,
        scratch_shapes=[
            pltpu.VMEM((4, chunk, width), BF16),
            pltpu.VMEM((1, width), F32),
            pltpu.VMEM((1, width), F32),
            pltpu.VMEM(neighbours.shape, jnp.int32),
            pltpu.VMEM((2, 4 * columns, 2, chunk, HD), BF16),
            pltpu.VMEM((2, 3, 3, 2, SLAB, HD), BF16),
            pltpu.VMEM((8, 128), F32),
            pltpu.VMEM((2, 2, 8, 128), F32),
            pltpu.VMEM((2, BLOCKS, 8, SLAB), F32),
            pltpu.VMEM((2, 3, 2, 8, 3 * 128), F32),
            pltpu.VMEM((3, 2, 3 * TILE, 3 * 128), F32),
            pltpu.VMEM((3, 2, 3 * TILE, 3 * 128), BF16),
            pltpu.VMEM((3, 3, 2, 8, SLAB), F32),
            pltpu.VMEM((2, 3, 3, 8, SLAB), F32),
            pltpu.VMEM((2, 2, 2, SLAB, HD), BF16),
            dma((7,)),
            dma((2,)),
            dma((2, 2)),
            dma,
            dma,
            dma((2, 7)),
            dma((2,)),
            dma((2, 3, 2)),
            dma((2, 2)),
            dma((2, 2)),
            dma((3,)),
            dma((3,)),
            dma((2,)),
            dma((2,)),
        ],
        compiler_params=pltpu.CompilerParams(
            collective_id=0, has_side_effects=True, vmem_limit_bytes=VMEM_BYTES
        ),
        name="tiles",
    )(
        query, key, value, grad_out,
        query_scale.reshape(1, width), key_scale.reshape(1, width), neighbours,
    )
    return pl.pallas_call(
        hand_out,
        out_shape=(out,) * 4,
        in_specs=[hbm],
        out_specs=(hbm,) * 4,
        scratch_shapes=[
            pltpu.VMEM(landing, BF16), pltpu.VMEM((4, chunk, width), BF16), dma((2, 4)),
        ],
        compiler_params=pltpu.CompilerParams(vmem_limit_bytes=VMEM_BYTES),
        name="hand_out",
    )(landed)


def solution(mesh):
    token = P(("slab", "head"), None)
    return jax.shard_map(
        local,
        mesh=mesh,
        in_specs=(token, token, token, token, P(), P(), P("slab", None)),
        out_specs=(token,) * 4,
        check_vma=False,
    )
```

```python
import functools

import jax
import jax.numpy as jnp
from jax import lax
from jax.experimental import pallas as pl
from jax.experimental.pallas import tpu as pltpu
from jax.sharding import PartitionSpec as P

HD = 128
TILE = 64
FT = 4
TW = 4
SLAB = TILE * TW
RING = 2 * FT
BLOCKS = 9
OUTER, INNER, BEYOND = 0, 1, 2
HIDDEN = -1e30
MESH = pl.DeviceIdType.MESH
BF16 = jnp.bfloat16
F32 = jnp.float32
KEY, VALUE, QUERY, GRAD = range(4)
KV, Q, G = range(3)
ARRAYS = (pl.ds(0, 2), pl.ds(2, 1), pl.ds(3, 1))
VMEM_BYTES = 58 * 1024 * 1024


def dot_nn(a, b):
    return lax.dot_general(a, b, (((1,), (0,)), ((), ())), preferred_element_type=F32)


def dot_nt(a, b):
    return lax.dot_general(a, b, (((1,), (1,)), ((), ())), preferred_element_type=F32)


def dot_tn(a, b):
    return lax.dot_general(a, b, (((0,), (0,)), ((), ())), preferred_element_type=F32)


def add_rows(scores, rows):
    shaped = scores.reshape(3, TILE, scores.shape[1]) + rows[:, None, :]
    return shaped.reshape(scores.shape)


def join(low, high, both):
    return jnp.concatenate(
        [low[:TILE], both(low[TILE:], high[: 2 * TILE]), high[2 * TILE :]], axis=0
    )


def fold(array, both):
    return both(both(array[:, :128], array[:, 128:256]), array[:, 256:])


def wide(column):
    return jnp.concatenate([column] * 3, axis=1)


def near(half):
    return slice(half * TILE, half * TILE + 3 * TILE)


def own(half):
    return slice(half * 2 * TILE, (half + 1) * 2 * TILE)


def kernel(
    rows, columns,
    query, key, value, grad_out, query_scale_in, key_scale_in, neighbours_in, landed,
    raw, query_scale, key_scale, neighbours,
    stage, data, listed, lists, bias, bias_rows, scores, weights, inverses, log_totals,
    stats, stats_sent, results,
    in_sem, a2a_send, a2a_recv, list_send, list_recv, halo_send, y_recv, r_recv,
    stat_send, stat_recv, far_send, far_recv, out_send, out_recv,
):
    loads = [
        pltpu.make_async_copy(source, target, in_sem.at[i])
        for i, (source, target) in enumerate((
            (key, raw.at[0]), (value, raw.at[1]), (query, raw.at[2]), (grad_out, raw.at[3]),
            (key_scale_in, key_scale), (query_scale_in, query_scale),
            (neighbours_in, neighbours),
        ))
    ]
    for load in (loads[4], *loads[:4], *loads[5:]):
        load.start()

    slab = lax.axis_index("slab")
    head = lax.axis_index("head")
    y_lo, r = slab // rows, slab % rows
    x, y_hi = head // 2, head % 2
    y = y_hi * FT + y_lo
    chunk = SLAB // (2 * columns)
    half = 1 - y_lo // 2
    far_y = (1 - y_lo // 2) * 2
    y_far = (far_y, far_y + 1, far_y + FT, far_y + FT + 1)
    frame_of = (3 * half, 1 + half, 2 - half)

    def quarter(at_y):
        return ((at_y + RING - 1) % RING) // 2

    def slot_of(at_y):
        return ((at_y % FT + 1) % FT) // 2

    my_head = x * 4 + quarter(y)
    y_partner = (y + RING - 1 + 2 * (y % 2)) % RING

    def device(to_y, to_r, to_x):
        return {"slab": (to_y % FT) * rows + to_r, "head": to_x * 2 + to_y // FT}

    r_at = ((r + rows - 1) % rows, r, (r + 1) % rows)
    x_at = tuple((x + step) % columns for step in range(columns))

    def at_side(side):
        return pl.when(r < rows - 1) if side == 2 else pl.when(r >= 1 - side)

    barrier = pltpu.get_barrier_semaphore()

    def greet(peers):
        for peer in peers:
            pl.semaphore_signal(barrier, 1, device_id=peer, device_id_type=MESH)

    greet([device(to_y, r, to_x) for to_y in y_far for to_x in x_at])
    greet([device(y_partner, r, x)])
    for side in (0, 2):
        @at_side(side)
        def _():
            greet([device(y, r_at[side], x), device(y_partner, r_at[side], x)])

    listed[...] = jnp.full(listed.shape, -2.0, F32)

    def put(which, array):
        for piece in range(4 * columns):
            stage[which, piece] = array[:, piece * HD : (piece + 1) * HD]

    loads[4].wait()
    loads[0].wait()
    put(KEY, (raw[0].astype(F32) * key_scale[...]).astype(BF16))
    loads[1].wait()
    put(VALUE, raw[1])
    row_sides = (r + rows - 1) // rows + (2 * rows - 2 - r) // rows
    pl.semaphore_wait(barrier, 4 * columns + 1 + 2 * row_sides)

    my_rows = pl.ds(pl.multiple_of(head * chunk, chunk), chunk)

    def send_heads(kind, places):
        for to_x in x_at:
            for to_y in places:
                pltpu.make_async_remote_copy(
                    src_ref=stage.at[ARRAYS[kind], to_x * 4 + quarter(to_y)],
                    dst_ref=data.at[ARRAYS[kind], slot_of(y), 1, my_rows, :],
                    send_sem=a2a_send.at[kind],
                    recv_sem=a2a_recv.at[kind, slot_of(y)],
                    device_id=device(to_y, r, to_x),
                    device_id_type=MESH,
                ).start()

    def wait_heads(kind, slot):
        whole = data.at[ARRAYS[kind], slot, 1]
        pltpu.make_async_copy(whole, whole, a2a_recv.at[kind, slot]).wait()

    def y_copy(kind):
        return pltpu.make_async_remote_copy(
            src_ref=data.at[ARRAYS[kind], INNER, 1],
            dst_ref=data.at[ARRAYS[kind], BEYOND, 1],
            send_sem=halo_send.at[kind, 6],
            recv_sem=y_recv.at[kind],
            device_id=device(y_partner, r, x),
            device_id_type=MESH,
        )

    def start_rows(copies):
        for side, copy in copies.items():
            at_side(side)(copy.start)

    def sent_rows(copies):
        for side, copy in copies.items():
            at_side(side)(copy.wait_send)

    def came_rows(copies):
        for side, copy in copies.items():
            at_side(2 - side)(copy.wait_recv)

    def r_copies(kind, slot):
        return {
            side: pltpu.make_async_remote_copy(
                src_ref=data.at[ARRAYS[kind], slot, 1],
                dst_ref=data.at[ARRAYS[kind], slot, 2 - side],
                send_sem=halo_send.at[kind, slot * 2 + side // 2],
                recv_sem=r_recv.at[kind, slot, side // 2],
                device_id=device(y, r_at[side], x),
                device_id_type=MESH,
            )
            for side in (0, 2)
        }

    def spread(kind, slot):
        start_rows(r_copies(kind, slot))

    def forward(kind):
        y_copy(kind).wait_recv()
        spread(kind, BEYOND)

    def wait_rows(kind, slot):
        came_rows(r_copies(kind, slot))

    send_heads(KV, y_far)
    loads[6].wait()
    listed[0:TW, 0:27] = neighbours[...].astype(F32)
    for to_y in y_far:
        pltpu.make_async_remote_copy(
            src_ref=listed, dst_ref=lists.at[y_hi, slot_of(y)],
            send_sem=list_send, recv_sem=list_recv,
            device_id=device(to_y, r, x), device_id_type=MESH,
        ).start()

    loads[5].wait()
    factor = query_scale[...] * HD ** (-0.5)
    loads[2].wait()
    put(QUERY, (raw[2].astype(F32) * factor).astype(BF16))
    send_heads(Q, y_far)
    loads[3].wait()
    put(GRAD, raw[3])

    for side in (0, 2):
        @pl.when(r == (rows - 1 if side == 2 else 0))
        def _():
            data[:, :, side] = jnp.zeros((4, 3, SLAB, HD), BF16)
            stats[:, side] = jnp.full((3, 2, 8, SLAB), HIDDEN, F32)

    wait_heads(KV, INNER)
    y_copy(KV).start()
    spread(KV, INNER)
    wait_heads(KV, OUTER)
    spread(KV, OUTER)
    send_heads(G, y_far)

    pltpu.make_async_copy(lists, lists, list_recv).wait()
    shape = (BLOCKS * 8, 128)
    line = lax.broadcasted_iota(jnp.int32, shape, 0)
    column = line % 8
    block_of = line // 8
    key_slot = block_of // 3
    key_frame = jnp.where(
        key_slot == 0, frame_of[0], jnp.where(key_slot == 1, frame_of[1], frame_of[2])
    )
    key_row = r + block_of % 3 - 1
    real = (column < TW) & (key_row >= 0) & (key_row < rows)
    ids = jnp.where(real, (key_frame * rows + key_row) * TW + column, -5).astype(F32)
    lane_tile = lax.broadcasted_iota(jnp.int32, (BLOCKS * 8, SLAB), 1) // TILE
    lane = lax.broadcasted_iota(jnp.int32, (8, 128), 1)
    for slot in (OUTER, INNER):
        found = jnp.full((BLOCKS * 8, SLAB), HIDDEN, F32)
        for tile in range(TW):
            hit = jnp.max(
                jnp.where(lists[0, slot, tile : tile + 1, :] == ids, 0.0, HIDDEN),
                axis=1, keepdims=True,
            )
            found = jnp.where(lane_tile == tile, hit, found)
        bias[slot] = found.reshape(BLOCKS, 8, SLAB)
        turned = jnp.concatenate(
            [
                jnp.concatenate(
                    [found[:, tile * TILE : tile * TILE + 1] for tile in range(TW)]
                    + [jnp.full((BLOCKS * 8, 124), HIDDEN, F32)],
                    axis=1,
                ),
                jnp.full((56, 128), HIDDEN, F32),
            ],
            axis=0,
        ).T[:8]
        for key_block in range(BLOCKS):
            for side in range(2):
                at = key_block * 8 + side * 2
                bias_rows[slot, key_block // 3, side, :, pl.ds(key_block % 3 * 128, 128)] = jnp.where(
                    lane < TILE, turned[:, at : at + 1], turned[:, at + 1 : at + 2]
                )

    wait_heads(Q, INNER)
    y_copy(Q).start()
    spread(Q, INNER)
    wait_heads(Q, OUTER)
    spread(Q, OUTER)

    def return_heads(kind, slot):
        for to_x in x_at:
            for far_hi in range(2):
                to_y = frame_of[slot] + far_hi * FT
                token_chunk = to_x * 2 + far_hi
                part = pl.ds(pl.multiple_of(token_chunk * chunk, chunk), chunk)
                pltpu.make_async_remote_copy(
                    src_ref=results.at[kind, slot, :, part, :],
                    dst_ref=landed.at[kind, my_head],
                    send_sem=out_send.at[kind],
                    recv_sem=out_recv.at[kind],
                    device_id=device(to_y, r, to_x),
                    device_id_type=MESH,
                ).start()

    def my_scale(scale):
        return scale[:, pl.ds(pl.multiple_of(my_head * HD, HD), HD)]

    def stat_copies(slot):
        return {
            side: pltpu.make_async_remote_copy(
                src_ref=stats_sent.at[slot, side, 0:2],
                dst_ref=stats.at[slot, 2 - side],
                send_sem=stat_send.at[slot, side // 2],
                recv_sem=stat_recv.at[slot, side // 2],
                device_id=device(y, r_at[side], x),
                device_id_type=MESH,
            )
            for side in (0, 2)
        }

    def far_stat_copies():
        return {
            side: pltpu.make_async_remote_copy(
                src_ref=stats_sent.at[INNER, side, BEYOND],
                dst_ref=stats.at[BEYOND, 2 - side, INNER],
                send_sem=far_send.at[side],
                recv_sem=far_recv.at[side],
                device_id=device(y_partner, r_at[side], x),
                device_id_type=MESH,
            )
            for side in range(3)
        }

    def rows_of(array, slot, side):
        return jnp.concatenate(
            [data[array, slot, row, own(side), :] for row in range(3)], axis=0
        )

    def parts_of(slot):
        key_slots = (INNER, OUTER) if slot == OUTER else (INNER, OUTER, BEYOND)
        return [(key_slot, side) for key_slot in key_slots for side in range(2)]

    def attend(slot, arrive, between):
        peak = [jnp.full((3 * TILE, 128), -3e38, F32) for side in range(2)]
        for key_slot, side in parts_of(slot):
            if side == 0:
                arrive(key_slot)
            part = add_rows(
                dot_nt(data[QUERY, slot, 1, near(side), :], rows_of(KEY, key_slot, side)),
                bias_rows[slot, key_slot, side, side : side + 3, :],
            )
            scores[key_slot, side] = part
            peak[side] = jnp.maximum(peak[side], fold(part, jnp.maximum))
        row_max = jnp.max(join(*peak, jnp.maximum), axis=1, keepdims=True)
        between()

        row_wide = jnp.broadcast_to(row_max, (SLAB, 128))
        totals = [jnp.zeros((3 * TILE, 128), F32) for side in range(2)]
        sums = [jnp.zeros((3 * TILE, HD), F32) for side in range(2)]
        for key_slot, side in parts_of(slot):
            part = jnp.exp(scores[key_slot, side] - wide(row_wide[near(side)]))
            low = part.astype(BF16)
            weights[slot, key_slot, side] = low
            totals[side] = totals[side] + fold(part, jnp.add)
            sums[side] = sums[side] + dot_nn(low, rows_of(VALUE, key_slot, side))
        total = jnp.sum(join(*totals, jnp.add), axis=1, keepdims=True)
        inverse = jnp.broadcast_to(1.0 / total, (SLAB, 128))
        results[0, slot, 0] = (join(*sums, jnp.add) * inverse).astype(BF16)
        inverses[slot] = inverse
        log_totals[slot] = jnp.broadcast_to(row_max + jnp.log(total), (SLAB, 128))

    def tell(slot):
        grads = data[GRAD, slot, 1].astype(F32)
        delta = jnp.sum(results[0, slot, 0].astype(F32) * grads, axis=1, keepdims=True)
        lane = lax.broadcasted_iota(jnp.int32, (SLAB, 128), 1)
        turned = jnp.where(lane == 0, log_totals[slot], delta).T
        log_row, delta_row = turned[0:1], turned[1:2]
        line8 = lax.broadcasted_iota(jnp.int32, (8, SLAB), 0)
        for key_slot in (OUTER, INNER) if slot == OUTER else (OUTER, INNER, BEYOND):
            for row in range(3):
                message = jnp.where(
                    line8 == TW, delta_row, bias[slot, key_slot * 3 + row] - log_row
                )
                if row == 1 and key_slot != BEYOND:
                    stats[slot, 1, key_slot] = message
                else:
                    stats_sent[slot, row, key_slot] = message
        start_rows(stat_copies(slot))
        if slot == INNER:
            start_rows(far_stat_copies())
        return delta * inverses[slot]

    def query_side(slot, delta_part):
        inverse = inverses[slot]
        sums = [jnp.zeros((3 * TILE, HD), F32) for side in range(2)]
        for key_slot, side in parts_of(slot):
            grad_weights = dot_nt(
                data[GRAD, slot, 1, near(side), :], rows_of(VALUE, key_slot, side)
            )
            part = weights[slot, key_slot, side].astype(F32) * (
                grad_weights * wide(inverse[near(side)]) - wide(delta_part[near(side)])
            )
            sums[side] = sums[side] + dot_nn(part.astype(BF16), rows_of(KEY, key_slot, side))
        scale = my_scale(query_scale) * HD ** (-0.5)
        results[0, slot, 1] = (join(*sums, jnp.add) * scale).astype(BF16)
        return_heads(0, slot)

    def key_side(slot, arrive):
        query_slots = (OUTER, INNER) if slot == OUTER else (OUTER, INNER, BEYOND)
        key_sums = [jnp.zeros((3 * TILE, HD), F32) for side in range(2)]
        value_sums = [jnp.zeros((3 * TILE, HD), F32) for side in range(2)]
        for query_slot in query_slots:
            arrive(query_slot)
            for side in range(2):
                message = jnp.concatenate(
                    [stats[query_slot, row, slot, :, own(side)] for row in range(3)], axis=1
                )
                queries = rows_of(QUERY, query_slot, side)
                grads = rows_of(GRAD, query_slot, side)
                part = jnp.exp(add_rows(
                    dot_nt(data[KEY, slot, 1, near(side), :], queries),
                    message[side : side + 3],
                ))
                grad_weights = dot_nt(data[VALUE, slot, 1, near(side), :], grads)
                slopes = (part * (grad_weights - message[TW : TW + 1])).astype(BF16)
                value_sums[side] = value_sums[side] + dot_nn(part.astype(BF16), grads)
                key_sums[side] = key_sums[side] + dot_nn(slopes, queries)
        grad_keys = join(*key_sums, jnp.add)
        results[1, slot, 0] = (grad_keys * my_scale(key_scale)).astype(BF16)
        results[1, slot, 1] = join(*value_sums, jnp.add).astype(BF16)
        return_heads(1, slot)

    def beyond_arrives(key_slot):
        if key_slot == BEYOND:
            wait_rows(KV, BEYOND)

    def pair_arrives(query_slot):
        wait_rows(Q, query_slot)
        wait_rows(G, query_slot)
        came_rows(stat_copies(query_slot))

    def beyond_queries_arrive(query_slot):
        if query_slot == BEYOND:
            wait_rows(Q, BEYOND)
            wait_rows(G, BEYOND)
            came_rows(far_stat_copies())

    attend(OUTER, lambda key_slot: wait_rows(KV, key_slot), lambda: forward(KV))
    attend(INNER, beyond_arrives, lambda: None)
    wait_heads(G, INNER)
    y_copy(G).start()
    spread(G, INNER)
    wait_heads(G, OUTER)
    spread(G, OUTER)
    outer_delta = tell(OUTER)
    inner_delta = tell(INNER)
    forward(Q)
    query_side(OUTER, outer_delta)
    forward(G)
    query_side(INNER, inner_delta)
    key_side(OUTER, pair_arrives)
    key_side(INNER, beyond_queries_arrive)

    for kind in range(2):
        pltpu.make_async_copy(landed.at[kind], landed.at[kind], out_recv.at[kind]).wait()
    sent = lists.at[0:2]
    pltpu.make_async_copy(sent, sent, list_send).wait()
    for kind in (KV, Q, G):
        sent = stage.at[ARRAYS[kind]]
        pltpu.make_async_copy(sent, sent, a2a_send.at[kind]).wait()
        for slot in range(3):
            sent_rows(r_copies(kind, slot))
        y_copy(kind).wait_send()
    for kind in range(2):
        sent = results.at[kind]
        pltpu.make_async_copy(sent, sent, out_send.at[kind]).wait()
    for slot in (OUTER, INNER):
        sent_rows(stat_copies(slot))
    sent_rows(far_stat_copies())


def hand_out(landed, attention, grad_query, grad_key, grad_value, pieces, held, sems):
    targets = (attention, grad_query, grad_key, grad_value)
    loads = [
        pltpu.make_async_copy(landed.at[kind], pieces.at[kind], sems.at[0, kind])
        for kind in range(2)
    ]
    stores = [pltpu.make_async_copy(held.at[i], targets[i], sems.at[1, i]) for i in range(4)]
    for load in loads:
        load.start()
    for i in range(4):
        if i % 2 == 0:
            loads[i // 2].wait()
        for head in range(landed.shape[1]):
            held[i, :, head * HD : (head + 1) * HD] = pieces[i // 2, head, i % 2]
        stores[i].start()
    for store in stores:
        store.wait()


def local(query, key, value, grad_out, query_scale, key_scale, neighbours):
    rows = lax.axis_size("slab") // FT
    columns = lax.axis_size("head") // 2
    chunk, width = query.shape
    out = jax.ShapeDtypeStruct((chunk, width), BF16)
    landing = (2, width // HD, 2, chunk, HD)
    hbm = pl.BlockSpec(memory_space=pltpu.HBM)
    dma = pltpu.SemaphoreType.DMA
    landed = pl.pallas_call(
        functools.partial(kernel, rows, columns),
        out_shape=jax.ShapeDtypeStruct(landing, BF16),
        in_specs=[hbm] * 7,
        out_specs=hbm,
        scratch_shapes=[
            pltpu.VMEM((4, chunk, width), BF16),
            pltpu.VMEM((1, width), F32),
            pltpu.VMEM((1, width), F32),
            pltpu.VMEM(neighbours.shape, jnp.int32),
            pltpu.VMEM((4, 4 * columns, chunk, HD), BF16),
            pltpu.VMEM((4, 3, 3, SLAB, HD), BF16),
            pltpu.VMEM((8, 128), F32),
            pltpu.VMEM((2, 2, 8, 128), F32),
            pltpu.VMEM((2, BLOCKS, 8, SLAB), F32),
            pltpu.VMEM((2, 3, 2, 8, 3 * 128), F32),
            pltpu.VMEM((3, 2, 3 * TILE, 3 * 128), F32),
            pltpu.VMEM((2, 3, 2, 3 * TILE, 3 * 128), BF16),
            pltpu.VMEM((2, SLAB, 128), F32),
            pltpu.VMEM((2, SLAB, 128), F32),
            pltpu.VMEM((3, 3, 2, 8, SLAB), F32),
            pltpu.VMEM((2, 3, 3, 8, SLAB), F32),
            pltpu.VMEM((2, 2, 2, SLAB, HD), BF16),
            dma((7,)),
            dma((3,)),
            dma((3, 2)),
            dma,
            dma,
            dma((3, 7)),
            dma((3,)),
            dma((3, 3, 2)),
            dma((2, 2)),
            dma((2, 2)),
            dma((3,)),
            dma((3,)),
            dma((2,)),
            dma((2,)),
        ],
        compiler_params=pltpu.CompilerParams(
            collective_id=0, has_side_effects=True, vmem_limit_bytes=VMEM_BYTES
        ),
        name="tiles",
    )(
        query, key, value, grad_out,
        query_scale.reshape(1, width), key_scale.reshape(1, width), neighbours,
    )
    return pl.pallas_call(
        hand_out,
        out_shape=(out,) * 4,
        in_specs=[hbm],
        out_specs=(hbm,) * 4,
        scratch_shapes=[
            pltpu.VMEM(landing, BF16), pltpu.VMEM((4, chunk, width), BF16), dma((2, 4)),
        ],
        compiler_params=pltpu.CompilerParams(vmem_limit_bytes=VMEM_BYTES),
        name="hand_out",
    )(landed)


def solution(mesh):
    token = P(("slab", "head"), None)
    return jax.shard_map(
        local,
        mesh=mesh,
        in_specs=(token, token, token, token, P(), P(), P("slab", None)),
        out_specs=(token,) * 4,
        check_vma=False,
    )
```

```python
import functools

import jax
import jax.numpy as jnp
from jax import lax
from jax.experimental import pallas as pl
from jax.experimental.pallas import tpu as pltpu
from jax.sharding import PartitionSpec as P

HD = 128
TILE = 64
FT = 4
TW = 4
SLAB = TILE * TW
RING = 2 * FT
BLOCKS = 9
OUTER, INNER, BEYOND = 0, 1, 2
HIDDEN = -1e30
MESH = pl.DeviceIdType.MESH
BF16 = jnp.bfloat16
F32 = jnp.float32
KEY, VALUE, QUERY, GRAD = range(4)
KV, Q, G = range(3)
ARRAYS = (pl.ds(0, 2), pl.ds(2, 1), pl.ds(3, 1))
VMEM_BYTES = 58 * 1024 * 1024


def dot_nn(a, b):
    return lax.dot_general(a, b, (((1,), (0,)), ((), ())), preferred_element_type=F32)


def dot_nt(a, b):
    return lax.dot_general(a, b, (((1,), (1,)), ((), ())), preferred_element_type=F32)


def dot_tn(a, b):
    return lax.dot_general(a, b, (((0,), (0,)), ((), ())), preferred_element_type=F32)


def add_rows(scores, rows):
    shaped = scores.reshape(3, TILE, scores.shape[1]) + rows[:, None, :]
    return shaped.reshape(scores.shape)


def join(low, high, both):
    return jnp.concatenate(
        [low[:TILE], both(low[TILE:], high[: 2 * TILE]), high[2 * TILE :]], axis=0
    )


def fold(array, both):
    return both(both(array[:, :128], array[:, 128:256]), array[:, 256:])


def wide(column):
    return jnp.concatenate([column] * 3, axis=1)


def near(half):
    return slice(half * TILE, half * TILE + 3 * TILE)


def own(half):
    return slice(half * 2 * TILE, (half + 1) * 2 * TILE)


def kernel(
    rows, columns,
    query, key, value, grad_out, query_scale_in, key_scale_in, neighbours_in, landed,
    raw, query_scale, key_scale, neighbours,
    stage, data, listed, lists, bias, bias_rows, scores, weights, inverses, log_totals, kept, key_sums,
    stats, stats_sent, results,
    in_sem, a2a_send, a2a_recv, list_send, list_recv, halo_send, y_recv, r_recv,
    stat_send, stat_recv, far_send, far_recv, out_send, out_recv,
):
    loads = [
        pltpu.make_async_copy(source, target, in_sem.at[i])
        for i, (source, target) in enumerate((
            (key, raw.at[0]), (value, raw.at[1]), (query, raw.at[2]), (grad_out, raw.at[3]),
            (key_scale_in, key_scale), (query_scale_in, query_scale),
            (neighbours_in, neighbours),
        ))
    ]
    for load in (loads[4], *loads[:4], *loads[5:]):
        load.start()

    slab = lax.axis_index("slab")
    head = lax.axis_index("head")
    y_lo, r = slab // rows, slab % rows
    x, y_hi = head // 2, head % 2
    y = y_hi * FT + y_lo
    chunk = SLAB // (2 * columns)
    half = 1 - y_lo // 2
    far_y = (1 - y_lo // 2) * 2
    y_far = (far_y, far_y + 1, far_y + FT, far_y + FT + 1)
    frame_of = (3 * half, 1 + half, 2 - half)

    def quarter(at_y):
        return ((at_y + RING - 1) % RING) // 2

    def slot_of(at_y):
        return ((at_y % FT + 1) % FT) // 2

    my_head = x * 4 + quarter(y)
    y_partner = (y + RING - 1 + 2 * (y % 2)) % RING

    def device(to_y, to_r, to_x):
        return {"slab": (to_y % FT) * rows + to_r, "head": to_x * 2 + to_y // FT}

    r_at = ((r + rows - 1) % rows, r, (r + 1) % rows)
    x_at = tuple((x + step) % columns for step in range(columns))

    def at_side(side):
        return pl.when(r < rows - 1) if side == 2 else pl.when(r >= 1 - side)

    barrier = pltpu.get_barrier_semaphore()

    def greet(peers):
        for peer in peers:
            pl.semaphore_signal(barrier, 1, device_id=peer, device_id_type=MESH)

    greet([device(to_y, r, to_x) for to_y in y_far for to_x in x_at])
    greet([device(y_partner, r, x)])
    for side in (0, 2):
        @at_side(side)
        def _():
            greet([device(y, r_at[side], x), device(y_partner, r_at[side], x)])

    listed[...] = jnp.full(listed.shape, -2.0, F32)

    def put(which, array):
        for piece in range(4 * columns):
            stage[which, piece] = array[:, piece * HD : (piece + 1) * HD]

    loads[4].wait()
    loads[0].wait()
    put(KEY, (raw[0].astype(F32) * key_scale[...]).astype(BF16))
    loads[1].wait()
    put(VALUE, raw[1])
    row_sides = (r + rows - 1) // rows + (2 * rows - 2 - r) // rows
    pl.semaphore_wait(barrier, 4 * columns + 1 + 2 * row_sides)

    my_rows = pl.ds(pl.multiple_of(head * chunk, chunk), chunk)

    def send_heads(kind, places):
        for to_x in x_at:
            for to_y in places:
                pltpu.make_async_remote_copy(
                    src_ref=stage.at[ARRAYS[kind], to_x * 4 + quarter(to_y)],
                    dst_ref=data.at[ARRAYS[kind], slot_of(y), 1, my_rows, :],
                    send_sem=a2a_send.at[kind],
                    recv_sem=a2a_recv.at[kind, slot_of(y)],
                    device_id=device(to_y, r, to_x),
                    device_id_type=MESH,
                ).start()

    def wait_heads(kind, slot):
        whole = data.at[ARRAYS[kind], slot, 1]
        pltpu.make_async_copy(whole, whole, a2a_recv.at[kind, slot]).wait()

    def y_copy(kind):
        return pltpu.make_async_remote_copy(
            src_ref=data.at[ARRAYS[kind], INNER, 1],
            dst_ref=data.at[ARRAYS[kind], BEYOND, 1],
            send_sem=halo_send.at[kind, 6],
            recv_sem=y_recv.at[kind],
            device_id=device(y_partner, r, x),
            device_id_type=MESH,
        )

    def start_rows(copies):
        for side, copy in copies.items():
            at_side(side)(copy.start)

    def sent_rows(copies):
        for side, copy in copies.items():
            at_side(side)(copy.wait_send)

    def came_rows(copies):
        for side, copy in copies.items():
            at_side(2 - side)(copy.wait_recv)

    def r_copies(kind, slot):
        return {
            side: pltpu.make_async_remote_copy(
                src_ref=data.at[ARRAYS[kind], slot, 1],
                dst_ref=data.at[ARRAYS[kind], slot, 2 - side],
                send_sem=halo_send.at[kind, slot * 2 + side // 2],
                recv_sem=r_recv.at[kind, slot, side // 2],
                device_id=device(y, r_at[side], x),
                device_id_type=MESH,
            )
            for side in (0, 2)
        }

    def spread(kind, slot):
        start_rows(r_copies(kind, slot))

    def forward(kind):
        y_copy(kind).wait_recv()
        spread(kind, BEYOND)

    def wait_rows(kind, slot):
        came_rows(r_copies(kind, slot))

    send_heads(KV, y_far)
    loads[6].wait()
    listed[0:TW, 0:27] = neighbours[...].astype(F32)
    for to_y in y_far:
        pltpu.make_async_remote_copy(
            src_ref=listed, dst_ref=lists.at[y_hi, slot_of(y)],
            send_sem=list_send, recv_sem=list_recv,
            device_id=device(to_y, r, x), device_id_type=MESH,
        ).start()

    loads[5].wait()
    factor = query_scale[...] * HD ** (-0.5)
    loads[2].wait()
    put(QUERY, (raw[2].astype(F32) * factor).astype(BF16))
    send_heads(Q, y_far)
    loads[3].wait()
    put(GRAD, raw[3])
    send_heads(G, y_far)

    for side in (0, 2):
        @pl.when(r == (rows - 1 if side == 2 else 0))
        def _():
            data[:, :, side] = jnp.zeros((4, 3, SLAB, HD), BF16)
            stats[:, side] = jnp.full((3, 2, 8, SLAB), HIDDEN, F32)

    wait_heads(KV, INNER)
    y_copy(KV).start()
    spread(KV, INNER)
    wait_heads(KV, OUTER)
    spread(KV, OUTER)

    pltpu.make_async_copy(lists, lists, list_recv).wait()
    shape = (BLOCKS * 8, 128)
    line = lax.broadcasted_iota(jnp.int32, shape, 0)
    column = line % 8
    block_of = line // 8
    key_slot = block_of // 3
    key_frame = jnp.where(
        key_slot == 0, frame_of[0], jnp.where(key_slot == 1, frame_of[1], frame_of[2])
    )
    key_row = r + block_of % 3 - 1
    real = (column < TW) & (key_row >= 0) & (key_row < rows)
    ids = jnp.where(real, (key_frame * rows + key_row) * TW + column, -5).astype(F32)
    lane_tile = lax.broadcasted_iota(jnp.int32, (BLOCKS * 8, SLAB), 1) // TILE
    lane = lax.broadcasted_iota(jnp.int32, (8, 128), 1)
    for slot in (OUTER, INNER):
        found = jnp.full((BLOCKS * 8, SLAB), HIDDEN, F32)
        for tile in range(TW):
            hit = jnp.max(
                jnp.where(lists[0, slot, tile : tile + 1, :] == ids, 0.0, HIDDEN),
                axis=1, keepdims=True,
            )
            found = jnp.where(lane_tile == tile, hit, found)
        bias[slot] = found.reshape(BLOCKS, 8, SLAB)
        turned = jnp.concatenate(
            [
                jnp.concatenate(
                    [found[:, tile * TILE : tile * TILE + 1] for tile in range(TW)]
                    + [jnp.full((BLOCKS * 8, 124), HIDDEN, F32)],
                    axis=1,
                ),
                jnp.full((56, 128), HIDDEN, F32),
            ],
            axis=0,
        ).T[:8]
        for key_block in range(BLOCKS):
            for side in range(2):
                at = key_block * 8 + side * 2
                bias_rows[slot, key_block // 3, side, :, pl.ds(key_block % 3 * 128, 128)] = jnp.where(
                    lane < TILE, turned[:, at : at + 1], turned[:, at + 1 : at + 2]
                )

    wait_heads(Q, INNER)
    y_copy(Q).start()
    spread(Q, INNER)
    wait_heads(Q, OUTER)
    spread(Q, OUTER)

    def return_heads(kind, slot):
        for to_x in x_at:
            for far_hi in range(2):
                to_y = frame_of[slot] + far_hi * FT
                token_chunk = to_x * 2 + far_hi
                part = pl.ds(pl.multiple_of(token_chunk * chunk, chunk), chunk)
                pltpu.make_async_remote_copy(
                    src_ref=results.at[kind, slot, :, part, :],
                    dst_ref=landed.at[kind, my_head],
                    send_sem=out_send.at[kind],
                    recv_sem=out_recv.at[kind],
                    device_id=device(to_y, r, to_x),
                    device_id_type=MESH,
                ).start()

    def my_scale(scale):
        return scale[:, pl.ds(pl.multiple_of(my_head * HD, HD), HD)]

    def stat_copies(slot):
        return {
            side: pltpu.make_async_remote_copy(
                src_ref=stats_sent.at[slot, side, 0:2],
                dst_ref=stats.at[slot, 2 - side],
                send_sem=stat_send.at[slot, side // 2],
                recv_sem=stat_recv.at[slot, side // 2],
                device_id=device(y, r_at[side], x),
                device_id_type=MESH,
            )
            for side in (0, 2)
        }

    def far_stat_copies():
        return {
            side: pltpu.make_async_remote_copy(
                src_ref=stats_sent.at[INNER, side, BEYOND],
                dst_ref=stats.at[BEYOND, 2 - side, INNER],
                send_sem=far_send.at[side],
                recv_sem=far_recv.at[side],
                device_id=device(y_partner, r_at[side], x),
                device_id_type=MESH,
            )
            for side in range(3)
        }

    def rows_of(array, slot, side):
        return jnp.concatenate(
            [data[array, slot, row, own(side), :] for row in range(3)], axis=0
        )

    def attend(slot, key_slots, arrive, least):
        parts = [(key_slot, side) for key_slot in key_slots for side in range(2)]
        peak = [jnp.full((3 * TILE, 128), -3e38, F32) for side in range(2)]
        for key_slot, side in parts:
            if side == 0:
                arrive(key_slot)
            part = add_rows(
                dot_nt(data[QUERY, slot, 1, near(side), :], rows_of(KEY, key_slot, side)),
                bias_rows[slot, key_slot, side, side : side + 3, :],
            )
            scores[key_slot, side] = part
            peak[side] = jnp.maximum(peak[side], fold(part, jnp.maximum))
        row_max = jnp.max(join(*peak, jnp.maximum), axis=1, keepdims=True)
        row_wide = jnp.maximum(jnp.broadcast_to(row_max, (SLAB, 128)), least)
        totals = [jnp.zeros((3 * TILE, 128), F32) for side in range(2)]
        sums = [jnp.zeros((3 * TILE, HD), F32) for side in range(2)]
        for key_slot, side in parts:
            part = jnp.exp(scores[key_slot, side] - wide(row_wide[near(side)]))
            low = part.astype(BF16)
            weights[slot, key_slot, side] = low
            totals[side] = totals[side] + fold(part, jnp.add)
            sums[side] = sums[side] + dot_nn(low, rows_of(VALUE, key_slot, side))
        total = jnp.sum(join(*totals, jnp.add), axis=1, keepdims=True)
        return row_wide, jnp.broadcast_to(total, (SLAB, 128)), join(*sums, jnp.add)

    def settle(slot, row_wide, total, summed, earlier):
        inverse = 1.0 / total
        results[0, slot, 0] = (summed * inverse).astype(BF16)
        inverses[slot, 0] = inverse * earlier
        inverses[slot, 1] = inverse
        log_totals[slot] = row_wide + jnp.log(total)

    def tell(slot):
        grads = data[GRAD, slot, 1].astype(F32)
        delta = jnp.sum(results[0, slot, 0].astype(F32) * grads, axis=1, keepdims=True)
        lane = lax.broadcasted_iota(jnp.int32, (SLAB, 128), 1)
        turned = jnp.where(lane == 0, log_totals[slot], delta).T
        log_row, delta_row = turned[0:1], turned[1:2]
        line8 = lax.broadcasted_iota(jnp.int32, (8, SLAB), 0)
        for key_slot in (OUTER, INNER) if slot == OUTER else (OUTER, INNER, BEYOND):
            for row in range(3):
                message = jnp.where(
                    line8 == TW, delta_row, bias[slot, key_slot * 3 + row] - log_row
                )
                if row == 1 and key_slot != BEYOND:
                    stats[slot, 1, key_slot] = message
                else:
                    stats_sent[slot, row, key_slot] = message
        start_rows(stat_copies(slot))
        if slot == INNER:
            start_rows(far_stat_copies())
        return delta

    def query_side(slot, delta):
        sums = [jnp.zeros((3 * TILE, HD), F32) for side in range(2)]
        for key_slot in (INNER, OUTER) if slot == OUTER else (INNER, OUTER, BEYOND):
            inverse = inverses[slot, 1 if key_slot == BEYOND else 0]
            delta_part = delta * inverse
            for side in range(2):
                grad_weights = dot_nt(
                    data[GRAD, slot, 1, near(side), :], rows_of(VALUE, key_slot, side)
                )
                part = weights[slot, key_slot, side].astype(F32) * (
                    grad_weights * wide(inverse[near(side)]) - wide(delta_part[near(side)])
                )
                sums[side] = sums[side] + dot_nn(
                    part.astype(BF16), rows_of(KEY, key_slot, side)
                )
        scale = my_scale(query_scale) * HD ** (-0.5)
        results[0, slot, 1] = (join(*sums, jnp.add) * scale).astype(BF16)
        return_heads(0, slot)

    def key_part(slot, query_slot):
        for side in range(2):
            message = jnp.concatenate(
                [stats[query_slot, row, slot, :, own(side)] for row in range(3)], axis=1
            )
            queries = rows_of(QUERY, query_slot, side)
            grads = rows_of(GRAD, query_slot, side)
            part = jnp.exp(add_rows(
                dot_nt(data[KEY, slot, 1, near(side), :], queries), message[side : side + 3]
            ))
            grad_weights = dot_nt(data[VALUE, slot, 1, near(side), :], grads)
            slopes = (part * (grad_weights - message[TW : TW + 1])).astype(BF16)
            for which, term in (
                (0, dot_nn(slopes, queries)), (1, dot_nn(part.astype(BF16), grads))
            ):
                if query_slot == OUTER:
                    key_sums[slot, which, side] = term
                else:
                    key_sums[slot, which, side] += term

    def key_end(slot):
        grad_keys = join(key_sums[slot, 0, 0], key_sums[slot, 0, 1], jnp.add)
        grad_values = join(key_sums[slot, 1, 0], key_sums[slot, 1, 1], jnp.add)
        results[1, slot, 0] = (grad_keys * my_scale(key_scale)).astype(BF16)
        results[1, slot, 1] = grad_values.astype(BF16)
        return_heads(1, slot)

    def queries_arrive(slot):
        wait_rows(Q, slot)
        wait_rows(G, slot)
        came_rows(far_stat_copies() if slot == BEYOND else stat_copies(slot))

    lowest = jnp.full((SLAB, 128), -3e38, F32)
    settle(
        OUTER,
        *attend(OUTER, (INNER, OUTER), lambda key_slot: wait_rows(KV, key_slot), lowest),
        1.0,
    )
    first = attend(INNER, (INNER, OUTER), lambda key_slot: None, lowest)
    for i in range(3):
        kept[i] = first[i]
    wait_heads(G, INNER)
    y_copy(G).start()
    spread(G, INNER)
    wait_heads(G, OUTER)
    spread(G, OUTER)
    outer_delta = tell(OUTER)
    forward(KV)
    query_side(OUTER, outer_delta)
    queries_arrive(OUTER)
    key_part(OUTER, OUTER)
    key_part(INNER, OUTER)
    forward(Q)
    forward(G)
    row_wide, total, summed = attend(
        INNER, (BEYOND,), lambda key_slot: wait_rows(KV, key_slot), kept[0]
    )
    earlier = jnp.exp(kept[0] - row_wide)
    settle(INNER, row_wide, total + kept[1] * earlier, summed + kept[2] * earlier, earlier)
    query_side(INNER, tell(INNER))
    queries_arrive(INNER)
    key_part(OUTER, INNER)
    key_end(OUTER)
    key_part(INNER, INNER)
    queries_arrive(BEYOND)
    key_part(INNER, BEYOND)
    key_end(INNER)

    for kind in range(2):
        pltpu.make_async_copy(landed.at[kind], landed.at[kind], out_recv.at[kind]).wait()
    sent = lists.at[0:2]
    pltpu.make_async_copy(sent, sent, list_send).wait()
    for kind in (KV, Q, G):
        sent = stage.at[ARRAYS[kind]]
        pltpu.make_async_copy(sent, sent, a2a_send.at[kind]).wait()
        for slot in range(3):
            sent_rows(r_copies(kind, slot))
        y_copy(kind).wait_send()
    for kind in range(2):
        sent = results.at[kind]
        pltpu.make_async_copy(sent, sent, out_send.at[kind]).wait()
    for slot in (OUTER, INNER):
        sent_rows(stat_copies(slot))
    sent_rows(far_stat_copies())


def hand_out(landed, attention, grad_query, grad_key, grad_value, pieces, held, sems):
    targets = (attention, grad_query, grad_key, grad_value)
    loads = [
        pltpu.make_async_copy(landed.at[kind], pieces.at[kind], sems.at[0, kind])
        for kind in range(2)
    ]
    stores = [pltpu.make_async_copy(held.at[i], targets[i], sems.at[1, i]) for i in range(4)]
    for load in loads:
        load.start()
    for i in range(4):
        if i % 2 == 0:
            loads[i // 2].wait()
        for head in range(landed.shape[1]):
            held[i, :, head * HD : (head + 1) * HD] = pieces[i // 2, head, i % 2]
        stores[i].start()
    for store in stores:
        store.wait()


def local(query, key, value, grad_out, query_scale, key_scale, neighbours):
    rows = lax.axis_size("slab") // FT
    columns = lax.axis_size("head") // 2
    chunk, width = query.shape
    out = jax.ShapeDtypeStruct((chunk, width), BF16)
    landing = (2, width // HD, 2, chunk, HD)
    hbm = pl.BlockSpec(memory_space=pltpu.HBM)
    dma = pltpu.SemaphoreType.DMA
    landed = pl.pallas_call(
        functools.partial(kernel, rows, columns),
        out_shape=jax.ShapeDtypeStruct(landing, BF16),
        in_specs=[hbm] * 7,
        out_specs=hbm,
        scratch_shapes=[
            pltpu.VMEM((4, chunk, width), BF16),
            pltpu.VMEM((1, width), F32),
            pltpu.VMEM((1, width), F32),
            pltpu.VMEM(neighbours.shape, jnp.int32),
            pltpu.VMEM((4, 4 * columns, chunk, HD), BF16),
            pltpu.VMEM((4, 3, 3, SLAB, HD), BF16),
            pltpu.VMEM((8, 128), F32),
            pltpu.VMEM((2, 2, 8, 128), F32),
            pltpu.VMEM((2, BLOCKS, 8, SLAB), F32),
            pltpu.VMEM((2, 3, 2, 8, 3 * 128), F32),
            pltpu.VMEM((3, 2, 3 * TILE, 3 * 128), F32),
            pltpu.VMEM((2, 3, 2, 3 * TILE, 3 * 128), BF16),
            pltpu.VMEM((2, 2, SLAB, 128), F32),
            pltpu.VMEM((2, SLAB, 128), F32),
            pltpu.VMEM((3, SLAB, 128), F32),
            pltpu.VMEM((2, 2, 2, 3 * TILE, HD), F32),
            pltpu.VMEM((3, 3, 2, 8, SLAB), F32),
            pltpu.VMEM((2, 3, 3, 8, SLAB), F32),
            pltpu.VMEM((2, 2, 2, SLAB, HD), BF16),
            dma((7,)),
            dma((3,)),
            dma((3, 2)),
            dma,
            dma,
            dma((3, 7)),
            dma((3,)),
            dma((3, 3, 2)),
            dma((2, 2)),
            dma((2, 2)),
            dma((3,)),
            dma((3,)),
            dma((2,)),
            dma((2,)),
        ],
        compiler_params=pltpu.CompilerParams(
            collective_id=0, has_side_effects=True, vmem_limit_bytes=VMEM_BYTES
        ),
        name="tiles",
    )(
        query, key, value, grad_out,
        query_scale.reshape(1, width), key_scale.reshape(1, width), neighbours,
    )
    return pl.pallas_call(
        hand_out,
        out_shape=(out,) * 4,
        in_specs=[hbm],
        out_specs=(hbm,) * 4,
        scratch_shapes=[
            pltpu.VMEM(landing, BF16), pltpu.VMEM((4, chunk, width), BF16), dma((2, 4)),
        ],
        compiler_params=pltpu.CompilerParams(vmem_limit_bytes=VMEM_BYTES),
        name="hand_out",
    )(landed)


def solution(mesh):
    token = P(("slab", "head"), None)
    return jax.shard_map(
        local,
        mesh=mesh,
        in_specs=(token, token, token, token, P(), P(), P("slab", None)),
        out_specs=(token,) * 4,
        check_vma=False,
    )
```

```python
import functools

import jax
import jax.numpy as jnp
from jax import lax
from jax.experimental import pallas as pl
from jax.experimental.pallas import tpu as pltpu
from jax.sharding import PartitionSpec as P

HD = 128
TILE = 64
FT = 4
TW = 4
SLAB = TILE * TW
RING = 2 * FT
BLOCKS = 9
OUTER, INNER, BEYOND = 0, 1, 2
HIDDEN = -1e30
MESH = pl.DeviceIdType.MESH
BF16 = jnp.bfloat16
F32 = jnp.float32
KV, QD = 0, 1
VMEM_BYTES = 58 * 1024 * 1024


def dot_nn(a, b):
    return lax.dot_general(a, b, (((1,), (0,)), ((), ())), preferred_element_type=F32)


def dot_nt(a, b):
    return lax.dot_general(a, b, (((1,), (1,)), ((), ())), preferred_element_type=F32)


def dot_tn(a, b):
    return lax.dot_general(a, b, (((0,), (0,)), ((), ())), preferred_element_type=F32)


def add_rows(scores, rows):
    shaped = scores.reshape(3, TILE, scores.shape[1]) + rows[:, None, :]
    return shaped.reshape(scores.shape)


def join(low, high, both):
    return jnp.concatenate(
        [low[:TILE], both(low[TILE:], high[: 2 * TILE]), high[2 * TILE :]], axis=0
    )


def fold(array, both):
    return both(both(array[:, :128], array[:, 128:256]), array[:, 256:])


def wide(column):
    return jnp.concatenate([column] * 3, axis=1)


def near(half):
    return slice(half * TILE, half * TILE + 3 * TILE)


def own(half):
    return slice(half * 2 * TILE, (half + 1) * 2 * TILE)


def kernel(
    rows, columns,
    query, key, value, grad_out, query_scale_in, key_scale_in, neighbours_in, landed,
    raw, query_scale, key_scale, neighbours,
    stage, data, listed, lists, bias, bias_rows, scores, weights, stats, stats_sent, results,
    in_sem, a2a_send, a2a_recv, list_send, list_recv, halo_send, y_recv, r_recv,
    stat_send, stat_recv, far_send, far_recv, out_send, out_recv,
):
    loads = [
        pltpu.make_async_copy(source, target, in_sem.at[i])
        for i, (source, target) in enumerate((
            (key, raw.at[0]), (value, raw.at[1]), (query, raw.at[2]), (grad_out, raw.at[3]),
            (key_scale_in, key_scale), (query_scale_in, query_scale),
            (neighbours_in, neighbours),
        ))
    ]
    for load in (loads[4], *loads[:4], *loads[5:]):
        load.start()

    slab = lax.axis_index("slab")
    head = lax.axis_index("head")
    y_lo, r = slab // rows, slab % rows
    x, y_hi = head // 2, head % 2
    y = y_hi * FT + y_lo
    chunk = SLAB // (2 * columns)
    half = 1 - y_lo // 2
    far_y = (1 - y_lo // 2) * 2
    y_far = (far_y, far_y + 1, far_y + FT, far_y + FT + 1)
    frame_of = (3 * half, 1 + half, 2 - half)

    def quarter(at_y):
        return ((at_y + RING - 1) % RING) // 2

    def slot_of(at_y):
        return ((at_y % FT + 1) % FT) // 2

    my_head = x * 4 + quarter(y)
    y_partner = (y + RING - 1 + 2 * (y % 2)) % RING

    def device(to_y, to_r, to_x):
        return {"slab": (to_y % FT) * rows + to_r, "head": to_x * 2 + to_y // FT}

    odd = r % 2
    planes = rows // 2
    plane = r // 2
    chip_slot, cross_slot = 2 - 2 * odd, 2 * odd
    chip_row = r + 1 - 2 * odd
    cross_row = (r + rows - 1 + 2 * odd) % rows
    relay_row = (r + rows + 2 - 4 * odd) % rows
    from_relay_row = (r + rows - 2 + 4 * odd) % rows
    below = (plane + planes - 1) // planes
    above = (2 * planes - 2 - plane) // planes
    crosses = below * (1 - odd) + above * odd
    relays = above * (1 - odd) + below * odd

    r_at = ((r + rows - 1) % rows, r, (r + 1) % rows)
    x_at = tuple((x + step) % columns for step in range(columns))

    def at_side(side):
        return pl.when(r < rows - 1) if side == 2 else pl.when(r >= 1 - side)

    barrier = pltpu.get_barrier_semaphore()

    def greet(peers):
        for peer in peers:
            pl.semaphore_signal(barrier, 1, device_id=peer, device_id_type=MESH)

    greet([device(to_y, r, to_x) for to_y in y_far for to_x in x_at])
    greet([device(y_partner, r, x)])
    for side in (0, 2):
        @at_side(side)
        def _():
            greet([device(y, r_at[side], x), device(y_partner, r_at[side], x)])

    @pl.when(relays == 1)
    def _():
        greet([device(y, relay_row, x)])

    @pl.when(crosses == 1)
    def _():
        greet([device(y, from_relay_row, x)])


    listed[...] = jnp.full(listed.shape, -2.0, F32)

    def put(kind, which, array):
        for piece in range(4 * columns):
            stage[kind, piece, which] = array[:, piece * HD : (piece + 1) * HD]

    loads[4].wait()
    loads[0].wait()
    put(KV, 0, (raw[0].astype(F32) * key_scale[...]).astype(BF16))
    loads[1].wait()
    put(KV, 1, raw[1])
    row_sides = (r + rows - 1) // rows + (2 * rows - 2 - r) // rows
    pl.semaphore_wait(barrier, 4 * columns + 1 + 2 * row_sides + below + above)

    my_rows = pl.ds(pl.multiple_of(head * chunk, chunk), chunk)

    def send_heads(kind, places):
        for to_x in x_at:
            for to_y in places:
                pltpu.make_async_remote_copy(
                    src_ref=stage.at[kind, to_x * 4 + quarter(to_y)],
                    dst_ref=data.at[kind, slot_of(y), 1, :, my_rows, :],
                    send_sem=a2a_send.at[kind],
                    recv_sem=a2a_recv.at[kind, slot_of(y)],
                    device_id=device(to_y, r, to_x),
                    device_id_type=MESH,
                ).start()

    def wait_heads(kind, slot):
        whole = data.at[kind, slot, 1]
        pltpu.make_async_copy(whole, whole, a2a_recv.at[kind, slot]).wait()

    def y_copy(kind):
        return pltpu.make_async_remote_copy(
            src_ref=data.at[kind, INNER, 1],
            dst_ref=data.at[kind, BEYOND, 1],
            send_sem=halo_send.at[kind, 3, 0],
            recv_sem=y_recv.at[kind],
            device_id=device(y_partner, r, x),
            device_id_type=MESH,
        )

    def start_rows(copies):
        for side, copy in copies.items():
            at_side(side)(copy.start)

    def sent_rows(copies):
        for side, copy in copies.items():
            at_side(side)(copy.wait_send)

    def came_rows(copies):
        for side, copy in copies.items():
            at_side(2 - side)(copy.wait_recv)

    def chip_copy(kind, slot):
        return pltpu.make_async_remote_copy(
            src_ref=data.at[kind, slot, 1],
            dst_ref=data.at[kind, slot, cross_slot],
            send_sem=halo_send.at[kind, slot, 0],
            recv_sem=r_recv.at[kind, slot, 0],
            device_id=device(y, chip_row, x),
            device_id_type=MESH,
        )

    def cross_copy(kind, slot):
        return pltpu.make_async_remote_copy(
            src_ref=data.at[kind, slot, 1, 0],
            dst_ref=data.at[kind, slot, chip_slot, 0],
            send_sem=halo_send.at[kind, slot, 1],
            recv_sem=r_recv.at[kind, slot, 1],
            device_id=device(y, cross_row, x),
            device_id_type=MESH,
        )

    def relay_copy(kind, slot):
        return pltpu.make_async_remote_copy(
            src_ref=data.at[kind, slot, chip_slot, 1],
            dst_ref=data.at[kind, slot, cross_slot, 1],
            send_sem=halo_send.at[kind, slot, 2],
            recv_sem=r_recv.at[kind, slot, 2],
            device_id=device(y, relay_row, x),
            device_id_type=MESH,
        )

    def spread(kind, slot):
        pl.when(crosses == 1)(cross_copy(kind, slot).start)
        chip_copy(kind, slot).start()

    def relay(kind, slot):
        chip_copy(kind, slot).wait_recv()
        pl.when(relays == 1)(relay_copy(kind, slot).start)

    def forward(kind):
        y_copy(kind).wait_recv()
        spread(kind, BEYOND)

    def wait_rows(kind, slot):
        pl.when(crosses == 1)(cross_copy(kind, slot).wait_recv)
        pl.when(crosses == 1)(relay_copy(kind, slot).wait_recv)

    def rows_left(kind, slot):
        chip_copy(kind, slot).wait_send()
        pl.when(crosses == 1)(cross_copy(kind, slot).wait_send)
        pl.when(relays == 1)(relay_copy(kind, slot).wait_send)

    send_heads(KV, y_far)
    loads[6].wait()
    listed[0:TW, 0:27] = neighbours[...].astype(F32)
    for to_y in y_far:
        pltpu.make_async_remote_copy(
            src_ref=listed, dst_ref=lists.at[y_hi, slot_of(y)],
            send_sem=list_send, recv_sem=list_recv,
            device_id=device(to_y, r, x), device_id_type=MESH,
        ).start()

    loads[5].wait()
    factor = query_scale[...] * HD ** (-0.5)
    loads[2].wait()
    put(QD, 0, (raw[2].astype(F32) * factor).astype(BF16))
    loads[3].wait()
    put(QD, 1, raw[3])

    send_heads(QD, y_far)

    for side in (0, 2):
        @pl.when(r == (rows - 1 if side == 2 else 0))
        def _():
            data[:, :, side] = jnp.zeros((2, 3, 2, SLAB, HD), BF16)
            stats[:, side] = jnp.full((3, 2, 8, SLAB), HIDDEN, F32)

    wait_heads(KV, INNER)
    y_copy(KV).start()
    spread(KV, INNER)
    wait_heads(KV, OUTER)
    spread(KV, OUTER)
    relay(KV, INNER)
    relay(KV, OUTER)

    pltpu.make_async_copy(lists, lists, list_recv).wait()
    shape = (BLOCKS * 8, 128)
    line = lax.broadcasted_iota(jnp.int32, shape, 0)
    column = line % 8
    block_of = line // 8
    key_slot = block_of // 3
    key_frame = jnp.where(
        key_slot == 0, frame_of[0], jnp.where(key_slot == 1, frame_of[1], frame_of[2])
    )
    key_row = r + block_of % 3 - 1
    real = (column < TW) & (key_row >= 0) & (key_row < rows)
    ids = jnp.where(real, (key_frame * rows + key_row) * TW + column, -5).astype(F32)
    lane_tile = lax.broadcasted_iota(jnp.int32, (BLOCKS * 8, SLAB), 1) // TILE
    lane = lax.broadcasted_iota(jnp.int32, (8, 128), 1)
    for slot in (OUTER, INNER):
        found = jnp.full((BLOCKS * 8, SLAB), HIDDEN, F32)
        for tile in range(TW):
            hit = jnp.max(
                jnp.where(lists[0, slot, tile : tile + 1, :] == ids, 0.0, HIDDEN),
                axis=1, keepdims=True,
            )
            found = jnp.where(lane_tile == tile, hit, found)
        bias[slot] = found.reshape(BLOCKS, 8, SLAB)
        turned = jnp.concatenate(
            [
                jnp.concatenate(
                    [found[:, tile * TILE : tile * TILE + 1] for tile in range(TW)]
                    + [jnp.full((BLOCKS * 8, 124), HIDDEN, F32)],
                    axis=1,
                ),
                jnp.full((56, 128), HIDDEN, F32),
            ],
            axis=0,
        ).T[:8]
        for key_block in range(BLOCKS):
            for side in range(2):
                at = key_block * 8 + side * 2
                bias_rows[slot, key_block // 3, side, :, pl.ds(key_block % 3 * 128, 128)] = jnp.where(
                    lane < TILE, turned[:, at : at + 1], turned[:, at + 1 : at + 2]
                )

    wait_heads(QD, INNER)
    y_copy(QD).start()
    spread(QD, INNER)
    wait_heads(QD, OUTER)

    def return_heads(kind, slot):
        for to_x in x_at:
            for far_hi in range(2):
                to_y = frame_of[slot] + far_hi * FT
                token_chunk = to_x * 2 + far_hi
                part = pl.ds(pl.multiple_of(token_chunk * chunk, chunk), chunk)
                pltpu.make_async_remote_copy(
                    src_ref=results.at[kind, slot, :, part, :],
                    dst_ref=landed.at[kind, my_head],
                    send_sem=out_send.at[kind],
                    recv_sem=out_recv.at[kind],
                    device_id=device(to_y, r, to_x),
                    device_id_type=MESH,
                ).start()

    def my_scale(scale):
        return scale[:, pl.ds(pl.multiple_of(my_head * HD, HD), HD)]

    def stat_copies(slot):
        return {
            side: pltpu.make_async_remote_copy(
                src_ref=stats_sent.at[slot, side, 0:2],
                dst_ref=stats.at[slot, 2 - side],
                send_sem=stat_send.at[slot, side // 2],
                recv_sem=stat_recv.at[slot, side // 2],
                device_id=device(y, r_at[side], x),
                device_id_type=MESH,
            )
            for side in (0, 2)
        }

    def far_stat_copies():
        return {
            side: pltpu.make_async_remote_copy(
                src_ref=stats_sent.at[INNER, side, BEYOND],
                dst_ref=stats.at[BEYOND, 2 - side, INNER],
                send_sem=far_send.at[side],
                recv_sem=far_recv.at[side],
                device_id=device(y_partner, r_at[side], x),
                device_id_type=MESH,
            )
            for side in range(3)
        }

    def rows_of(kind, slot, which, side):
        return jnp.concatenate(
            [data[kind, slot, row, which, own(side), :] for row in range(3)], axis=0
        )

    def query_side(slot, arrive, between, later):
        key_slots = (INNER, OUTER) if slot == OUTER else (INNER, OUTER, BEYOND)
        parts = [(key_slot, side) for key_slot in key_slots for side in range(2)]
        peak = [jnp.full((3 * TILE, 128), -3e38, F32) for side in range(2)]
        for key_slot, side in parts:
            if side == 0:
                arrive(key_slot)
            part = add_rows(
                dot_nt(data[QD, slot, 1, 0, near(side), :], rows_of(KV, key_slot, 0, side)),
                bias_rows[slot, key_slot, side, side : side + 3, :],
            )
            scores[key_slot, side] = part
            peak[side] = jnp.maximum(peak[side], fold(part, jnp.maximum))
        row_max = jnp.max(join(*peak, jnp.maximum), axis=1, keepdims=True)
        between()

        row_wide = jnp.broadcast_to(row_max, (SLAB, 128))
        totals = [jnp.zeros((3 * TILE, 128), F32) for side in range(2)]
        sums = [jnp.zeros((3 * TILE, HD), F32) for side in range(2)]
        for key_slot, side in parts:
            part = jnp.exp(scores[key_slot, side] - wide(row_wide[near(side)]))
            low = part.astype(BF16)
            weights[key_slot, side] = low
            totals[side] = totals[side] + fold(part, jnp.add)
            sums[side] = sums[side] + dot_nn(low, rows_of(KV, key_slot, 1, side))
        total = jnp.sum(join(*totals, jnp.add), axis=1, keepdims=True)
        inverse = jnp.broadcast_to(1.0 / total, (SLAB, 128))
        attended = (join(*sums, jnp.add) * inverse).astype(BF16)
        results[0, slot, 0] = attended
        grads = data[QD, slot, 1, 1].astype(F32)
        delta = jnp.sum(attended.astype(F32) * grads, axis=1, keepdims=True)
        log_total = row_max + jnp.log(total)
        lane = lax.broadcasted_iota(jnp.int32, (SLAB, 128), 1)
        turned = jnp.where(lane == 0, log_total, delta).T
        log_row, delta_row = turned[0:1], turned[1:2]
        line8 = lax.broadcasted_iota(jnp.int32, (8, SLAB), 0)
        for key_slot in key_slots:
            for row in range(3):
                message = jnp.where(
                    line8 == TW, delta_row, bias[slot, key_slot * 3 + row] - log_row
                )
                if row == 1 and key_slot != BEYOND:
                    stats[slot, 1, key_slot] = message
                else:
                    stats_sent[slot, row, key_slot] = message
        start_rows(stat_copies(slot))
        if slot == INNER:
            start_rows(far_stat_copies())
        delta_part = delta * inverse
        later()

        sums = [jnp.zeros((3 * TILE, HD), F32) for side in range(2)]
        for key_slot, side in parts:
            grad_weights = dot_nt(
                data[QD, slot, 1, 1, near(side), :], rows_of(KV, key_slot, 1, side)
            )
            part = weights[key_slot, side].astype(F32) * (
                grad_weights * wide(inverse[near(side)]) - wide(delta_part[near(side)])
            )
            sums[side] = sums[side] + dot_nn(part.astype(BF16), rows_of(KV, key_slot, 0, side))
        scale = my_scale(query_scale) * HD ** (-0.5)
        results[0, slot, 1] = (join(*sums, jnp.add) * scale).astype(BF16)
        return_heads(0, slot)

    def key_side(slot, arrive):
        query_slots = (OUTER, INNER) if slot == OUTER else (OUTER, INNER, BEYOND)
        key_sums = [jnp.zeros((3 * TILE, HD), F32) for side in range(2)]
        value_sums = [jnp.zeros((3 * TILE, HD), F32) for side in range(2)]
        for query_slot in query_slots:
            arrive(query_slot)
            for side in range(2):
                message = jnp.concatenate(
                    [stats[query_slot, row, slot, :, own(side)] for row in range(3)], axis=1
                )
                queries = rows_of(QD, query_slot, 0, side)
                grads = rows_of(QD, query_slot, 1, side)
                part = jnp.exp(add_rows(
                    dot_nt(data[KV, slot, 1, 0, near(side), :], queries),
                    message[side : side + 3],
                ))
                grad_weights = dot_nt(data[KV, slot, 1, 1, near(side), :], grads)
                slopes = (part * (grad_weights - message[TW : TW + 1])).astype(BF16)
                value_sums[side] = value_sums[side] + dot_nn(part.astype(BF16), grads)
                key_sums[side] = key_sums[side] + dot_nn(slopes, queries)
        grad_keys = join(*key_sums, jnp.add)
        results[1, slot, 0] = (grad_keys * my_scale(key_scale)).astype(BF16)
        results[1, slot, 1] = join(*value_sums, jnp.add).astype(BF16)
        return_heads(1, slot)

    def beyond_arrives(key_slot):
        if key_slot == BEYOND:
            wait_rows(KV, BEYOND)

    def pair_arrives(query_slot):
        wait_rows(QD, query_slot)
        came_rows(stat_copies(query_slot))

    def beyond_queries_arrive(query_slot):
        if query_slot == BEYOND:
            wait_rows(QD, BEYOND)
            came_rows(far_stat_copies())

    def after_scores():
        forward(KV)
        relay(QD, INNER)
        spread(QD, OUTER)

    def after_attention():
        relay(KV, BEYOND)
        relay(QD, OUTER)

    query_side(
        OUTER, lambda key_slot: wait_rows(KV, key_slot), after_scores, after_attention
    )
    query_side(
        INNER, beyond_arrives, lambda: forward(QD), lambda: relay(QD, BEYOND)
    )
    key_side(OUTER, pair_arrives)
    key_side(INNER, beyond_queries_arrive)

    for kind in range(2):
        pltpu.make_async_copy(landed.at[kind], landed.at[kind], out_recv.at[kind]).wait()
    sent = lists.at[0:2]
    pltpu.make_async_copy(sent, sent, list_send).wait()
    for kind in range(2):
        sent = stage.at[kind]
        pltpu.make_async_copy(sent, sent, a2a_send.at[kind]).wait()
        for slot in range(3):
            rows_left(kind, slot)
        y_copy(kind).wait_send()
        sent = results.at[kind]
        pltpu.make_async_copy(sent, sent, out_send.at[kind]).wait()
    for slot in (OUTER, INNER):
        sent_rows(stat_copies(slot))
    sent_rows(far_stat_copies())


def hand_out(landed, attention, grad_query, grad_key, grad_value, pieces, held, sems):
    targets = (attention, grad_query, grad_key, grad_value)
    loads = [
        pltpu.make_async_copy(landed.at[kind], pieces.at[kind], sems.at[0, kind])
        for kind in range(2)
    ]
    stores = [pltpu.make_async_copy(held.at[i], targets[i], sems.at[1, i]) for i in range(4)]
    for load in loads:
        load.start()
    for i in range(4):
        if i % 2 == 0:
            loads[i // 2].wait()
        for head in range(landed.shape[1]):
            held[i, :, head * HD : (head + 1) * HD] = pieces[i // 2, head, i % 2]
        stores[i].start()
    for store in stores:
        store.wait()


def local(query, key, value, grad_out, query_scale, key_scale, neighbours):
    rows = lax.axis_size("slab") // FT
    columns = lax.axis_size("head") // 2
    chunk, width = query.shape
    out = jax.ShapeDtypeStruct((chunk, width), BF16)
    landing = (2, width // HD, 2, chunk, HD)
    hbm = pl.BlockSpec(memory_space=pltpu.HBM)
    dma = pltpu.SemaphoreType.DMA
    landed = pl.pallas_call(
        functools.partial(kernel, rows, columns),
        out_shape=jax.ShapeDtypeStruct(landing, BF16),
        in_specs=[hbm] * 7,
        out_specs=hbm,
        scratch_shapes=[
            pltpu.VMEM((4, chunk, width), BF16),
            pltpu.VMEM((1, width), F32),
            pltpu.VMEM((1, width), F32),
            pltpu.VMEM(neighbours.shape, jnp.int32),
            pltpu.VMEM((2, 4 * columns, 2, chunk, HD), BF16),
            pltpu.VMEM((2, 3, 3, 2, SLAB, HD), BF16),
            pltpu.VMEM((8, 128), F32),
            pltpu.VMEM((2, 2, 8, 128), F32),
            pltpu.VMEM((2, BLOCKS, 8, SLAB), F32),
            pltpu.VMEM((2, 3, 2, 8, 3 * 128), F32),
            pltpu.VMEM((3, 2, 3 * TILE, 3 * 128), F32),
            pltpu.VMEM((3, 2, 3 * TILE, 3 * 128), BF16),
            pltpu.VMEM((3, 3, 2, 8, SLAB), F32),
            pltpu.VMEM((2, 3, 3, 8, SLAB), F32),
            pltpu.VMEM((2, 2, 2, SLAB, HD), BF16),
            dma((7,)),
            dma((2,)),
            dma((2, 2)),
            dma,
            dma,
            dma((2, 4, 3)),
            dma((2,)),
            dma((2, 3, 3)),
            dma((2, 2)),
            dma((2, 2)),
            dma((3,)),
            dma((3,)),
            dma((2,)),
            dma((2,)),
        ],
        compiler_params=pltpu.CompilerParams(
            collective_id=0, has_side_effects=True, vmem_limit_bytes=VMEM_BYTES
        ),
        name="tiles",
    )(
        query, key, value, grad_out,
        query_scale.reshape(1, width), key_scale.reshape(1, width), neighbours,
    )
    return pl.pallas_call(
        hand_out,
        out_shape=(out,) * 4,
        in_specs=[hbm],
        out_specs=(hbm,) * 4,
        scratch_shapes=[
            pltpu.VMEM(landing, BF16), pltpu.VMEM((4, chunk, width), BF16), dma((2, 4)),
        ],
        compiler_params=pltpu.CompilerParams(vmem_limit_bytes=VMEM_BYTES),
        name="hand_out",
    )(landed)


def solution(mesh):
    token = P(("slab", "head"), None)
    return jax.shard_map(
        local,
        mesh=mesh,
        in_specs=(token, token, token, token, P(), P(), P("slab", None)),
        out_specs=(token,) * 4,
        check_vma=False,
    )
```

```python
import functools

import jax
import jax.numpy as jnp
from jax import lax
from jax.experimental import pallas as pl
from jax.experimental.pallas import tpu as pltpu
from jax.sharding import PartitionSpec as P

HD = 128
TILE = 64
FT = 4
TW = 4
SLAB = TILE * TW
RING = 2 * FT
BLOCKS = 9
OUTER, INNER, BEYOND = 0, 1, 2
PAIR = (OUTER, INNER)
HIDDEN = -1e30
MESH = pl.DeviceIdType.MESH
BF16 = jnp.bfloat16
F32 = jnp.float32
KV, QD = 0, 1
VMEM_BYTES = 58 * 1024 * 1024


def dot_nn(a, b):
    return lax.dot_general(a, b, (((1,), (0,)), ((), ())), preferred_element_type=F32)


def dot_nt(a, b):
    return lax.dot_general(a, b, (((1,), (1,)), ((), ())), preferred_element_type=F32)


def dot_tn(a, b):
    return lax.dot_general(a, b, (((0,), (0,)), ((), ())), preferred_element_type=F32)


def add_rows(scores, rows):
    shaped = scores.reshape(3, TILE, scores.shape[1]) + rows[:, None, :]
    return shaped.reshape(scores.shape)


def join(low, high, both):
    return jnp.concatenate(
        [low[:TILE], both(low[TILE:], high[: 2 * TILE]), high[2 * TILE :]], axis=0
    )


def fold(array, both):
    parts = [array[:, at : at + 128] for at in range(0, array.shape[1], 128)]
    return functools.reduce(both, parts)


def wide(column, slots):
    return jnp.concatenate([column] * (3 * len(slots)), axis=1)


def place(slots, half):
    at = 0 if slots == PAIR else len(PAIR) * 3 * 128
    return half, slice(None), slice(at, at + len(slots) * 3 * 128)


def near(half):
    return slice(half * TILE, half * TILE + 3 * TILE)


def own(half):
    return slice(half * 2 * TILE, (half + 1) * 2 * TILE)


def kernel(
    rows, columns,
    query, key, value, grad_out, query_scale_in, key_scale_in, neighbours_in, landed,
    raw, query_scale, key_scale, neighbours,
    stage, data, listed, lists, bias, bias_rows, scores, weights, stats, stats_sent, results,
    in_sem, a2a_send, a2a_recv, list_send, list_recv, halo_send, y_recv, r_recv,
    stat_send, stat_recv, far_send, far_recv, out_send, out_recv,
):
    loads = [
        pltpu.make_async_copy(source, target, in_sem.at[i])
        for i, (source, target) in enumerate((
            (key, raw.at[0]), (value, raw.at[1]), (query, raw.at[2]), (grad_out, raw.at[3]),
            (key_scale_in, key_scale), (query_scale_in, query_scale),
            (neighbours_in, neighbours),
        ))
    ]
    for load in (loads[4], *loads[:4], *loads[5:]):
        load.start()

    slab = lax.axis_index("slab")
    head = lax.axis_index("head")
    y_lo, r = slab // rows, slab % rows
    x, y_hi = head // 2, head % 2
    y = y_hi * FT + y_lo
    chunk = SLAB // (2 * columns)
    half = 1 - y_lo // 2
    far_y = (1 - y_lo // 2) * 2
    y_far = (far_y, far_y + 1, far_y + FT, far_y + FT + 1)
    frame_of = (3 * half, 1 + half, 2 - half)

    def quarter(at_y):
        return ((at_y + RING - 1) % RING) // 2

    def slot_of(at_y):
        return ((at_y % FT + 1) % FT) // 2

    my_head = x * 4 + quarter(y)
    y_partner = (y + RING - 1 + 2 * (y % 2)) % RING

    def device(to_y, to_r, to_x):
        return {"slab": (to_y % FT) * rows + to_r, "head": to_x * 2 + to_y // FT}

    r_at = ((r + rows - 1) % rows, r, (r + 1) % rows)
    x_at = tuple((x + step) % columns for step in range(columns))

    def at_side(side):
        return pl.when(r < rows - 1) if side == 2 else pl.when(r >= 1 - side)

    barrier = pltpu.get_barrier_semaphore()

    def greet(peers):
        for peer in peers:
            pl.semaphore_signal(barrier, 1, device_id=peer, device_id_type=MESH)

    greet([device(to_y, r, to_x) for to_y in y_far for to_x in x_at])
    greet([device(y_partner, r, x)])
    for side in (0, 2):
        @at_side(side)
        def _():
            greet([device(y, r_at[side], x), device(y_partner, r_at[side], x)])

    listed[...] = jnp.full(listed.shape, -2.0, F32)

    def put(kind, which, array):
        for piece in range(4 * columns):
            stage[kind, piece, which] = array[:, piece * HD : (piece + 1) * HD]

    loads[4].wait()
    loads[0].wait()
    put(KV, 0, (raw[0].astype(F32) * key_scale[...]).astype(BF16))
    loads[1].wait()
    put(KV, 1, raw[1])
    row_sides = (r + rows - 1) // rows + (2 * rows - 2 - r) // rows
    pl.semaphore_wait(barrier, 4 * columns + 1 + 2 * row_sides)

    my_rows = pl.ds(pl.multiple_of(head * chunk, chunk), chunk)

    def send_heads(kind, places):
        for to_x in x_at:
            for to_y in places:
                pltpu.make_async_remote_copy(
                    src_ref=stage.at[kind, to_x * 4 + quarter(to_y)],
                    dst_ref=data.at[kind, slot_of(y), 1, :, my_rows, :],
                    send_sem=a2a_send.at[kind],
                    recv_sem=a2a_recv.at[kind, slot_of(y)],
                    device_id=device(to_y, r, to_x),
                    device_id_type=MESH,
                ).start()

    def wait_heads(kind, slot):
        whole = data.at[kind, slot, 1]
        pltpu.make_async_copy(whole, whole, a2a_recv.at[kind, slot]).wait()

    def y_copy(kind):
        return pltpu.make_async_remote_copy(
            src_ref=data.at[kind, INNER, 1],
            dst_ref=data.at[kind, BEYOND, 1],
            send_sem=halo_send.at[kind, 6],
            recv_sem=y_recv.at[kind],
            device_id=device(y_partner, r, x),
            device_id_type=MESH,
        )

    def start_rows(copies):
        for side, copy in copies.items():
            at_side(side)(copy.start)

    def sent_rows(copies):
        for side, copy in copies.items():
            at_side(side)(copy.wait_send)

    def came_rows(copies):
        for side, copy in copies.items():
            at_side(2 - side)(copy.wait_recv)

    def r_copies(kind, slot):
        return {
            side: pltpu.make_async_remote_copy(
                src_ref=data.at[kind, slot, 1],
                dst_ref=data.at[kind, slot, 2 - side],
                send_sem=halo_send.at[kind, slot * 2 + side // 2],
                recv_sem=r_recv.at[kind, slot, side // 2],
                device_id=device(y, r_at[side], x),
                device_id_type=MESH,
            )
            for side in (0, 2)
        }

    def spread(kind, slot):
        start_rows(r_copies(kind, slot))

    def forward(kind):
        y_copy(kind).wait_recv()
        spread(kind, BEYOND)

    def wait_rows(kind, slot):
        came_rows(r_copies(kind, slot))

    send_heads(KV, y_far)
    loads[6].wait()
    listed[0:TW, 0:27] = neighbours[...].astype(F32)
    for to_y in y_far:
        pltpu.make_async_remote_copy(
            src_ref=listed, dst_ref=lists.at[y_hi, slot_of(y)],
            send_sem=list_send, recv_sem=list_recv,
            device_id=device(to_y, r, x), device_id_type=MESH,
        ).start()

    loads[5].wait()
    factor = query_scale[...] * HD ** (-0.5)
    loads[2].wait()
    put(QD, 0, (raw[2].astype(F32) * factor).astype(BF16))
    loads[3].wait()
    put(QD, 1, raw[3])

    send_heads(QD, y_far)

    for side in (0, 2):
        @pl.when(r == (rows - 1 if side == 2 else 0))
        def _():
            data[:, :, side] = jnp.zeros((2, 3, 2, SLAB, HD), BF16)
            stats[:, side] = jnp.full((3, 2, 8, SLAB), HIDDEN, F32)

    wait_heads(KV, INNER)
    y_copy(KV).start()
    spread(KV, INNER)
    wait_heads(KV, OUTER)
    spread(KV, OUTER)

    pltpu.make_async_copy(lists, lists, list_recv).wait()
    shape = (BLOCKS * 8, 128)
    line = lax.broadcasted_iota(jnp.int32, shape, 0)
    column = line % 8
    block_of = line // 8
    key_slot = block_of // 3
    key_frame = jnp.where(
        key_slot == 0, frame_of[0], jnp.where(key_slot == 1, frame_of[1], frame_of[2])
    )
    key_row = r + block_of % 3 - 1
    real = (column < TW) & (key_row >= 0) & (key_row < rows)
    ids = jnp.where(real, (key_frame * rows + key_row) * TW + column, -5).astype(F32)
    lane_tile = lax.broadcasted_iota(jnp.int32, (BLOCKS * 8, SLAB), 1) // TILE
    lane = lax.broadcasted_iota(jnp.int32, (8, 128), 1)
    for slot in (OUTER, INNER):
        found = jnp.full((BLOCKS * 8, SLAB), HIDDEN, F32)
        for tile in range(TW):
            hit = jnp.max(
                jnp.where(lists[0, slot, tile : tile + 1, :] == ids, 0.0, HIDDEN),
                axis=1, keepdims=True,
            )
            found = jnp.where(lane_tile == tile, hit, found)
        bias[slot] = found.reshape(BLOCKS, 8, SLAB)
        turned = jnp.concatenate(
            [
                jnp.concatenate(
                    [found[:, tile * TILE : tile * TILE + 1] for tile in range(TW)]
                    + [jnp.full((BLOCKS * 8, 124), HIDDEN, F32)],
                    axis=1,
                ),
                jnp.full((56, 128), HIDDEN, F32),
            ],
            axis=0,
        ).T[:8]
        for key_block in range(BLOCKS):
            for side in range(2):
                at = key_block * 8 + side * 2
                bias_rows[slot, key_block // 3, side, :, pl.ds(key_block % 3 * 128, 128)] = jnp.where(
                    lane < TILE, turned[:, at : at + 1], turned[:, at + 1 : at + 2]
                )

    wait_heads(QD, INNER)
    y_copy(QD).start()
    spread(QD, INNER)
    wait_heads(QD, OUTER)

    def return_heads(kind, slot):
        for to_x in x_at:
            for far_hi in range(2):
                to_y = frame_of[slot] + far_hi * FT
                token_chunk = to_x * 2 + far_hi
                part = pl.ds(pl.multiple_of(token_chunk * chunk, chunk), chunk)
                pltpu.make_async_remote_copy(
                    src_ref=results.at[kind, slot, :, part, :],
                    dst_ref=landed.at[kind, my_head],
                    send_sem=out_send.at[kind],
                    recv_sem=out_recv.at[kind],
                    device_id=device(to_y, r, to_x),
                    device_id_type=MESH,
                ).start()

    def my_scale(scale):
        return scale[:, pl.ds(pl.multiple_of(my_head * HD, HD), HD)]

    def stat_copies(slot):
        return {
            side: pltpu.make_async_remote_copy(
                src_ref=stats_sent.at[slot, side, 0:2],
                dst_ref=stats.at[slot, 2 - side],
                send_sem=stat_send.at[slot, side // 2],
                recv_sem=stat_recv.at[slot, side // 2],
                device_id=device(y, r_at[side], x),
                device_id_type=MESH,
            )
            for side in (0, 2)
        }

    def far_stat_copies():
        return {
            side: pltpu.make_async_remote_copy(
                src_ref=stats_sent.at[INNER, side, BEYOND],
                dst_ref=stats.at[BEYOND, 2 - side, INNER],
                send_sem=far_send.at[side],
                recv_sem=far_recv.at[side],
                device_id=device(y_partner, r_at[side], x),
                device_id_type=MESH,
            )
            for side in range(3)
        }

    def rows_of(kind, slots, which, side):
        return jnp.concatenate(
            [data[kind, slot, row, which, own(side), :] for slot in slots for row in range(3)],
            axis=0,
        )

    def query_side(slot, arrive, between):
        key_slots = PAIR if slot == OUTER else PAIR + (BEYOND,)
        groups = (PAIR,) if slot == OUTER else (PAIR, (BEYOND,))
        parts = [(slots, side) for slots in groups for side in range(2)]
        peak = [jnp.full((3 * TILE, 128), -3e38, F32) for side in range(2)]
        for slots, side in parts:
            if side == 0:
                for key_slot in slots:
                    arrive(key_slot)
            rows_bias = jnp.concatenate(
                [bias_rows[slot, key_slot, side, side : side + 3, :] for key_slot in slots], axis=1
            )
            part = add_rows(
                dot_nt(data[QD, slot, 1, 0, near(side), :], rows_of(KV, slots, 0, side)), rows_bias
            )
            scores[place(slots, side)] = part
            peak[side] = jnp.maximum(peak[side], fold(part, jnp.maximum))
        row_max = jnp.max(join(*peak, jnp.maximum), axis=1, keepdims=True)
        between()

        row_wide = jnp.broadcast_to(row_max, (SLAB, 128))
        totals = [jnp.zeros((3 * TILE, 128), F32) for side in range(2)]
        sums = [jnp.zeros((3 * TILE, HD), F32) for side in range(2)]
        for slots, side in parts:
            part = jnp.exp(scores[place(slots, side)] - wide(row_wide[near(side)], slots))
            low = part.astype(BF16)
            weights[place(slots, side)] = low
            totals[side] = totals[side] + fold(part, jnp.add)
            sums[side] = sums[side] + dot_nn(low, rows_of(KV, slots, 1, side))
        total = jnp.sum(join(*totals, jnp.add), axis=1, keepdims=True)
        inverse = jnp.broadcast_to(1.0 / total, (SLAB, 128))
        attended = (join(*sums, jnp.add) * inverse).astype(BF16)
        results[0, slot, 0] = attended
        grads = data[QD, slot, 1, 1].astype(F32)
        delta = jnp.sum(attended.astype(F32) * grads, axis=1, keepdims=True)
        log_total = row_max + jnp.log(total)
        lane = lax.broadcasted_iota(jnp.int32, (SLAB, 128), 1)
        turned = jnp.where(lane == 0, log_total, delta).T
        log_row, delta_row = turned[0:1], turned[1:2]
        line8 = lax.broadcasted_iota(jnp.int32, (8, SLAB), 0)
        for key_slot in key_slots:
            for row in range(3):
                message = jnp.where(
                    line8 == TW, delta_row, bias[slot, key_slot * 3 + row] - log_row
                )
                if row == 1 and key_slot != BEYOND:
                    stats[slot, 1, key_slot] = message
                else:
                    stats_sent[slot, row, key_slot] = message
        start_rows(stat_copies(slot))
        if slot == INNER:
            start_rows(far_stat_copies())
        delta_part = delta * inverse

        sums = [jnp.zeros((3 * TILE, HD), F32) for side in range(2)]
        for slots, side in parts:
            grad_weights = dot_nt(
                data[QD, slot, 1, 1, near(side), :], rows_of(KV, slots, 1, side)
            )
            part = weights[place(slots, side)].astype(F32) * (
                grad_weights * wide(inverse[near(side)], slots)
                - wide(delta_part[near(side)], slots)
            )
            sums[side] = sums[side] + dot_nn(part.astype(BF16), rows_of(KV, slots, 0, side))
        scale = my_scale(query_scale) * HD ** (-0.5)
        results[0, slot, 1] = (join(*sums, jnp.add) * scale).astype(BF16)
        return_heads(0, slot)

    def key_side(slot, arrive):
        groups = (PAIR,) if slot == OUTER else (PAIR, (BEYOND,))
        key_sums = [jnp.zeros((3 * TILE, HD), F32) for side in range(2)]
        value_sums = [jnp.zeros((3 * TILE, HD), F32) for side in range(2)]
        for slots in groups:
            for query_slot in slots:
                arrive(query_slot)
            for side in range(2):
                message = jnp.concatenate(
                    [
                        stats[query_slot, row, slot, :, own(side)]
                        for query_slot in slots for row in range(3)
                    ],
                    axis=1,
                )
                queries = rows_of(QD, slots, 0, side)
                grads = rows_of(QD, slots, 1, side)
                part = jnp.exp(add_rows(
                    dot_nt(data[KV, slot, 1, 0, near(side), :], queries),
                    message[side : side + 3],
                ))
                grad_weights = dot_nt(data[KV, slot, 1, 1, near(side), :], grads)
                slopes = (part * (grad_weights - message[TW : TW + 1])).astype(BF16)
                value_sums[side] = value_sums[side] + dot_nn(part.astype(BF16), grads)
                key_sums[side] = key_sums[side] + dot_nn(slopes, queries)
        grad_keys = join(*key_sums, jnp.add)
        results[1, slot, 0] = (grad_keys * my_scale(key_scale)).astype(BF16)
        results[1, slot, 1] = join(*value_sums, jnp.add).astype(BF16)
        return_heads(1, slot)

    def beyond_arrives(key_slot):
        if key_slot == BEYOND:
            wait_rows(KV, BEYOND)

    def pair_arrives(query_slot):
        wait_rows(QD, query_slot)
        came_rows(stat_copies(query_slot))

    def beyond_queries_arrive(query_slot):
        if query_slot == BEYOND:
            wait_rows(QD, BEYOND)
            came_rows(far_stat_copies())

    def forward_first():
        forward(KV)
        spread(QD, OUTER)

    query_side(OUTER, lambda key_slot: wait_rows(KV, key_slot), forward_first)
    query_side(INNER, beyond_arrives, lambda: forward(QD))
    key_side(OUTER, pair_arrives)
    key_side(INNER, beyond_queries_arrive)

    for kind in range(2):
        pltpu.make_async_copy(landed.at[kind], landed.at[kind], out_recv.at[kind]).wait()
    sent = lists.at[0:2]
    pltpu.make_async_copy(sent, sent, list_send).wait()
    for kind in range(2):
        sent = stage.at[kind]
        pltpu.make_async_copy(sent, sent, a2a_send.at[kind]).wait()
        for slot in range(3):
            sent_rows(r_copies(kind, slot))
        y_copy(kind).wait_send()
        sent = results.at[kind]
        pltpu.make_async_copy(sent, sent, out_send.at[kind]).wait()
    for slot in (OUTER, INNER):
        sent_rows(stat_copies(slot))
    sent_rows(far_stat_copies())


def hand_out(landed, attention, grad_query, grad_key, grad_value, pieces, held, sems):
    targets = (attention, grad_query, grad_key, grad_value)
    loads = [
        pltpu.make_async_copy(landed.at[kind], pieces.at[kind], sems.at[0, kind])
        for kind in range(2)
    ]
    stores = [pltpu.make_async_copy(held.at[i], targets[i], sems.at[1, i]) for i in range(4)]
    for load in loads:
        load.start()
    for i in range(4):
        if i % 2 == 0:
            loads[i // 2].wait()
        for head in range(landed.shape[1]):
            held[i, :, head * HD : (head + 1) * HD] = pieces[i // 2, head, i % 2]
        stores[i].start()
    for store in stores:
        store.wait()


def local(query, key, value, grad_out, query_scale, key_scale, neighbours):
    rows = lax.axis_size("slab") // FT
    columns = lax.axis_size("head") // 2
    chunk, width = query.shape
    out = jax.ShapeDtypeStruct((chunk, width), BF16)
    landing = (2, width // HD, 2, chunk, HD)
    hbm = pl.BlockSpec(memory_space=pltpu.HBM)
    dma = pltpu.SemaphoreType.DMA
    landed = pl.pallas_call(
        functools.partial(kernel, rows, columns),
        out_shape=jax.ShapeDtypeStruct(landing, BF16),
        in_specs=[hbm] * 7,
        out_specs=hbm,
        scratch_shapes=[
            pltpu.VMEM((4, chunk, width), BF16),
            pltpu.VMEM((1, width), F32),
            pltpu.VMEM((1, width), F32),
            pltpu.VMEM(neighbours.shape, jnp.int32),
            pltpu.VMEM((2, 4 * columns, 2, chunk, HD), BF16),
            pltpu.VMEM((2, 3, 3, 2, SLAB, HD), BF16),
            pltpu.VMEM((8, 128), F32),
            pltpu.VMEM((2, 2, 8, 128), F32),
            pltpu.VMEM((2, BLOCKS, 8, SLAB), F32),
            pltpu.VMEM((2, 3, 2, 8, 3 * 128), F32),
            pltpu.VMEM((2, 3 * TILE, 9 * 128), F32),
            pltpu.VMEM((2, 3 * TILE, 9 * 128), BF16),
            pltpu.VMEM((3, 3, 2, 8, SLAB), F32),
            pltpu.VMEM((2, 3, 3, 8, SLAB), F32),
            pltpu.VMEM((2, 2, 2, SLAB, HD), BF16),
            dma((7,)),
            dma((2,)),
            dma((2, 2)),
            dma,
            dma,
            dma((2, 7)),
            dma((2,)),
            dma((2, 3, 2)),
            dma((2, 2)),
            dma((2, 2)),
            dma((3,)),
            dma((3,)),
            dma((2,)),
            dma((2,)),
        ],
        compiler_params=pltpu.CompilerParams(
            collective_id=0, has_side_effects=True, vmem_limit_bytes=VMEM_BYTES
        ),
        name="tiles",
    )(
        query, key, value, grad_out,
        query_scale.reshape(1, width), key_scale.reshape(1, width), neighbours,
    )
    return pl.pallas_call(
        hand_out,
        out_shape=(out,) * 4,
        in_specs=[hbm],
        out_specs=(hbm,) * 4,
        scratch_shapes=[
            pltpu.VMEM(landing, BF16), pltpu.VMEM((4, chunk, width), BF16), dma((2, 4)),
        ],
        compiler_params=pltpu.CompilerParams(vmem_limit_bytes=VMEM_BYTES),
        name="hand_out",
    )(landed)


def solution(mesh):
    token = P(("slab", "head"), None)
    return jax.shard_map(
        local,
        mesh=mesh,
        in_specs=(token, token, token, token, P(), P(), P("slab", None)),
        out_specs=(token,) * 4,
        check_vma=False,
    )
```

```python
import functools

import jax
import jax.numpy as jnp
from jax import lax
from jax.experimental import pallas as pl
from jax.experimental.pallas import tpu as pltpu
from jax.sharding import PartitionSpec as P

HD = 128
TILE = 64
FT = 4
TW = 4
SLAB = TILE * TW
RING = 2 * FT
BLOCKS = 9
OUTER, INNER, BEYOND = 0, 1, 2
HIDDEN = -1e30
MESH = pl.DeviceIdType.MESH
BF16 = jnp.bfloat16
F32 = jnp.float32
KEY, VALUE, QUERY, GRAD = range(4)
KV, QD = range(2)
ARRAYS = (pl.ds(0, 2), pl.ds(2, 2))
VMEM_BYTES = 58 * 1024 * 1024


def dot_nn(a, b):
    return lax.dot_general(a, b, (((1,), (0,)), ((), ())), preferred_element_type=F32)


def dot_nt(a, b):
    return lax.dot_general(a, b, (((1,), (1,)), ((), ())), preferred_element_type=F32)


def dot_tn(a, b):
    return lax.dot_general(a, b, (((0,), (0,)), ((), ())), preferred_element_type=F32)


def add_rows(scores, rows):
    shaped = scores.reshape(3, TILE, scores.shape[1]) + rows[:, None, :]
    return shaped.reshape(scores.shape)


def join(low, high, both):
    return jnp.concatenate(
        [low[:TILE], both(low[TILE:], high[: 2 * TILE]), high[2 * TILE :]], axis=0
    )


def fold(array, both):
    return both(both(array[:, :128], array[:, 128:256]), array[:, 256:])


def wide(column):
    return jnp.concatenate([column] * 3, axis=1)


def near(half):
    return slice(half * TILE, half * TILE + 3 * TILE)


def own(half):
    return slice(half * 2 * TILE, (half + 1) * 2 * TILE)


def kernel(
    rows, columns,
    query, key, value, grad_out, query_scale_in, key_scale_in, neighbours_in, landed,
    raw, query_scale, key_scale, neighbours,
    stage, data, listed, lists, bias, bias_rows, scores, weights, inverses, log_totals, kept, key_sums,
    stats, stats_sent, results,
    in_sem, a2a_send, a2a_recv, list_send, list_recv, halo_send, y_recv, r_recv,
    stat_send, stat_recv, far_send, far_recv, out_send, out_recv,
):
    loads = [
        pltpu.make_async_copy(source, target, in_sem.at[i])
        for i, (source, target) in enumerate((
            (key, raw.at[0]), (value, raw.at[1]), (query, raw.at[2]), (grad_out, raw.at[3]),
            (key_scale_in, key_scale), (query_scale_in, query_scale),
            (neighbours_in, neighbours),
        ))
    ]
    for load in (loads[4], *loads[:4], *loads[5:]):
        load.start()

    slab = lax.axis_index("slab")
    head = lax.axis_index("head")
    y_lo, r = slab // rows, slab % rows
    x, y_hi = head // 2, head % 2
    y = y_hi * FT + y_lo
    chunk = SLAB // (2 * columns)
    half = 1 - y_lo // 2
    far_y = (1 - y_lo // 2) * 2
    y_far = (far_y, far_y + 1, far_y + FT, far_y + FT + 1)
    frame_of = (3 * half, 1 + half, 2 - half)

    def quarter(at_y):
        return ((at_y + RING - 1) % RING) // 2

    def slot_of(at_y):
        return ((at_y % FT + 1) % FT) // 2

    my_head = x * 4 + quarter(y)
    y_partner = (y + RING - 1 + 2 * (y % 2)) % RING

    def device(to_y, to_r, to_x):
        return {"slab": (to_y % FT) * rows + to_r, "head": to_x * 2 + to_y // FT}

    r_at = ((r + rows - 1) % rows, r, (r + 1) % rows)
    x_at = tuple((x + step) % columns for step in range(columns))

    def at_side(side):
        return pl.when(r < rows - 1) if side == 2 else pl.when(r >= 1 - side)

    barrier = pltpu.get_barrier_semaphore()

    def greet(peers):
        for peer in peers:
            pl.semaphore_signal(barrier, 1, device_id=peer, device_id_type=MESH)

    greet([device(to_y, r, to_x) for to_y in y_far for to_x in x_at])
    greet([device(y_partner, r, x)])
    for side in (0, 2):
        @at_side(side)
        def _():
            greet([device(y, r_at[side], x), device(y_partner, r_at[side], x)])

    listed[...] = jnp.full(listed.shape, -2.0, F32)

    def put(which, array):
        for piece in range(4 * columns):
            stage[which, piece] = array[:, piece * HD : (piece + 1) * HD]

    loads[4].wait()
    loads[0].wait()
    put(KEY, (raw[0].astype(F32) * key_scale[...]).astype(BF16))
    loads[1].wait()
    put(VALUE, raw[1])
    row_sides = (r + rows - 1) // rows + (2 * rows - 2 - r) // rows
    pl.semaphore_wait(barrier, 4 * columns + 1 + 2 * row_sides)

    my_rows = pl.ds(pl.multiple_of(head * chunk, chunk), chunk)

    def send_heads(kind, places):
        for to_x in x_at:
            for to_y in places:
                pltpu.make_async_remote_copy(
                    src_ref=stage.at[ARRAYS[kind], to_x * 4 + quarter(to_y)],
                    dst_ref=data.at[ARRAYS[kind], slot_of(y), 1, my_rows, :],
                    send_sem=a2a_send.at[kind],
                    recv_sem=a2a_recv.at[kind, slot_of(y)],
                    device_id=device(to_y, r, to_x),
                    device_id_type=MESH,
                ).start()

    def wait_heads(kind, slot):
        whole = data.at[ARRAYS[kind], slot, 1]
        pltpu.make_async_copy(whole, whole, a2a_recv.at[kind, slot]).wait()

    def y_copy(kind):
        return pltpu.make_async_remote_copy(
            src_ref=data.at[ARRAYS[kind], INNER, 1],
            dst_ref=data.at[ARRAYS[kind], BEYOND, 1],
            send_sem=halo_send.at[kind, 6],
            recv_sem=y_recv.at[kind],
            device_id=device(y_partner, r, x),
            device_id_type=MESH,
        )

    def start_rows(copies):
        for side, copy in copies.items():
            at_side(side)(copy.start)

    def sent_rows(copies):
        for side, copy in copies.items():
            at_side(side)(copy.wait_send)

    def came_rows(copies):
        for side, copy in copies.items():
            at_side(2 - side)(copy.wait_recv)

    def r_copies(kind, slot):
        return {
            side: pltpu.make_async_remote_copy(
                src_ref=data.at[ARRAYS[kind], slot, 1],
                dst_ref=data.at[ARRAYS[kind], slot, 2 - side],
                send_sem=halo_send.at[kind, slot * 2 + side // 2],
                recv_sem=r_recv.at[kind, slot, side // 2],
                device_id=device(y, r_at[side], x),
                device_id_type=MESH,
            )
            for side in (0, 2)
        }

    def spread(kind, slot):
        start_rows(r_copies(kind, slot))

    def forward(kind):
        y_copy(kind).wait_recv()
        spread(kind, BEYOND)

    def wait_rows(kind, slot):
        came_rows(r_copies(kind, slot))

    send_heads(KV, y_far)
    loads[6].wait()
    listed[0:TW, 0:27] = neighbours[...].astype(F32)
    for to_y in y_far:
        pltpu.make_async_remote_copy(
            src_ref=listed, dst_ref=lists.at[y_hi, slot_of(y)],
            send_sem=list_send, recv_sem=list_recv,
            device_id=device(to_y, r, x), device_id_type=MESH,
        ).start()

    loads[5].wait()
    factor = query_scale[...] * HD ** (-0.5)
    loads[2].wait()
    put(QUERY, (raw[2].astype(F32) * factor).astype(BF16))
    loads[3].wait()
    put(GRAD, raw[3])
    send_heads(QD, y_far)

    for side in (0, 2):
        @pl.when(r == (rows - 1 if side == 2 else 0))
        def _():
            data[:, :, side] = jnp.zeros((4, 3, SLAB, HD), BF16)
            stats[:, side] = jnp.full((3, 2, 8, SLAB), HIDDEN, F32)

    wait_heads(KV, INNER)
    y_copy(KV).start()
    spread(KV, INNER)
    wait_heads(KV, OUTER)
    spread(KV, OUTER)

    pltpu.make_async_copy(lists, lists, list_recv).wait()
    shape = (BLOCKS * 8, 128)
    line = lax.broadcasted_iota(jnp.int32, shape, 0)
    column = line % 8
    block_of = line // 8
    key_slot = block_of // 3
    key_frame = jnp.where(
        key_slot == 0, frame_of[0], jnp.where(key_slot == 1, frame_of[1], frame_of[2])
    )
    key_row = r + block_of % 3 - 1
    real = (column < TW) & (key_row >= 0) & (key_row < rows)
    ids = jnp.where(real, (key_frame * rows + key_row) * TW + column, -5).astype(F32)
    lane_tile = lax.broadcasted_iota(jnp.int32, (BLOCKS * 8, SLAB), 1) // TILE
    lane = lax.broadcasted_iota(jnp.int32, (8, 128), 1)
    for slot in (OUTER, INNER):
        found = jnp.full((BLOCKS * 8, SLAB), HIDDEN, F32)
        for tile in range(TW):
            hit = jnp.max(
                jnp.where(lists[0, slot, tile : tile + 1, :] == ids, 0.0, HIDDEN),
                axis=1, keepdims=True,
            )
            found = jnp.where(lane_tile == tile, hit, found)
        bias[slot] = found.reshape(BLOCKS, 8, SLAB)
        turned = jnp.concatenate(
            [
                jnp.concatenate(
                    [found[:, tile * TILE : tile * TILE + 1] for tile in range(TW)]
                    + [jnp.full((BLOCKS * 8, 124), HIDDEN, F32)],
                    axis=1,
                ),
                jnp.full((56, 128), HIDDEN, F32),
            ],
            axis=0,
        ).T[:8]
        for key_block in range(BLOCKS):
            for side in range(2):
                at = key_block * 8 + side * 2
                bias_rows[slot, key_block // 3, side, :, pl.ds(key_block % 3 * 128, 128)] = jnp.where(
                    lane < TILE, turned[:, at : at + 1], turned[:, at + 1 : at + 2]
                )

    wait_heads(QD, INNER)
    y_copy(QD).start()
    wait_heads(QD, OUTER)
    spread(QD, OUTER)

    def return_heads(kind, slot):
        for to_x in x_at:
            for far_hi in range(2):
                to_y = frame_of[slot] + far_hi * FT
                token_chunk = to_x * 2 + far_hi
                part = pl.ds(pl.multiple_of(token_chunk * chunk, chunk), chunk)
                pltpu.make_async_remote_copy(
                    src_ref=results.at[kind, slot, :, part, :],
                    dst_ref=landed.at[kind, my_head],
                    send_sem=out_send.at[kind],
                    recv_sem=out_recv.at[kind],
                    device_id=device(to_y, r, to_x),
                    device_id_type=MESH,
                ).start()

    def my_scale(scale):
        return scale[:, pl.ds(pl.multiple_of(my_head * HD, HD), HD)]

    def stat_copies(slot):
        return {
            side: pltpu.make_async_remote_copy(
                src_ref=stats_sent.at[slot, side, 0:2],
                dst_ref=stats.at[slot, 2 - side],
                send_sem=stat_send.at[slot, side // 2],
                recv_sem=stat_recv.at[slot, side // 2],
                device_id=device(y, r_at[side], x),
                device_id_type=MESH,
            )
            for side in (0, 2)
        }

    def far_stat_copies():
        return {
            side: pltpu.make_async_remote_copy(
                src_ref=stats_sent.at[INNER, side, BEYOND],
                dst_ref=stats.at[BEYOND, 2 - side, INNER],
                send_sem=far_send.at[side],
                recv_sem=far_recv.at[side],
                device_id=device(y_partner, r_at[side], x),
                device_id_type=MESH,
            )
            for side in range(3)
        }

    def rows_of(array, slot, side):
        return jnp.concatenate(
            [data[array, slot, row, own(side), :] for row in range(3)], axis=0
        )

    def attend(slot, key_slots, arrive, least, between):
        parts = [(key_slot, side) for key_slot in key_slots for side in range(2)]
        peak = [jnp.full((3 * TILE, 128), -3e38, F32) for side in range(2)]
        for key_slot, side in parts:
            if side == 0:
                arrive(key_slot)
            part = add_rows(
                dot_nt(data[QUERY, slot, 1, near(side), :], rows_of(KEY, key_slot, side)),
                bias_rows[slot, key_slot, side, side : side + 3, :],
            )
            scores[key_slot, side] = part
            peak[side] = jnp.maximum(peak[side], fold(part, jnp.maximum))
        row_max = jnp.max(join(*peak, jnp.maximum), axis=1, keepdims=True)
        between()
        row_wide = jnp.maximum(jnp.broadcast_to(row_max, (SLAB, 128)), least)
        totals = [jnp.zeros((3 * TILE, 128), F32) for side in range(2)]
        sums = [jnp.zeros((3 * TILE, HD), F32) for side in range(2)]
        for key_slot, side in parts:
            part = jnp.exp(scores[key_slot, side] - wide(row_wide[near(side)]))
            low = part.astype(BF16)
            weights[slot, key_slot, side] = low
            totals[side] = totals[side] + fold(part, jnp.add)
            sums[side] = sums[side] + dot_nn(low, rows_of(VALUE, key_slot, side))
        total = jnp.sum(join(*totals, jnp.add), axis=1, keepdims=True)
        return row_wide, jnp.broadcast_to(total, (SLAB, 128)), join(*sums, jnp.add)

    def settle(slot, row_wide, total, summed, earlier):
        inverse = 1.0 / total
        results[0, slot, 0] = (summed * inverse).astype(BF16)
        inverses[slot, 0] = inverse * earlier
        inverses[slot, 1] = inverse
        log_totals[slot] = row_wide + jnp.log(total)

    def tell(slot):
        grads = data[GRAD, slot, 1].astype(F32)
        delta = jnp.sum(results[0, slot, 0].astype(F32) * grads, axis=1, keepdims=True)
        lane = lax.broadcasted_iota(jnp.int32, (SLAB, 128), 1)
        turned = jnp.where(lane == 0, log_totals[slot], delta).T
        log_row, delta_row = turned[0:1], turned[1:2]
        line8 = lax.broadcasted_iota(jnp.int32, (8, SLAB), 0)
        for key_slot in (OUTER, INNER) if slot == OUTER else (OUTER, INNER, BEYOND):
            for row in range(3):
                message = jnp.where(
                    line8 == TW, delta_row, bias[slot, key_slot * 3 + row] - log_row
                )
                if row == 1 and key_slot != BEYOND:
                    stats[slot, 1, key_slot] = message
                else:
                    stats_sent[slot, row, key_slot] = message
        start_rows(stat_copies(slot))
        if slot == INNER:
            start_rows(far_stat_copies())
        return delta

    def query_side(slot, delta):
        sums = [jnp.zeros((3 * TILE, HD), F32) for side in range(2)]
        for key_slot in (INNER, OUTER) if slot == OUTER else (INNER, OUTER, BEYOND):
            inverse = inverses[slot, 1 if key_slot == BEYOND else 0]
            delta_part = delta * inverse
            for side in range(2):
                grad_weights = dot_nt(
                    data[GRAD, slot, 1, near(side), :], rows_of(VALUE, key_slot, side)
                )
                part = weights[slot, key_slot, side].astype(F32) * (
                    grad_weights * wide(inverse[near(side)]) - wide(delta_part[near(side)])
                )
                sums[side] = sums[side] + dot_nn(
                    part.astype(BF16), rows_of(KEY, key_slot, side)
                )
        scale = my_scale(query_scale) * HD ** (-0.5)
        results[0, slot, 1] = (join(*sums, jnp.add) * scale).astype(BF16)
        return_heads(0, slot)

    def key_part(slot, query_slot):
        for side in range(2):
            message = jnp.concatenate(
                [stats[query_slot, row, slot, :, own(side)] for row in range(3)], axis=1
            )
            queries = rows_of(QUERY, query_slot, side)
            grads = rows_of(GRAD, query_slot, side)
            part = jnp.exp(add_rows(
                dot_nt(data[KEY, slot, 1, near(side), :], queries), message[side : side + 3]
            ))
            grad_weights = dot_nt(data[VALUE, slot, 1, near(side), :], grads)
            slopes = (part * (grad_weights - message[TW : TW + 1])).astype(BF16)
            for which, term in (
                (0, dot_nn(slopes, queries)), (1, dot_nn(part.astype(BF16), grads))
            ):
                if query_slot == OUTER:
                    key_sums[slot, which, side] = term
                else:
                    key_sums[slot, which, side] += term

    def key_end(slot):
        grad_keys = join(key_sums[slot, 0, 0], key_sums[slot, 0, 1], jnp.add)
        grad_values = join(key_sums[slot, 1, 0], key_sums[slot, 1, 1], jnp.add)
        results[1, slot, 0] = (grad_keys * my_scale(key_scale)).astype(BF16)
        results[1, slot, 1] = grad_values.astype(BF16)
        return_heads(1, slot)

    def queries_arrive(slot):
        wait_rows(QD, slot)
        came_rows(far_stat_copies() if slot == BEYOND else stat_copies(slot))

    def after_outer_scores():
        forward(KV)
        spread(QD, INNER)

    lowest = jnp.full((SLAB, 128), -3e38, F32)
    outer = attend(
        OUTER, (INNER, OUTER), lambda key_slot: wait_rows(KV, key_slot), lowest, after_outer_scores
    )
    settle(OUTER, *outer, 1.0)
    query_side(OUTER, tell(OUTER))
    first = attend(INNER, (INNER, OUTER), lambda key_slot: None, lowest, lambda: None)
    for i in range(3):
        kept[i] = first[i]
    forward(QD)
    row_wide, total, summed = attend(
        INNER, (BEYOND,), lambda key_slot: wait_rows(KV, key_slot), kept[0], lambda: None
    )
    earlier = jnp.exp(kept[0] - row_wide)
    settle(INNER, row_wide, total + kept[1] * earlier, summed + kept[2] * earlier, earlier)
    query_side(INNER, tell(INNER))
    queries_arrive(OUTER)
    key_part(OUTER, OUTER)
    key_part(INNER, OUTER)
    queries_arrive(INNER)
    key_part(OUTER, INNER)
    key_end(OUTER)
    key_part(INNER, INNER)
    queries_arrive(BEYOND)
    key_part(INNER, BEYOND)
    key_end(INNER)

    for kind in range(2):
        pltpu.make_async_copy(landed.at[kind], landed.at[kind], out_recv.at[kind]).wait()
    sent = lists.at[0:2]
    pltpu.make_async_copy(sent, sent, list_send).wait()
    for kind in (KV, QD):
        sent = stage.at[ARRAYS[kind]]
        pltpu.make_async_copy(sent, sent, a2a_send.at[kind]).wait()
        for slot in range(3):
            sent_rows(r_copies(kind, slot))
        y_copy(kind).wait_send()
    for kind in range(2):
        sent = results.at[kind]
        pltpu.make_async_copy(sent, sent, out_send.at[kind]).wait()
    for slot in (OUTER, INNER):
        sent_rows(stat_copies(slot))
    sent_rows(far_stat_copies())


def hand_out(landed, attention, grad_query, grad_key, grad_value, pieces, held, sems):
    targets = (attention, grad_query, grad_key, grad_value)
    loads = [
        pltpu.make_async_copy(landed.at[kind], pieces.at[kind], sems.at[0, kind])
        for kind in range(2)
    ]
    stores = [pltpu.make_async_copy(held.at[i], targets[i], sems.at[1, i]) for i in range(4)]
    for load in loads:
        load.start()
    for i in range(4):
        if i % 2 == 0:
            loads[i // 2].wait()
        for head in range(landed.shape[1]):
            held[i, :, head * HD : (head + 1) * HD] = pieces[i // 2, head, i % 2]
        stores[i].start()
    for store in stores:
        store.wait()


def local(query, key, value, grad_out, query_scale, key_scale, neighbours):
    rows = lax.axis_size("slab") // FT
    columns = lax.axis_size("head") // 2
    chunk, width = query.shape
    out = jax.ShapeDtypeStruct((chunk, width), BF16)
    landing = (2, width // HD, 2, chunk, HD)
    hbm = pl.BlockSpec(memory_space=pltpu.HBM)
    dma = pltpu.SemaphoreType.DMA
    landed = pl.pallas_call(
        functools.partial(kernel, rows, columns),
        out_shape=jax.ShapeDtypeStruct(landing, BF16),
        in_specs=[hbm] * 7,
        out_specs=hbm,
        scratch_shapes=[
            pltpu.VMEM((4, chunk, width), BF16),
            pltpu.VMEM((1, width), F32),
            pltpu.VMEM((1, width), F32),
            pltpu.VMEM(neighbours.shape, jnp.int32),
            pltpu.VMEM((4, 4 * columns, chunk, HD), BF16),
            pltpu.VMEM((4, 3, 3, SLAB, HD), BF16),
            pltpu.VMEM((8, 128), F32),
            pltpu.VMEM((2, 2, 8, 128), F32),
            pltpu.VMEM((2, BLOCKS, 8, SLAB), F32),
            pltpu.VMEM((2, 3, 2, 8, 3 * 128), F32),
            pltpu.VMEM((3, 2, 3 * TILE, 3 * 128), F32),
            pltpu.VMEM((2, 3, 2, 3 * TILE, 3 * 128), BF16),
            pltpu.VMEM((2, 2, SLAB, 128), F32),
            pltpu.VMEM((2, SLAB, 128), F32),
            pltpu.VMEM((3, SLAB, 128), F32),
            pltpu.VMEM((2, 2, 2, 3 * TILE, HD), F32),
            pltpu.VMEM((3, 3, 2, 8, SLAB), F32),
            pltpu.VMEM((2, 3, 3, 8, SLAB), F32),
            pltpu.VMEM((2, 2, 2, SLAB, HD), BF16),
            dma((7,)),
            dma((2,)),
            dma((2, 2)),
            dma,
            dma,
            dma((2, 7)),
            dma((2,)),
            dma((2, 3, 2)),
            dma((2, 2)),
            dma((2, 2)),
            dma((3,)),
            dma((3,)),
            dma((2,)),
            dma((2,)),
        ],
        compiler_params=pltpu.CompilerParams(
            collective_id=0, has_side_effects=True, vmem_limit_bytes=VMEM_BYTES
        ),
        name="tiles",
    )(
        query, key, value, grad_out,
        query_scale.reshape(1, width), key_scale.reshape(1, width), neighbours,
    )
    return pl.pallas_call(
        hand_out,
        out_shape=(out,) * 4,
        in_specs=[hbm],
        out_specs=(hbm,) * 4,
        scratch_shapes=[
            pltpu.VMEM(landing, BF16), pltpu.VMEM((4, chunk, width), BF16), dma((2, 4)),
        ],
        compiler_params=pltpu.CompilerParams(vmem_limit_bytes=VMEM_BYTES),
        name="hand_out",
    )(landed)


def solution(mesh):
    token = P(("slab", "head"), None)
    return jax.shard_map(
        local,
        mesh=mesh,
        in_specs=(token, token, token, token, P(), P(), P("slab", None)),
        out_specs=(token,) * 4,
        check_vma=False,
    )
```

```python
import functools

import jax
import jax.numpy as jnp
from jax import lax
from jax.experimental import pallas as pl
from jax.experimental.pallas import tpu as pltpu
from jax.sharding import PartitionSpec as P

HD = 128
TILE = 64
FT = 4
TW = 4
SLAB = TILE * TW
RING = 2 * FT
BLOCKS = 9
OUTER, INNER, BEYOND = 0, 1, 2
HIDDEN = -1e30
MESH = pl.DeviceIdType.MESH
BF16 = jnp.bfloat16
F32 = jnp.float32
KEY, VALUE, QUERY, GRAD = range(4)
KV, QD = range(2)
ARRAYS = (pl.ds(0, 2), pl.ds(2, 2))
VMEM_BYTES = 58 * 1024 * 1024


def dot_nn(a, b):
    return lax.dot_general(a, b, (((1,), (0,)), ((), ())), preferred_element_type=F32)


def dot_nt(a, b):
    return lax.dot_general(a, b, (((1,), (1,)), ((), ())), preferred_element_type=F32)


def dot_tn(a, b):
    return lax.dot_general(a, b, (((0,), (0,)), ((), ())), preferred_element_type=F32)


def add_rows(scores, rows):
    shaped = scores.reshape(3, TILE, scores.shape[1]) + rows[:, None, :]
    return shaped.reshape(scores.shape)


def join(low, high, both):
    return jnp.concatenate(
        [low[:TILE], both(low[TILE:], high[: 2 * TILE]), high[2 * TILE :]], axis=0
    )


def fold(array, both):
    return both(both(array[:, :128], array[:, 128:256]), array[:, 256:])


def wide(column):
    return jnp.concatenate([column] * 3, axis=1)


def near(half):
    return slice(half * TILE, half * TILE + 3 * TILE)


def own(half):
    return slice(half * 2 * TILE, (half + 1) * 2 * TILE)


def kernel(
    rows, columns,
    query, key, value, grad_out, query_scale_in, key_scale_in, neighbours_in, landed,
    raw, query_scale, key_scale, neighbours,
    stage, data, listed, lists, bias, bias_rows, scores, weights, inverses, log_totals, kept, key_sums,
    stats, stats_sent, results,
    in_sem, a2a_send, a2a_recv, list_send, list_recv, halo_send, y_recv, r_recv,
    stat_send, stat_recv, far_send, far_recv, out_send, out_recv,
):
    loads = [
        pltpu.make_async_copy(source, target, in_sem.at[i])
        for i, (source, target) in enumerate((
            (key, raw.at[0]), (value, raw.at[1]), (query, raw.at[2]), (grad_out, raw.at[3]),
            (key_scale_in, key_scale), (query_scale_in, query_scale),
            (neighbours_in, neighbours),
        ))
    ]
    for load in (loads[4], *loads[:2]):
        load.start()

    slab = lax.axis_index("slab")
    head = lax.axis_index("head")
    y_lo, r = slab // rows, slab % rows
    x, y_hi = head // 2, head % 2
    y = y_hi * FT + y_lo
    chunk = SLAB // (2 * columns)
    half = 1 - y_lo // 2
    far_y = (1 - y_lo // 2) * 2
    y_far = (far_y, far_y + 1, far_y + FT, far_y + FT + 1)
    frame_of = (3 * half, 1 + half, 2 - half)

    def quarter(at_y):
        return ((at_y + RING - 1) % RING) // 2

    def slot_of(at_y):
        return ((at_y % FT + 1) % FT) // 2

    my_head = x * 4 + quarter(y)
    y_partner = (y + RING - 1 + 2 * (y % 2)) % RING

    def device(to_y, to_r, to_x):
        return {"slab": (to_y % FT) * rows + to_r, "head": to_x * 2 + to_y // FT}

    r_at = ((r + rows - 1) % rows, r, (r + 1) % rows)
    x_at = tuple((x + step) % columns for step in range(columns))

    def at_side(side):
        return pl.when(r < rows - 1) if side == 2 else pl.when(r >= 1 - side)

    barrier = pltpu.get_barrier_semaphore()

    def greet(peers):
        for peer in peers:
            pl.semaphore_signal(barrier, 1, device_id=peer, device_id_type=MESH)

    greet([device(to_y, r, to_x) for to_y in y_far for to_x in x_at])
    greet([device(y_partner, r, x)])
    for side in (0, 2):
        @at_side(side)
        def _():
            greet([device(y, r_at[side], x), device(y_partner, r_at[side], x)])

    for load in (*loads[2:4], *loads[5:]):
        load.start()
    listed[...] = jnp.full(listed.shape, -2.0, F32)

    def put(which, array):
        for piece in range(4 * columns):
            stage[which, piece] = array[:, piece * HD : (piece + 1) * HD]

    loads[4].wait()
    loads[0].wait()
    put(KEY, (raw[0].astype(F32) * key_scale[...]).astype(BF16))
    loads[1].wait()
    put(VALUE, raw[1])
    row_sides = (r + rows - 1) // rows + (2 * rows - 2 - r) // rows
    pl.semaphore_wait(barrier, 4 * columns + 1 + 2 * row_sides)

    my_rows = pl.ds(pl.multiple_of(head * chunk, chunk), chunk)

    def send_heads(kind, places):
        for to_x in x_at:
            for to_y in places:
                pltpu.make_async_remote_copy(
                    src_ref=stage.at[ARRAYS[kind], to_x * 4 + quarter(to_y)],
                    dst_ref=data.at[ARRAYS[kind], slot_of(y), 1, my_rows, :],
                    send_sem=a2a_send.at[kind],
                    recv_sem=a2a_recv.at[kind, slot_of(y)],
                    device_id=device(to_y, r, to_x),
                    device_id_type=MESH,
                ).start()

    def wait_heads(kind, slot):
        whole = data.at[ARRAYS[kind], slot, 1]
        pltpu.make_async_copy(whole, whole, a2a_recv.at[kind, slot]).wait()

    def y_copy(kind):
        return pltpu.make_async_remote_copy(
            src_ref=data.at[ARRAYS[kind], INNER, 1],
            dst_ref=data.at[ARRAYS[kind], BEYOND, 1],
            send_sem=halo_send.at[kind, 6],
            recv_sem=y_recv.at[kind],
            device_id=device(y_partner, r, x),
            device_id_type=MESH,
        )

    def start_rows(copies):
        if 1 in copies:
            copies[1].start()
        for side, parity in ((0, 0), (2, 1), (2, 0), (0, 1)):
            exists = r < rows - 1 if side == 2 else r > 0
            pl.when(exists & (r % 2 == parity))(copies[side].start)

    def sent_rows(copies):
        for side, copy in copies.items():
            at_side(side)(copy.wait_send)

    def came_rows(copies):
        for side, copy in copies.items():
            at_side(2 - side)(copy.wait_recv)

    def r_copies(kind, slot):
        return {
            side: pltpu.make_async_remote_copy(
                src_ref=data.at[ARRAYS[kind], slot, 1],
                dst_ref=data.at[ARRAYS[kind], slot, 2 - side],
                send_sem=halo_send.at[kind, slot * 2 + side // 2],
                recv_sem=r_recv.at[kind, slot, side // 2],
                device_id=device(y, r_at[side], x),
                device_id_type=MESH,
            )
            for side in (0, 2)
        }

    def spread(kind, slot):
        start_rows(r_copies(kind, slot))

    def forward(kind):
        y_copy(kind).wait_recv()
        spread(kind, BEYOND)

    def wait_rows(kind, slot):
        came_rows(r_copies(kind, slot))

    send_heads(KV, y_far)
    loads[6].wait()
    listed[0:TW, 0:27] = neighbours[...].astype(F32)
    for to_y in y_far:
        pltpu.make_async_remote_copy(
            src_ref=listed, dst_ref=lists.at[y_hi, slot_of(y)],
            send_sem=list_send, recv_sem=list_recv,
            device_id=device(to_y, r, x), device_id_type=MESH,
        ).start()

    loads[5].wait()
    factor = query_scale[...] * HD ** (-0.5)
    loads[2].wait()
    put(QUERY, (raw[2].astype(F32) * factor).astype(BF16))
    loads[3].wait()
    put(GRAD, raw[3])
    send_heads(QD, y_far)

    for side in (0, 2):
        @pl.when(r == (rows - 1 if side == 2 else 0))
        def _():
            data[:, :, side] = jnp.zeros((4, 3, SLAB, HD), BF16)
            stats[:, side] = jnp.full((3, 2, 8, SLAB), HIDDEN, F32)

    wait_heads(KV, INNER)
    y_copy(KV).start()
    spread(KV, INNER)
    wait_heads(KV, OUTER)
    spread(KV, OUTER)

    pltpu.make_async_copy(lists, lists, list_recv).wait()
    shape = (BLOCKS * 8, 128)
    line = lax.broadcasted_iota(jnp.int32, shape, 0)
    column = line % 8
    block_of = line // 8
    key_slot = block_of // 3
    key_frame = jnp.where(
        key_slot == 0, frame_of[0], jnp.where(key_slot == 1, frame_of[1], frame_of[2])
    )
    key_row = r + block_of % 3 - 1
    real = (column < TW) & (key_row >= 0) & (key_row < rows)
    ids = jnp.where(real, (key_frame * rows + key_row) * TW + column, -5).astype(F32)
    lane_tile = lax.broadcasted_iota(jnp.int32, (BLOCKS * 8, SLAB), 1) // TILE
    lane = lax.broadcasted_iota(jnp.int32, (8, 128), 1)
    for slot in (OUTER, INNER):
        found = jnp.full((BLOCKS * 8, SLAB), HIDDEN, F32)
        for tile in range(TW):
            hit = jnp.max(
                jnp.where(lists[0, slot, tile : tile + 1, :] == ids, 0.0, HIDDEN),
                axis=1, keepdims=True,
            )
            found = jnp.where(lane_tile == tile, hit, found)
        bias[slot] = found.reshape(BLOCKS, 8, SLAB)
        turned = jnp.concatenate(
            [
                jnp.concatenate(
                    [found[:, tile * TILE : tile * TILE + 1] for tile in range(TW)]
                    + [jnp.full((BLOCKS * 8, 124), HIDDEN, F32)],
                    axis=1,
                ),
                jnp.full((56, 128), HIDDEN, F32),
            ],
            axis=0,
        ).T[:8]
        for key_block in range(BLOCKS):
            for side in range(2):
                at = key_block * 8 + side * 2
                bias_rows[slot, key_block // 3, side, :, pl.ds(key_block % 3 * 128, 128)] = jnp.where(
                    lane < TILE, turned[:, at : at + 1], turned[:, at + 1 : at + 2]
                )

    wait_heads(QD, INNER)
    y_copy(QD).start()
    wait_heads(QD, OUTER)

    def return_heads(kind, slot):
        for to_x in x_at:
            for far_hi in range(2):
                to_y = frame_of[slot] + far_hi * FT
                token_chunk = to_x * 2 + far_hi
                part = pl.ds(pl.multiple_of(token_chunk * chunk, chunk), chunk)
                pltpu.make_async_remote_copy(
                    src_ref=results.at[kind, slot, :, part, :],
                    dst_ref=landed.at[kind, my_head],
                    send_sem=out_send.at[kind],
                    recv_sem=out_recv.at[kind],
                    device_id=device(to_y, r, to_x),
                    device_id_type=MESH,
                ).start()

    def my_scale(scale):
        return scale[:, pl.ds(pl.multiple_of(my_head * HD, HD), HD)]

    def stat_copies(slot):
        return {
            side: pltpu.make_async_remote_copy(
                src_ref=stats_sent.at[slot, side, 0:2],
                dst_ref=stats.at[slot, 2 - side],
                send_sem=stat_send.at[slot, side // 2],
                recv_sem=stat_recv.at[slot, side // 2],
                device_id=device(y, r_at[side], x),
                device_id_type=MESH,
            )
            for side in (0, 2)
        }

    def far_stat_copies():
        return {
            side: pltpu.make_async_remote_copy(
                src_ref=stats_sent.at[INNER, side, BEYOND],
                dst_ref=stats.at[BEYOND, 2 - side, INNER],
                send_sem=far_send.at[side],
                recv_sem=far_recv.at[side],
                device_id=device(y_partner, r_at[side], x),
                device_id_type=MESH,
            )
            for side in range(3)
        }

    def rows_of(array, slot, side):
        return jnp.concatenate(
            [data[array, slot, row, own(side), :] for row in range(3)], axis=0
        )

    def attend(slot, key_slots, arrive, least, between):
        parts = [(key_slot, side) for key_slot in key_slots for side in range(2)]
        peak = [jnp.full((3 * TILE, 128), -3e38, F32) for side in range(2)]
        for key_slot, side in parts:
            if side == 0:
                arrive(key_slot)
            part = add_rows(
                dot_nt(data[QUERY, slot, 1, near(side), :], rows_of(KEY, key_slot, side)),
                bias_rows[slot, key_slot, side, side : side + 3, :],
            )
            scores[key_slot, side] = part
            peak[side] = jnp.maximum(peak[side], fold(part, jnp.maximum))
        row_max = jnp.max(join(*peak, jnp.maximum), axis=1, keepdims=True)
        between()
        row_wide = jnp.maximum(jnp.broadcast_to(row_max, (SLAB, 128)), least)
        totals = [jnp.zeros((3 * TILE, 128), F32) for side in range(2)]
        sums = [jnp.zeros((3 * TILE, HD), F32) for side in range(2)]
        for key_slot, side in parts:
            part = jnp.exp(scores[key_slot, side] - wide(row_wide[near(side)]))
            low = part.astype(BF16)
            weights[slot, key_slot, side] = low
            totals[side] = totals[side] + fold(part, jnp.add)
            sums[side] = sums[side] + dot_nn(low, rows_of(VALUE, key_slot, side))
        total = jnp.sum(join(*totals, jnp.add), axis=1, keepdims=True)
        return row_wide, jnp.broadcast_to(total, (SLAB, 128)), join(*sums, jnp.add)

    def settle(slot, row_wide, total, summed, earlier):
        inverse = 1.0 / total
        results[0, slot, 0] = (summed * inverse).astype(BF16)
        inverses[slot, 0] = inverse * earlier
        inverses[slot, 1] = inverse
        log_totals[slot] = row_wide + jnp.log(total)

    def tell(slot):
        grads = data[GRAD, slot, 1].astype(F32)
        delta = jnp.sum(results[0, slot, 0].astype(F32) * grads, axis=1, keepdims=True)
        lane = lax.broadcasted_iota(jnp.int32, (SLAB, 128), 1)
        turned = jnp.where(lane == 0, log_totals[slot], delta).T
        log_row, delta_row = turned[0:1], turned[1:2]
        line8 = lax.broadcasted_iota(jnp.int32, (8, SLAB), 0)
        for key_slot in (OUTER, INNER) if slot == OUTER else (OUTER, INNER, BEYOND):
            for row in range(3):
                message = jnp.where(
                    line8 == TW, delta_row, bias[slot, key_slot * 3 + row] - log_row
                )
                if row == 1 and key_slot != BEYOND:
                    stats[slot, 1, key_slot] = message
                else:
                    stats_sent[slot, row, key_slot] = message
        start_rows(stat_copies(slot))
        if slot == INNER:
            start_rows(far_stat_copies())
        return delta

    def query_side(slot, delta):
        sums = [jnp.zeros((3 * TILE, HD), F32) for side in range(2)]
        for key_slot in (INNER, OUTER) if slot == OUTER else (INNER, OUTER, BEYOND):
            inverse = inverses[slot, 1 if key_slot == BEYOND else 0]
            delta_part = delta * inverse
            for side in range(2):
                grad_weights = dot_nt(
                    data[GRAD, slot, 1, near(side), :], rows_of(VALUE, key_slot, side)
                )
                part = weights[slot, key_slot, side].astype(F32) * (
                    grad_weights * wide(inverse[near(side)]) - wide(delta_part[near(side)])
                )
                sums[side] = sums[side] + dot_nn(
                    part.astype(BF16), rows_of(KEY, key_slot, side)
                )
        scale = my_scale(query_scale) * HD ** (-0.5)
        results[0, slot, 1] = (join(*sums, jnp.add) * scale).astype(BF16)
        return_heads(0, slot)

    def key_part(slot, query_slot):
        for side in range(2):
            message = jnp.concatenate(
                [stats[query_slot, row, slot, :, own(side)] for row in range(3)], axis=1
            )
            queries = rows_of(QUERY, query_slot, side)
            grads = rows_of(GRAD, query_slot, side)
            part = jnp.exp(add_rows(
                dot_nt(data[KEY, slot, 1, near(side), :], queries), message[side : side + 3]
            ))
            grad_weights = dot_nt(data[VALUE, slot, 1, near(side), :], grads)
            slopes = (part * (grad_weights - message[TW : TW + 1])).astype(BF16)
            for which, term in (
                (0, dot_nn(slopes, queries)), (1, dot_nn(part.astype(BF16), grads))
            ):
                if query_slot == OUTER:
                    key_sums[slot, which, side] = term
                else:
                    key_sums[slot, which, side] += term

    def key_end(slot):
        grad_keys = join(key_sums[slot, 0, 0], key_sums[slot, 0, 1], jnp.add)
        grad_values = join(key_sums[slot, 1, 0], key_sums[slot, 1, 1], jnp.add)
        results[1, slot, 0] = (grad_keys * my_scale(key_scale)).astype(BF16)
        results[1, slot, 1] = grad_values.astype(BF16)
        return_heads(1, slot)

    def queries_arrive(slot):
        wait_rows(QD, slot)
        came_rows(far_stat_copies() if slot == BEYOND else stat_copies(slot))

    def after_outer_scores():
        forward(KV)
        spread(QD, OUTER)
        spread(QD, INNER)

    lowest = jnp.full((SLAB, 128), -3e38, F32)
    outer = attend(
        OUTER, (INNER, OUTER), lambda key_slot: wait_rows(KV, key_slot), lowest, after_outer_scores
    )
    settle(OUTER, *outer, 1.0)
    query_side(OUTER, tell(OUTER))
    first = attend(INNER, (INNER, OUTER), lambda key_slot: None, lowest, lambda: None)
    for i in range(3):
        kept[i] = first[i]
    forward(QD)
    row_wide, total, summed = attend(
        INNER, (BEYOND,), lambda key_slot: wait_rows(KV, key_slot), kept[0], lambda: None
    )
    earlier = jnp.exp(kept[0] - row_wide)
    settle(INNER, row_wide, total + kept[1] * earlier, summed + kept[2] * earlier, earlier)
    query_side(INNER, tell(INNER))
    queries_arrive(OUTER)
    key_part(OUTER, OUTER)
    key_part(INNER, OUTER)
    queries_arrive(INNER)
    key_part(OUTER, INNER)
    key_end(OUTER)
    key_part(INNER, INNER)
    queries_arrive(BEYOND)
    key_part(INNER, BEYOND)
    key_end(INNER)

    for kind in range(2):
        pltpu.make_async_copy(landed.at[kind], landed.at[kind], out_recv.at[kind]).wait()
    sent = lists.at[0:2]
    pltpu.make_async_copy(sent, sent, list_send).wait()
    for kind in (KV, QD):
        sent = stage.at[ARRAYS[kind]]
        pltpu.make_async_copy(sent, sent, a2a_send.at[kind]).wait()
        for slot in range(3):
            sent_rows(r_copies(kind, slot))
        y_copy(kind).wait_send()
    for kind in range(2):
        sent = results.at[kind]
        pltpu.make_async_copy(sent, sent, out_send.at[kind]).wait()
    for slot in (OUTER, INNER):
        sent_rows(stat_copies(slot))
    sent_rows(far_stat_copies())


def hand_out(landed, attention, grad_query, grad_key, grad_value, pieces, held, sems):
    targets = (attention, grad_query, grad_key, grad_value)
    loads = [
        pltpu.make_async_copy(landed.at[kind], pieces.at[kind], sems.at[0, kind])
        for kind in range(2)
    ]
    stores = [pltpu.make_async_copy(held.at[i], targets[i], sems.at[1, i]) for i in range(4)]
    for load in loads:
        load.start()
    for i in range(4):
        if i % 2 == 0:
            loads[i // 2].wait()
        for head in range(landed.shape[1]):
            held[i, :, head * HD : (head + 1) * HD] = pieces[i // 2, head, i % 2]
        stores[i].start()
    for store in stores:
        store.wait()


def local(query, key, value, grad_out, query_scale, key_scale, neighbours):
    rows = lax.axis_size("slab") // FT
    columns = lax.axis_size("head") // 2
    chunk, width = query.shape
    out = jax.ShapeDtypeStruct((chunk, width), BF16)
    landing = (2, width // HD, 2, chunk, HD)
    hbm = pl.BlockSpec(memory_space=pltpu.HBM)
    dma = pltpu.SemaphoreType.DMA
    landed = pl.pallas_call(
        functools.partial(kernel, rows, columns),
        out_shape=jax.ShapeDtypeStruct(landing, BF16),
        in_specs=[hbm] * 7,
        out_specs=hbm,
        scratch_shapes=[
            pltpu.VMEM((4, chunk, width), BF16),
            pltpu.VMEM((1, width), F32),
            pltpu.VMEM((1, width), F32),
            pltpu.VMEM(neighbours.shape, jnp.int32),
            pltpu.VMEM((4, 4 * columns, chunk, HD), BF16),
            pltpu.VMEM((4, 3, 3, SLAB, HD), BF16),
            pltpu.VMEM((8, 128), F32),
            pltpu.VMEM((2, 2, 8, 128), F32),
            pltpu.VMEM((2, BLOCKS, 8, SLAB), F32),
            pltpu.VMEM((2, 3, 2, 8, 3 * 128), F32),
            pltpu.VMEM((3, 2, 3 * TILE, 3 * 128), F32),
            pltpu.VMEM((2, 3, 2, 3 * TILE, 3 * 128), BF16),
            pltpu.VMEM((2, 2, SLAB, 128), F32),
            pltpu.VMEM((2, SLAB, 128), F32),
            pltpu.VMEM((3, SLAB, 128), F32),
            pltpu.VMEM((2, 2, 2, 3 * TILE, HD), F32),
            pltpu.VMEM((3, 3, 2, 8, SLAB), F32),
            pltpu.VMEM((2, 3, 3, 8, SLAB), F32),
            pltpu.VMEM((2, 2, 2, SLAB, HD), BF16),
            dma((7,)),
            dma((2,)),
            dma((2, 2)),
            dma,
            dma,
            dma((2, 7)),
            dma((2,)),
            dma((2, 3, 2)),
            dma((2, 2)),
            dma((2, 2)),
            dma((3,)),
            dma((3,)),
            dma((2,)),
            dma((2,)),
        ],
        compiler_params=pltpu.CompilerParams(
            collective_id=0, has_side_effects=True, vmem_limit_bytes=VMEM_BYTES
        ),
        name="tiles",
    )(
        query, key, value, grad_out,
        query_scale.reshape(1, width), key_scale.reshape(1, width), neighbours,
    )
    return pl.pallas_call(
        hand_out,
        out_shape=(out,) * 4,
        in_specs=[hbm],
        out_specs=(hbm,) * 4,
        scratch_shapes=[
            pltpu.VMEM(landing, BF16), pltpu.VMEM((4, chunk, width), BF16), dma((2, 4)),
        ],
        compiler_params=pltpu.CompilerParams(vmem_limit_bytes=VMEM_BYTES),
        name="hand_out",
    )(landed)


def solution(mesh):
    token = P(("slab", "head"), None)
    return jax.shard_map(
        local,
        mesh=mesh,
        in_specs=(token, token, token, token, P(), P(), P("slab", None)),
        out_specs=(token,) * 4,
        check_vma=False,
    )
```

```python
import functools

import jax
import jax.numpy as jnp
from jax import lax
from jax.experimental import pallas as pl
from jax.experimental.pallas import tpu as pltpu
from jax.sharding import PartitionSpec as P

HD = 128
TILE = 64
FT = 4
TW = 4
SLAB = TILE * TW
RING = 2 * FT
BLOCKS = 9
OUTER, INNER, BEYOND = 0, 1, 2
HIDDEN = -1e30
MESH = pl.DeviceIdType.MESH
BF16 = jnp.bfloat16
F32 = jnp.float32
KEY, VALUE, QUERY, GRAD = range(4)
KV, QD = range(2)
ARRAYS = (pl.ds(0, 2), pl.ds(2, 2))
VMEM_BYTES = 58 * 1024 * 1024


def dot_nn(a, b):
    return lax.dot_general(a, b, (((1,), (0,)), ((), ())), preferred_element_type=F32)


def dot_nt(a, b):
    return lax.dot_general(a, b, (((1,), (1,)), ((), ())), preferred_element_type=F32)


def dot_tn(a, b):
    return lax.dot_general(a, b, (((0,), (0,)), ((), ())), preferred_element_type=F32)


def add_rows(scores, rows):
    shaped = scores.reshape(3, TILE, scores.shape[1]) + rows[:, None, :]
    return shaped.reshape(scores.shape)


def join(low, high, both):
    return jnp.concatenate(
        [low[:TILE], both(low[TILE:], high[: 2 * TILE]), high[2 * TILE :]], axis=0
    )


def fold(array, both):
    return both(both(array[:, :128], array[:, 128:256]), array[:, 256:])


def wide(column):
    return jnp.concatenate([column] * 3, axis=1)


def near(half):
    return slice(half * TILE, half * TILE + 3 * TILE)


def own(half):
    return slice(half * 2 * TILE, (half + 1) * 2 * TILE)


def kernel(
    rows, columns,
    query, key, value, grad_out, query_scale_in, key_scale_in, neighbours_in, landed,
    raw, query_scale, key_scale, neighbours,
    stage, data, listed, lists, bias, bias_rows, scores, weights, inverses, log_totals, kept, key_sums,
    stats, stats_sent, results,
    in_sem, a2a_send, a2a_recv, list_send, list_recv, halo_send, y_recv, r_recv,
    stat_send, stat_recv, far_send, far_recv, out_send, out_recv, above_sem,
):
    loads = [
        pltpu.make_async_copy(source, target, in_sem.at[i])
        for i, (source, target) in enumerate((
            (key, raw.at[0]), (value, raw.at[1]), (query, raw.at[2]), (grad_out, raw.at[3]),
            (key_scale_in, key_scale), (query_scale_in, query_scale),
            (neighbours_in, neighbours),
        ))
    ]
    for load in (loads[4], *loads[:2]):
        load.start()

    slab = lax.axis_index("slab")
    head = lax.axis_index("head")
    y_lo, r = slab // rows, slab % rows
    x, y_hi = head // 2, head % 2
    y = y_hi * FT + y_lo
    chunk = SLAB // (2 * columns)
    half = 1 - y_lo // 2
    far_y = (1 - y_lo // 2) * 2
    y_far = (far_y, far_y + 1, far_y + FT, far_y + FT + 1)
    frame_of = (3 * half, 1 + half, 2 - half)

    def quarter(at_y):
        return ((at_y + RING - 1) % RING) // 2

    def slot_of(at_y):
        return ((at_y % FT + 1) % FT) // 2

    my_head = x * 4 + quarter(y)
    y_partner = (y + RING - 1 + 2 * (y % 2)) % RING

    def device(to_y, to_r, to_x):
        return {"slab": (to_y % FT) * rows + to_r, "head": to_x * 2 + to_y // FT}

    r_at = ((r + rows - 1) % rows, r, (r + 1) % rows)
    x_at = tuple((x + step) % columns for step in range(columns))

    def at_side(side):
        return pl.when(r < rows - 1) if side == 2 else pl.when(r >= 1 - side)

    barrier = pltpu.get_barrier_semaphore()

    def greet(peers):
        for peer in peers:
            pl.semaphore_signal(barrier, 1, device_id=peer, device_id_type=MESH)

    greet([device(to_y, r, to_x) for to_y in y_far for to_x in x_at])
    greet([device(y_partner, r, x)])
    @at_side(2)
    def _():
        greet([device(y, r_at[2], x), device(y_partner, r_at[2], x)])

    for load in (*loads[2:4], *loads[5:]):
        load.start()
    listed[...] = jnp.full(listed.shape, -2.0, F32)

    def put(which, array):
        for piece in range(4 * columns):
            stage[which, piece] = array[:, piece * HD : (piece + 1) * HD]

    loads[4].wait()
    loads[0].wait()
    put(KEY, (raw[0].astype(F32) * key_scale[...]).astype(BF16))
    loads[1].wait()
    put(VALUE, raw[1])
    pl.semaphore_wait(barrier, 4 * columns + 1 + 2 * ((r + rows - 1) // rows))

    my_rows = pl.ds(pl.multiple_of(head * chunk, chunk), chunk)

    def send_heads(kind, places):
        for to_x in x_at:
            for to_y in places:
                pltpu.make_async_remote_copy(
                    src_ref=stage.at[ARRAYS[kind], to_x * 4 + quarter(to_y)],
                    dst_ref=data.at[ARRAYS[kind], slot_of(y), 1, my_rows, :],
                    send_sem=a2a_send.at[kind],
                    recv_sem=a2a_recv.at[kind, slot_of(y)],
                    device_id=device(to_y, r, to_x),
                    device_id_type=MESH,
                ).start()

    def wait_heads(kind, slot):
        whole = data.at[ARRAYS[kind], slot, 1]
        pltpu.make_async_copy(whole, whole, a2a_recv.at[kind, slot]).wait()

    def y_copy(kind):
        return pltpu.make_async_remote_copy(
            src_ref=data.at[ARRAYS[kind], INNER, 1],
            dst_ref=data.at[ARRAYS[kind], BEYOND, 1],
            send_sem=halo_send.at[kind, 6],
            recv_sem=y_recv.at[kind],
            device_id=device(y_partner, r, x),
            device_id_type=MESH,
        )

    def start_rows(copies):
        if 1 in copies:
            copies[1].start()
        for side, parity in ((0, 0), (2, 1), (2, 0), (0, 1)):
            exists = r < rows - 1 if side == 2 else r > 0
            pl.when(exists & (r % 2 == parity))(copies[side].start)

    def sent_rows(copies):
        for side, copy in copies.items():
            at_side(side)(copy.wait_send)

    def came_rows(copies):
        for side, copy in copies.items():
            at_side(2 - side)(copy.wait_recv)

    def r_copies(kind, slot):
        return {
            side: pltpu.make_async_remote_copy(
                src_ref=data.at[ARRAYS[kind], slot, 1],
                dst_ref=data.at[ARRAYS[kind], slot, 2 - side],
                send_sem=halo_send.at[kind, slot * 2 + side // 2],
                recv_sem=r_recv.at[kind, slot, side // 2],
                device_id=device(y, r_at[side], x),
                device_id_type=MESH,
            )
            for side in (0, 2)
        }

    def spread(kind, slot):
        start_rows(r_copies(kind, slot))

    def forward(kind):
        y_copy(kind).wait_recv()
        spread(kind, BEYOND)

    def wait_rows(kind, slot):
        came_rows(r_copies(kind, slot))

    send_heads(KV, y_far)

    @at_side(0)
    def _():
        for to_y in (y, y_partner):
            pl.semaphore_signal(
                above_sem, 1, device_id=device(to_y, r_at[0], x), device_id_type=MESH
            )

    loads[6].wait()
    listed[0:TW, 0:27] = neighbours[...].astype(F32)
    for to_y in y_far:
        pltpu.make_async_remote_copy(
            src_ref=listed, dst_ref=lists.at[y_hi, slot_of(y)],
            send_sem=list_send, recv_sem=list_recv,
            device_id=device(to_y, r, x), device_id_type=MESH,
        ).start()

    loads[5].wait()
    factor = query_scale[...] * HD ** (-0.5)
    loads[2].wait()
    put(QUERY, (raw[2].astype(F32) * factor).astype(BF16))
    loads[3].wait()
    put(GRAD, raw[3])
    send_heads(QD, y_far)

    for side in (0, 2):
        @pl.when(r == (rows - 1 if side == 2 else 0))
        def _():
            data[:, :, side] = jnp.zeros((4, 3, SLAB, HD), BF16)
            stats[:, side] = jnp.full((3, 2, 8, SLAB), HIDDEN, F32)

    wait_heads(KV, INNER)
    y_copy(KV).start()

    @at_side(2)
    def _():
        pl.semaphore_wait(above_sem, 2)

    spread(KV, INNER)
    wait_heads(KV, OUTER)
    spread(KV, OUTER)

    pltpu.make_async_copy(lists, lists, list_recv).wait()
    shape = (BLOCKS * 8, 128)
    line = lax.broadcasted_iota(jnp.int32, shape, 0)
    column = line % 8
    block_of = line // 8
    key_slot = block_of // 3
    key_frame = jnp.where(
        key_slot == 0, frame_of[0], jnp.where(key_slot == 1, frame_of[1], frame_of[2])
    )
    key_row = r + block_of % 3 - 1
    real = (column < TW) & (key_row >= 0) & (key_row < rows)
    ids = jnp.where(real, (key_frame * rows + key_row) * TW + column, -5).astype(F32)
    lane_tile = lax.broadcasted_iota(jnp.int32, (BLOCKS * 8, SLAB), 1) // TILE
    lane = lax.broadcasted_iota(jnp.int32, (8, 128), 1)
    for slot in (OUTER, INNER):
        found = jnp.full((BLOCKS * 8, SLAB), HIDDEN, F32)
        for tile in range(TW):
            hit = jnp.max(
                jnp.where(lists[0, slot, tile : tile + 1, :] == ids, 0.0, HIDDEN),
                axis=1, keepdims=True,
            )
            found = jnp.where(lane_tile == tile, hit, found)
        bias[slot] = found.reshape(BLOCKS, 8, SLAB)
        turned = jnp.concatenate(
            [
                jnp.concatenate(
                    [found[:, tile * TILE : tile * TILE + 1] for tile in range(TW)]
                    + [jnp.full((BLOCKS * 8, 124), HIDDEN, F32)],
                    axis=1,
                ),
                jnp.full((56, 128), HIDDEN, F32),
            ],
            axis=0,
        ).T[:8]
        for key_block in range(BLOCKS):
            for side in range(2):
                at = key_block * 8 + side * 2
                bias_rows[slot, key_block // 3, side, :, pl.ds(key_block % 3 * 128, 128)] = jnp.where(
                    lane < TILE, turned[:, at : at + 1], turned[:, at + 1 : at + 2]
                )

    wait_heads(QD, INNER)
    y_copy(QD).start()
    wait_heads(QD, OUTER)

    def return_heads(kind, slot):
        for to_x in x_at:
            for far_hi in range(2):
                to_y = frame_of[slot] + far_hi * FT
                token_chunk = to_x * 2 + far_hi
                part = pl.ds(pl.multiple_of(token_chunk * chunk, chunk), chunk)
                pltpu.make_async_remote_copy(
                    src_ref=results.at[kind, slot, :, part, :],
                    dst_ref=landed.at[kind, my_head],
                    send_sem=out_send.at[kind],
                    recv_sem=out_recv.at[kind],
                    device_id=device(to_y, r, to_x),
                    device_id_type=MESH,
                ).start()

    def my_scale(scale):
        return scale[:, pl.ds(pl.multiple_of(my_head * HD, HD), HD)]

    def stat_copies(slot):
        return {
            side: pltpu.make_async_remote_copy(
                src_ref=stats_sent.at[slot, side, 0:2],
                dst_ref=stats.at[slot, 2 - side],
                send_sem=stat_send.at[slot, side // 2],
                recv_sem=stat_recv.at[slot, side // 2],
                device_id=device(y, r_at[side], x),
                device_id_type=MESH,
            )
            for side in (0, 2)
        }

    def far_stat_copies():
        return {
            side: pltpu.make_async_remote_copy(
                src_ref=stats_sent.at[INNER, side, BEYOND],
                dst_ref=stats.at[BEYOND, 2 - side, INNER],
                send_sem=far_send.at[side],
                recv_sem=far_recv.at[side],
                device_id=device(y_partner, r_at[side], x),
                device_id_type=MESH,
            )
            for side in range(3)
        }

    def rows_of(array, slot, side):
        return jnp.concatenate(
            [data[array, slot, row, own(side), :] for row in range(3)], axis=0
        )

    def attend(slot, key_slots, arrive, least, between):
        parts = [(key_slot, side) for key_slot in key_slots for side in range(2)]
        peak = [jnp.full((3 * TILE, 128), -3e38, F32) for side in range(2)]
        for key_slot, side in parts:
            if side == 0:
                arrive(key_slot)
            part = add_rows(
                dot_nt(data[QUERY, slot, 1, near(side), :], rows_of(KEY, key_slot, side)),
                bias_rows[slot, key_slot, side, side : side + 3, :],
            )
            scores[key_slot, side] = part
            peak[side] = jnp.maximum(peak[side], fold(part, jnp.maximum))
        row_max = jnp.max(join(*peak, jnp.maximum), axis=1, keepdims=True)
        between()
        row_wide = jnp.maximum(jnp.broadcast_to(row_max, (SLAB, 128)), least)
        totals = [jnp.zeros((3 * TILE, 128), F32) for side in range(2)]
        sums = [jnp.zeros((3 * TILE, HD), F32) for side in range(2)]
        for key_slot, side in parts:
            part = jnp.exp(scores[key_slot, side] - wide(row_wide[near(side)]))
            low = part.astype(BF16)
            weights[slot, key_slot, side] = low
            totals[side] = totals[side] + fold(part, jnp.add)
            sums[side] = sums[side] + dot_nn(low, rows_of(VALUE, key_slot, side))
        total = jnp.sum(join(*totals, jnp.add), axis=1, keepdims=True)
        return row_wide, jnp.broadcast_to(total, (SLAB, 128)), join(*sums, jnp.add)

    def settle(slot, row_wide, total, summed, earlier):
        inverse = 1.0 / total
        results[0, slot, 0] = (summed * inverse).astype(BF16)
        inverses[slot, 0] = inverse * earlier
        inverses[slot, 1] = inverse
        log_totals[slot] = row_wide + jnp.log(total)

    def tell(slot):
        grads = data[GRAD, slot, 1].astype(F32)
        delta = jnp.sum(results[0, slot, 0].astype(F32) * grads, axis=1, keepdims=True)
        lane = lax.broadcasted_iota(jnp.int32, (SLAB, 128), 1)
        turned = jnp.where(lane == 0, log_totals[slot], delta).T
        log_row, delta_row = turned[0:1], turned[1:2]
        line8 = lax.broadcasted_iota(jnp.int32, (8, SLAB), 0)
        for key_slot in (OUTER, INNER) if slot == OUTER else (OUTER, INNER, BEYOND):
            for row in range(3):
                message = jnp.where(
                    line8 == TW, delta_row, bias[slot, key_slot * 3 + row] - log_row
                )
                if row == 1 and key_slot != BEYOND:
                    stats[slot, 1, key_slot] = message
                else:
                    stats_sent[slot, row, key_slot] = message
        start_rows(stat_copies(slot))
        if slot == INNER:
            start_rows(far_stat_copies())
        return delta

    def query_side(slot, delta):
        sums = [jnp.zeros((3 * TILE, HD), F32) for side in range(2)]
        for key_slot in (INNER, OUTER) if slot == OUTER else (INNER, OUTER, BEYOND):
            inverse = inverses[slot, 1 if key_slot == BEYOND else 0]
            delta_part = delta * inverse
            for side in range(2):
                grad_weights = dot_nt(
                    data[GRAD, slot, 1, near(side), :], rows_of(VALUE, key_slot, side)
                )
                part = weights[slot, key_slot, side].astype(F32) * (
                    grad_weights * wide(inverse[near(side)]) - wide(delta_part[near(side)])
                )
                sums[side] = sums[side] + dot_nn(
                    part.astype(BF16), rows_of(KEY, key_slot, side)
                )
        scale = my_scale(query_scale) * HD ** (-0.5)
        results[0, slot, 1] = (join(*sums, jnp.add) * scale).astype(BF16)
        return_heads(0, slot)

    def key_part(slot, query_slot):
        for side in range(2):
            message = jnp.concatenate(
                [stats[query_slot, row, slot, :, own(side)] for row in range(3)], axis=1
            )
            queries = rows_of(QUERY, query_slot, side)
            grads = rows_of(GRAD, query_slot, side)
            part = jnp.exp(add_rows(
                dot_nt(data[KEY, slot, 1, near(side), :], queries), message[side : side + 3]
            ))
            grad_weights = dot_nt(data[VALUE, slot, 1, near(side), :], grads)
            slopes = (part * (grad_weights - message[TW : TW + 1])).astype(BF16)
            for which, term in (
                (0, dot_nn(slopes, queries)), (1, dot_nn(part.astype(BF16), grads))
            ):
                if query_slot == OUTER:
                    key_sums[slot, which, side] = term
                else:
                    key_sums[slot, which, side] += term

    def key_end(slot):
        grad_keys = join(key_sums[slot, 0, 0], key_sums[slot, 0, 1], jnp.add)
        grad_values = join(key_sums[slot, 1, 0], key_sums[slot, 1, 1], jnp.add)
        results[1, slot, 0] = (grad_keys * my_scale(key_scale)).astype(BF16)
        results[1, slot, 1] = grad_values.astype(BF16)
        return_heads(1, slot)

    def queries_arrive(slot):
        wait_rows(QD, slot)
        came_rows(far_stat_copies() if slot == BEYOND else stat_copies(slot))

    def after_outer_scores():
        forward(KV)
        spread(QD, OUTER)
        spread(QD, INNER)

    lowest = jnp.full((SLAB, 128), -3e38, F32)
    outer = attend(
        OUTER, (INNER, OUTER), lambda key_slot: wait_rows(KV, key_slot), lowest, after_outer_scores
    )
    settle(OUTER, *outer, 1.0)
    query_side(OUTER, tell(OUTER))
    first = attend(INNER, (INNER, OUTER), lambda key_slot: None, lowest, lambda: None)
    for i in range(3):
        kept[i] = first[i]
    forward(QD)
    row_wide, total, summed = attend(
        INNER, (BEYOND,), lambda key_slot: wait_rows(KV, key_slot), kept[0], lambda: None
    )
    earlier = jnp.exp(kept[0] - row_wide)
    settle(INNER, row_wide, total + kept[1] * earlier, summed + kept[2] * earlier, earlier)
    query_side(INNER, tell(INNER))
    queries_arrive(OUTER)
    key_part(OUTER, OUTER)
    key_part(INNER, OUTER)
    queries_arrive(INNER)
    key_part(OUTER, INNER)
    key_end(OUTER)
    key_part(INNER, INNER)
    queries_arrive(BEYOND)
    key_part(INNER, BEYOND)
    key_end(INNER)

    for kind in range(2):
        pltpu.make_async_copy(landed.at[kind], landed.at[kind], out_recv.at[kind]).wait()
    sent = lists.at[0:2]
    pltpu.make_async_copy(sent, sent, list_send).wait()
    for kind in (KV, QD):
        sent = stage.at[ARRAYS[kind]]
        pltpu.make_async_copy(sent, sent, a2a_send.at[kind]).wait()
        for slot in range(3):
            sent_rows(r_copies(kind, slot))
        y_copy(kind).wait_send()
    for kind in range(2):
        sent = results.at[kind]
        pltpu.make_async_copy(sent, sent, out_send.at[kind]).wait()
    for slot in (OUTER, INNER):
        sent_rows(stat_copies(slot))
    sent_rows(far_stat_copies())


def hand_out(landed, attention, grad_query, grad_key, grad_value, pieces, held, sems):
    targets = (attention, grad_query, grad_key, grad_value)
    loads = [
        pltpu.make_async_copy(landed.at[kind], pieces.at[kind], sems.at[0, kind])
        for kind in range(2)
    ]
    stores = [pltpu.make_async_copy(held.at[i], targets[i], sems.at[1, i]) for i in range(4)]
    for load in loads:
        load.start()
    for i in range(4):
        if i % 2 == 0:
            loads[i // 2].wait()
        for head in range(landed.shape[1]):
            held[i, :, head * HD : (head + 1) * HD] = pieces[i // 2, head, i % 2]
        stores[i].start()
    for store in stores:
        store.wait()


def local(query, key, value, grad_out, query_scale, key_scale, neighbours):
    rows = lax.axis_size("slab") // FT
    columns = lax.axis_size("head") // 2
    chunk, width = query.shape
    out = jax.ShapeDtypeStruct((chunk, width), BF16)
    landing = (2, width // HD, 2, chunk, HD)
    hbm = pl.BlockSpec(memory_space=pltpu.HBM)
    dma = pltpu.SemaphoreType.DMA
    landed = pl.pallas_call(
        functools.partial(kernel, rows, columns),
        out_shape=jax.ShapeDtypeStruct(landing, BF16),
        in_specs=[hbm] * 7,
        out_specs=hbm,
        scratch_shapes=[
            pltpu.VMEM((4, chunk, width), BF16),
            pltpu.VMEM((1, width), F32),
            pltpu.VMEM((1, width), F32),
            pltpu.VMEM(neighbours.shape, jnp.int32),
            pltpu.VMEM((4, 4 * columns, chunk, HD), BF16),
            pltpu.VMEM((4, 3, 3, SLAB, HD), BF16),
            pltpu.VMEM((8, 128), F32),
            pltpu.VMEM((2, 2, 8, 128), F32),
            pltpu.VMEM((2, BLOCKS, 8, SLAB), F32),
            pltpu.VMEM((2, 3, 2, 8, 3 * 128), F32),
            pltpu.VMEM((3, 2, 3 * TILE, 3 * 128), F32),
            pltpu.VMEM((2, 3, 2, 3 * TILE, 3 * 128), BF16),
            pltpu.VMEM((2, 2, SLAB, 128), F32),
            pltpu.VMEM((2, SLAB, 128), F32),
            pltpu.VMEM((3, SLAB, 128), F32),
            pltpu.VMEM((2, 2, 2, 3 * TILE, HD), F32),
            pltpu.VMEM((3, 3, 2, 8, SLAB), F32),
            pltpu.VMEM((2, 3, 3, 8, SLAB), F32),
            pltpu.VMEM((2, 2, 2, SLAB, HD), BF16),
            dma((7,)),
            dma((2,)),
            dma((2, 2)),
            dma,
            dma,
            dma((2, 7)),
            dma((2,)),
            dma((2, 3, 2)),
            dma((2, 2)),
            dma((2, 2)),
            dma((3,)),
            dma((3,)),
            dma((2,)),
            dma((2,)),
            pltpu.SemaphoreType.REGULAR,
        ],
        compiler_params=pltpu.CompilerParams(
            collective_id=0, has_side_effects=True, vmem_limit_bytes=VMEM_BYTES
        ),
        name="tiles",
    )(
        query, key, value, grad_out,
        query_scale.reshape(1, width), key_scale.reshape(1, width), neighbours,
    )
    return pl.pallas_call(
        hand_out,
        out_shape=(out,) * 4,
        in_specs=[hbm],
        out_specs=(hbm,) * 4,
        scratch_shapes=[
            pltpu.VMEM(landing, BF16), pltpu.VMEM((4, chunk, width), BF16), dma((2, 4)),
        ],
        compiler_params=pltpu.CompilerParams(vmem_limit_bytes=VMEM_BYTES),
        name="hand_out",
    )(landed)


def solution(mesh):
    token = P(("slab", "head"), None)
    return jax.shard_map(
        local,
        mesh=mesh,
        in_specs=(token, token, token, token, P(), P(), P("slab", None)),
        out_specs=(token,) * 4,
        check_vma=False,
    )
```

```python
import functools

import jax
import jax.numpy as jnp
from jax import lax
from jax.experimental import pallas as pl
from jax.experimental.pallas import tpu as pltpu
from jax.sharding import PartitionSpec as P

HD = 128
TILE = 64
FT = 4
TW = 4
SLAB = TILE * TW
RING = 2 * FT
BLOCKS = 9
OUTER, INNER, BEYOND = 0, 1, 2
HIDDEN = -1e30
MESH = pl.DeviceIdType.MESH
BF16 = jnp.bfloat16
F32 = jnp.float32
KEY, VALUE, QUERY, GRAD = range(4)
KV, QD = range(2)
ARRAYS = (pl.ds(0, 2), pl.ds(2, 2))
VMEM_BYTES = 58 * 1024 * 1024


def dot_nn(a, b):
    return lax.dot_general(a, b, (((1,), (0,)), ((), ())), preferred_element_type=F32)


def dot_nt(a, b):
    return lax.dot_general(a, b, (((1,), (1,)), ((), ())), preferred_element_type=F32)


def dot_tn(a, b):
    return lax.dot_general(a, b, (((0,), (0,)), ((), ())), preferred_element_type=F32)


def add_rows(scores, rows):
    shaped = scores.reshape(3, TILE, scores.shape[1]) + rows[:, None, :]
    return shaped.reshape(scores.shape)


def join(low, high, both):
    return jnp.concatenate(
        [low[:TILE], both(low[TILE:], high[: 2 * TILE]), high[2 * TILE :]], axis=0
    )


def fold(array, both):
    return both(both(array[:, :128], array[:, 128:256]), array[:, 256:])


def wide(column):
    return jnp.concatenate([column] * 3, axis=1)


def near(half):
    return slice(half * TILE, half * TILE + 3 * TILE)


def own(half):
    return slice(half * 2 * TILE, (half + 1) * 2 * TILE)


def kernel(
    rows, columns,
    query, key, value, grad_out, query_scale_in, key_scale_in, neighbours_in, landed,
    raw, query_scale, key_scale, neighbours,
    stage, data, listed, lists, bias, bias_rows, scores, weights, inverses, log_totals, kept, key_sums,
    stats, stats_sent, results,
    in_sem, a2a_send, a2a_recv, list_send, list_recv, halo_send, y_recv, r_recv,
    stat_send, stat_recv, far_send, far_recv, out_send, out_recv,
):
    loads = [
        pltpu.make_async_copy(source, target, in_sem.at[i])
        for i, (source, target) in enumerate((
            (key, raw.at[0]), (value, raw.at[1]), (query, raw.at[2]), (grad_out, raw.at[3]),
            (key_scale_in, key_scale), (query_scale_in, query_scale),
            (neighbours_in, neighbours),
        ))
    ]
    for load in (loads[4], *loads[:2]):
        load.start()

    slab = lax.axis_index("slab")
    head = lax.axis_index("head")
    y_lo, r = slab // rows, slab % rows
    x, y_hi = head // 2, head % 2
    y = y_hi * FT + y_lo
    chunk = SLAB // (2 * columns)
    half = 1 - y_lo // 2
    far_y = (1 - y_lo // 2) * 2
    y_far = (far_y, far_y + 1, far_y + FT, far_y + FT + 1)
    frame_of = (3 * half, 1 + half, 2 - half)

    def quarter(at_y):
        return ((at_y + RING - 1) % RING) // 2

    def slot_of(at_y):
        return ((at_y % FT + 1) % FT) // 2

    my_head = x * 4 + quarter(y)
    y_partner = (y + RING - 1 + 2 * (y % 2)) % RING

    def device(to_y, to_r, to_x):
        return {"slab": (to_y % FT) * rows + to_r, "head": to_x * 2 + to_y // FT}

    r_at = ((r + rows - 1) % rows, r, (r + 1) % rows)
    x_at = tuple((x + step) % columns for step in range(columns))

    def at_side(side):
        return pl.when(r < rows - 1) if side == 2 else pl.when(r >= 1 - side)

    barrier = pltpu.get_barrier_semaphore()

    def greet(peers):
        for peer in peers:
            pl.semaphore_signal(barrier, 1, device_id=peer, device_id_type=MESH)

    greet([device(to_y, r, to_x) for to_y in y_far for to_x in x_at])
    greet([device(y_partner, r, x)])
    for side in (0, 2):
        @at_side(side)
        def _():
            greet([device(y, r_at[side], x), device(y_partner, r_at[side], x)])

    for load in (*loads[2:4], *loads[5:]):
        load.start()
    listed[...] = jnp.full(listed.shape, -2.0, F32)

    def put(which, array):
        for piece in range(4 * columns):
            stage[which, piece] = array[:, piece * HD : (piece + 1) * HD]

    loads[4].wait()
    loads[0].wait()
    put(KEY, (raw[0].astype(F32) * key_scale[...]).astype(BF16))
    loads[1].wait()
    put(VALUE, raw[1])
    row_sides = (r + rows - 1) // rows + (2 * rows - 2 - r) // rows
    pl.semaphore_wait(barrier, 4 * columns + 1 + 2 * row_sides)

    my_rows = pl.ds(pl.multiple_of(head * chunk, chunk), chunk)

    def send_heads(kind, places):
        for to_x in x_at:
            for to_y in places:
                pltpu.make_async_remote_copy(
                    src_ref=stage.at[ARRAYS[kind], to_x * 4 + quarter(to_y)],
                    dst_ref=data.at[ARRAYS[kind], slot_of(y), 1, my_rows, :],
                    send_sem=a2a_send.at[kind],
                    recv_sem=a2a_recv.at[kind, slot_of(y)],
                    device_id=device(to_y, r, to_x),
                    device_id_type=MESH,
                ).start()

    def wait_heads(kind, slot):
        whole = data.at[ARRAYS[kind], slot, 1]
        pltpu.make_async_copy(whole, whole, a2a_recv.at[kind, slot]).wait()

    def y_copy(kind):
        return pltpu.make_async_remote_copy(
            src_ref=data.at[ARRAYS[kind], INNER, 1],
            dst_ref=data.at[ARRAYS[kind], BEYOND, 1],
            send_sem=halo_send.at[kind, 6],
            recv_sem=y_recv.at[kind],
            device_id=device(y_partner, r, x),
            device_id_type=MESH,
        )

    def start_rows(copies):
        if 1 in copies:
            copies[1].start()
        for side, parity in ((0, 0), (2, 1), (2, 0), (0, 1)):
            exists = r < rows - 1 if side == 2 else r > 0
            pl.when(exists & (r % 2 == parity))(copies[side].start)

    def sent_rows(copies):
        for side, copy in copies.items():
            at_side(side)(copy.wait_send)

    def came_rows(copies):
        for side, copy in copies.items():
            at_side(2 - side)(copy.wait_recv)

    def r_copies(kind, slot):
        return {
            side: pltpu.make_async_remote_copy(
                src_ref=data.at[ARRAYS[kind], slot, 1],
                dst_ref=data.at[ARRAYS[kind], slot, 2 - side],
                send_sem=halo_send.at[kind, slot * 2 + side // 2],
                recv_sem=r_recv.at[kind, slot, side // 2],
                device_id=device(y, r_at[side], x),
                device_id_type=MESH,
            )
            for side in (0, 2)
        }

    def spread(kind, slot):
        start_rows(r_copies(kind, slot))

    def forward(kind):
        y_copy(kind).wait_recv()
        spread(kind, BEYOND)

    def wait_rows(kind, slot):
        came_rows(r_copies(kind, slot))

    send_heads(KV, y_far)
    loads[6].wait()
    listed[0:TW, 0:27] = neighbours[...].astype(F32)
    for to_y in y_far:
        pltpu.make_async_remote_copy(
            src_ref=listed, dst_ref=lists.at[y_hi, slot_of(y)],
            send_sem=list_send, recv_sem=list_recv,
            device_id=device(to_y, r, x), device_id_type=MESH,
        ).start()

    loads[5].wait()
    factor = query_scale[...] * HD ** (-0.5)
    loads[2].wait()
    put(QUERY, (raw[2].astype(F32) * factor).astype(BF16))
    loads[3].wait()
    put(GRAD, raw[3])
    send_heads(QD, y_far)

    for side in (0, 2):
        @pl.when(r == (rows - 1 if side == 2 else 0))
        def _():
            data[:, :, side] = jnp.zeros((4, 3, SLAB, HD), BF16)
            stats[:, side] = jnp.full((3, 2, 8, SLAB), HIDDEN, F32)

    wait_heads(KV, INNER)
    y_copy(KV).start()
    spread(KV, INNER)
    wait_heads(KV, OUTER)
    spread(KV, OUTER)

    pltpu.make_async_copy(lists, lists, list_recv).wait()
    shape = (BLOCKS * 8, 128)
    line = lax.broadcasted_iota(jnp.int32, shape, 0)
    column = line % 8
    block_of = line // 8
    key_slot = block_of // 3
    key_frame = jnp.where(
        key_slot == 0, frame_of[0], jnp.where(key_slot == 1, frame_of[1], frame_of[2])
    )
    key_row = r + block_of % 3 - 1
    real = (column < TW) & (key_row >= 0) & (key_row < rows)
    ids = jnp.where(real, (key_frame * rows + key_row) * TW + column, -5).astype(F32)
    lane_tile = lax.broadcasted_iota(jnp.int32, (BLOCKS * 8, SLAB), 1) // TILE
    lane = lax.broadcasted_iota(jnp.int32, (8, 128), 1)
    for slot in (OUTER, INNER):
        found = jnp.full((BLOCKS * 8, SLAB), HIDDEN, F32)
        for tile in range(TW):
            hit = jnp.max(
                jnp.where(lists[0, slot, tile : tile + 1, :] == ids, 0.0, HIDDEN),
                axis=1, keepdims=True,
            )
            found = jnp.where(lane_tile == tile, hit, found)
        bias[slot] = found.reshape(BLOCKS, 8, SLAB)
        turned = jnp.concatenate(
            [
                jnp.concatenate(
                    [found[:, tile * TILE : tile * TILE + 1] for tile in range(TW)]
                    + [jnp.full((BLOCKS * 8, 124), HIDDEN, F32)],
                    axis=1,
                ),
                jnp.full((56, 128), HIDDEN, F32),
            ],
            axis=0,
        ).T[:8]
        for key_block in range(BLOCKS):
            for side in range(2):
                at = key_block * 8 + side * 2
                bias_rows[slot, key_block // 3, side, :, pl.ds(key_block % 3 * 128, 128)] = jnp.where(
                    lane < TILE, turned[:, at : at + 1], turned[:, at + 1 : at + 2]
                )

    wait_heads(QD, INNER)
    y_copy(QD).start()
    wait_heads(QD, OUTER)

    def return_heads(kind, slot):
        for to_x in x_at:
            for far_hi in range(2):
                to_y = frame_of[slot] + far_hi * FT
                token_chunk = to_x * 2 + far_hi
                part = pl.ds(pl.multiple_of(token_chunk * chunk, chunk), chunk)
                pltpu.make_async_remote_copy(
                    src_ref=results.at[kind, slot, :, part, :],
                    dst_ref=landed.at[kind, my_head],
                    send_sem=out_send.at[kind],
                    recv_sem=out_recv.at[kind],
                    device_id=device(to_y, r, to_x),
                    device_id_type=MESH,
                ).start()

    def my_scale(scale):
        return scale[:, pl.ds(pl.multiple_of(my_head * HD, HD), HD)]

    def stat_copies(slot):
        return {
            side: pltpu.make_async_remote_copy(
                src_ref=stats_sent.at[slot, side, 0:2],
                dst_ref=stats.at[slot, 2 - side],
                send_sem=stat_send.at[slot, side // 2],
                recv_sem=stat_recv.at[slot, side // 2],
                device_id=device(y, r_at[side], x),
                device_id_type=MESH,
            )
            for side in (0, 2)
        }

    def far_stat_copies():
        return {
            side: pltpu.make_async_remote_copy(
                src_ref=stats_sent.at[INNER, side, BEYOND],
                dst_ref=stats.at[BEYOND, 2 - side, INNER],
                send_sem=far_send.at[side],
                recv_sem=far_recv.at[side],
                device_id=device(y_partner, r_at[side], x),
                device_id_type=MESH,
            )
            for side in range(3)
        }

    def rows_of(array, slot, side):
        return jnp.concatenate(
            [data[array, slot, row, own(side), :] for row in range(3)], axis=0
        )

    def attend(slot, key_slots, arrive, least, between):
        parts = [(key_slot, side) for key_slot in key_slots for side in range(2)]
        peak = [jnp.full((3 * TILE, 128), -3e38, F32) for side in range(2)]
        for key_slot, side in parts:
            if side == 0:
                arrive(key_slot)
            part = add_rows(
                dot_nt(data[QUERY, slot, 1, near(side), :], rows_of(KEY, key_slot, side)),
                bias_rows[slot, key_slot, side, side : side + 3, :],
            )
            scores[key_slot, side] = part
            peak[side] = jnp.maximum(peak[side], fold(part, jnp.maximum))
        row_max = jnp.max(join(*peak, jnp.maximum), axis=1, keepdims=True)
        between()
        row_wide = jnp.maximum(jnp.broadcast_to(row_max, (SLAB, 128)), least)
        totals = [jnp.zeros((3 * TILE, 128), F32) for side in range(2)]
        sums = [jnp.zeros((3 * TILE, HD), F32) for side in range(2)]
        for key_slot, side in parts:
            part = jnp.exp(scores[key_slot, side] - wide(row_wide[near(side)]))
            low = part.astype(BF16)
            weights[slot, key_slot, side] = low
            totals[side] = totals[side] + fold(part, jnp.add)
            sums[side] = sums[side] + dot_nn(low, rows_of(VALUE, key_slot, side))
        total = jnp.sum(join(*totals, jnp.add), axis=1, keepdims=True)
        return row_wide, jnp.broadcast_to(total, (SLAB, 128)), join(*sums, jnp.add)

    def settle(slot, row_wide, total, summed, earlier):
        inverse = 1.0 / total
        results[0, slot, 0] = (summed * inverse).astype(BF16)
        inverses[slot, 0] = inverse * earlier
        inverses[slot, 1] = inverse
        log_totals[slot] = row_wide + jnp.log(total)

    def tell(slot):
        grads = data[GRAD, slot, 1].astype(F32)
        delta = jnp.sum(results[0, slot, 0].astype(F32) * grads, axis=1, keepdims=True)
        lane = lax.broadcasted_iota(jnp.int32, (SLAB, 128), 1)
        turned = jnp.where(lane == 0, log_totals[slot], delta).T
        log_row, delta_row = turned[0:1], turned[1:2]
        line8 = lax.broadcasted_iota(jnp.int32, (8, SLAB), 0)
        for key_slot in (OUTER, INNER) if slot == OUTER else (OUTER, INNER, BEYOND):
            for row in range(3):
                message = jnp.where(
                    line8 == TW, delta_row, bias[slot, key_slot * 3 + row] - log_row
                )
                if row == 1 and key_slot != BEYOND:
                    stats[slot, 1, key_slot] = message
                else:
                    stats_sent[slot, row, key_slot] = message
        start_rows(stat_copies(slot))
        if slot == INNER:
            start_rows(far_stat_copies())
        return delta

    def query_side(slot, delta):
        sums = [jnp.zeros((3 * TILE, HD), F32) for side in range(2)]
        for key_slot in (INNER, OUTER) if slot == OUTER else (INNER, OUTER, BEYOND):
            inverse = inverses[slot, 1 if key_slot == BEYOND else 0]
            delta_part = delta * inverse
            for side in range(2):
                grad_weights = dot_nt(
                    data[GRAD, slot, 1, near(side), :], rows_of(VALUE, key_slot, side)
                )
                part = weights[slot, key_slot, side].astype(F32) * (
                    grad_weights * wide(inverse[near(side)]) - wide(delta_part[near(side)])
                )
                sums[side] = sums[side] + dot_nn(
                    part.astype(BF16), rows_of(KEY, key_slot, side)
                )
        scale = my_scale(query_scale) * HD ** (-0.5)
        results[0, slot, 1] = (join(*sums, jnp.add) * scale).astype(BF16)
        return_heads(0, slot)

    def key_part(slot, query_slot):
        def half(side, carry):
            mine = pl.ds(pl.multiple_of(side * 2 * TILE, 2 * TILE), 2 * TILE)
            seen = pl.ds(pl.multiple_of(side * TILE, TILE), 3 * TILE)
            message = jnp.concatenate(
                [stats[query_slot, row, slot, :, mine] for row in range(3)], axis=1
            )
            rows_added = jnp.where(side == 0, message[0:3], message[1:4])
            queries = jnp.concatenate(
                [data[QUERY, query_slot, row, mine, :] for row in range(3)], axis=0
            )
            grads = jnp.concatenate(
                [data[GRAD, query_slot, row, mine, :] for row in range(3)], axis=0
            )
            part = jnp.exp(add_rows(dot_nt(data[KEY, slot, 1, seen, :], queries), rows_added))
            grad_weights = dot_nt(data[VALUE, slot, 1, seen, :], grads)
            slopes = (part * (grad_weights - message[TW : TW + 1])).astype(BF16)
            for which, term in (
                (0, dot_nn(slopes, queries)), (1, dot_nn(part.astype(BF16), grads))
            ):
                if query_slot == OUTER:
                    key_sums[slot, which, side] = term
                else:
                    key_sums[slot, which, side] += term
            return carry

        lax.fori_loop(0, 2, half, 0)

    def key_end(slot):
        grad_keys = join(key_sums[slot, 0, 0], key_sums[slot, 0, 1], jnp.add)
        grad_values = join(key_sums[slot, 1, 0], key_sums[slot, 1, 1], jnp.add)
        results[1, slot, 0] = (grad_keys * my_scale(key_scale)).astype(BF16)
        results[1, slot, 1] = grad_values.astype(BF16)
        return_heads(1, slot)

    def queries_arrive(slot):
        wait_rows(QD, slot)
        came_rows(far_stat_copies() if slot == BEYOND else stat_copies(slot))

    def after_outer_scores():
        forward(KV)
        spread(QD, OUTER)
        spread(QD, INNER)

    lowest = jnp.full((SLAB, 128), -3e38, F32)
    outer = attend(
        OUTER, (INNER, OUTER), lambda key_slot: wait_rows(KV, key_slot), lowest, after_outer_scores
    )
    settle(OUTER, *outer, 1.0)
    query_side(OUTER, tell(OUTER))
    first = attend(INNER, (INNER, OUTER), lambda key_slot: None, lowest, lambda: None)
    for i in range(3):
        kept[i] = first[i]
    forward(QD)
    row_wide, total, summed = attend(
        INNER, (BEYOND,), lambda key_slot: wait_rows(KV, key_slot), kept[0], lambda: None
    )
    earlier = jnp.exp(kept[0] - row_wide)
    settle(INNER, row_wide, total + kept[1] * earlier, summed + kept[2] * earlier, earlier)
    query_side(INNER, tell(INNER))
    queries_arrive(OUTER)
    key_part(OUTER, OUTER)
    key_part(INNER, OUTER)
    queries_arrive(INNER)
    key_part(OUTER, INNER)
    key_end(OUTER)
    key_part(INNER, INNER)
    queries_arrive(BEYOND)
    key_part(INNER, BEYOND)
    key_end(INNER)

    for kind in range(2):
        pltpu.make_async_copy(landed.at[kind], landed.at[kind], out_recv.at[kind]).wait()
    sent = lists.at[0:2]
    pltpu.make_async_copy(sent, sent, list_send).wait()
    for kind in (KV, QD):
        sent = stage.at[ARRAYS[kind]]
        pltpu.make_async_copy(sent, sent, a2a_send.at[kind]).wait()
        for slot in range(3):
            sent_rows(r_copies(kind, slot))
        y_copy(kind).wait_send()
    for kind in range(2):
        sent = results.at[kind]
        pltpu.make_async_copy(sent, sent, out_send.at[kind]).wait()
    for slot in (OUTER, INNER):
        sent_rows(stat_copies(slot))
    sent_rows(far_stat_copies())


def hand_out(landed, attention, grad_query, grad_key, grad_value, pieces, held, sems):
    targets = (attention, grad_query, grad_key, grad_value)
    loads = [
        pltpu.make_async_copy(landed.at[kind], pieces.at[kind], sems.at[0, kind])
        for kind in range(2)
    ]
    stores = [pltpu.make_async_copy(held.at[i], targets[i], sems.at[1, i]) for i in range(4)]
    for load in loads:
        load.start()
    for i in range(4):
        if i % 2 == 0:
            loads[i // 2].wait()
        for head in range(landed.shape[1]):
            held[i, :, head * HD : (head + 1) * HD] = pieces[i // 2, head, i % 2]
        stores[i].start()
    for store in stores:
        store.wait()


def local(query, key, value, grad_out, query_scale, key_scale, neighbours):
    rows = lax.axis_size("slab") // FT
    columns = lax.axis_size("head") // 2
    chunk, width = query.shape
    out = jax.ShapeDtypeStruct((chunk, width), BF16)
    landing = (2, width // HD, 2, chunk, HD)
    hbm = pl.BlockSpec(memory_space=pltpu.HBM)
    dma = pltpu.SemaphoreType.DMA
    landed = pl.pallas_call(
        functools.partial(kernel, rows, columns),
        out_shape=jax.ShapeDtypeStruct(landing, BF16),
        in_specs=[hbm] * 7,
        out_specs=hbm,
        scratch_shapes=[
            pltpu.VMEM((4, chunk, width), BF16),
            pltpu.VMEM((1, width), F32),
            pltpu.VMEM((1, width), F32),
            pltpu.VMEM(neighbours.shape, jnp.int32),
            pltpu.VMEM((4, 4 * columns, chunk, HD), BF16),
            pltpu.VMEM((4, 3, 3, SLAB, HD), BF16),
            pltpu.VMEM((8, 128), F32),
            pltpu.VMEM((2, 2, 8, 128), F32),
            pltpu.VMEM((2, BLOCKS, 8, SLAB), F32),
            pltpu.VMEM((2, 3, 2, 8, 3 * 128), F32),
            pltpu.VMEM((3, 2, 3 * TILE, 3 * 128), F32),
            pltpu.VMEM((2, 3, 2, 3 * TILE, 3 * 128), BF16),
            pltpu.VMEM((2, 2, SLAB, 128), F32),
            pltpu.VMEM((2, SLAB, 128), F32),
            pltpu.VMEM((3, SLAB, 128), F32),
            pltpu.VMEM((2, 2, 2, 3 * TILE, HD), F32),
            pltpu.VMEM((3, 3, 2, 8, SLAB), F32),
            pltpu.VMEM((2, 3, 3, 8, SLAB), F32),
            pltpu.VMEM((2, 2, 2, SLAB, HD), BF16),
            dma((7,)),
            dma((2,)),
            dma((2, 2)),
            dma,
            dma,
            dma((2, 7)),
            dma((2,)),
            dma((2, 3, 2)),
            dma((2, 2)),
            dma((2, 2)),
            dma((3,)),
            dma((3,)),
            dma((2,)),
            dma((2,)),
        ],
        compiler_params=pltpu.CompilerParams(
            collective_id=0, has_side_effects=True, vmem_limit_bytes=VMEM_BYTES
        ),
        name="tiles",
    )(
        query, key, value, grad_out,
        query_scale.reshape(1, width), key_scale.reshape(1, width), neighbours,
    )
    return pl.pallas_call(
        hand_out,
        out_shape=(out,) * 4,
        in_specs=[hbm],
        out_specs=(hbm,) * 4,
        scratch_shapes=[
            pltpu.VMEM(landing, BF16), pltpu.VMEM((4, chunk, width), BF16), dma((2, 4)),
        ],
        compiler_params=pltpu.CompilerParams(vmem_limit_bytes=VMEM_BYTES),
        name="hand_out",
    )(landed)


def solution(mesh):
    token = P(("slab", "head"), None)
    return jax.shard_map(
        local,
        mesh=mesh,
        in_specs=(token, token, token, token, P(), P(), P("slab", None)),
        out_specs=(token,) * 4,
        check_vma=False,
    )
```
